32 devices in a mesh: gx: 4 (over z), gy: 4 (over y, core), gz: 2 (over x).
Axes of the slice: x: 2, y: 2, z: 4, core: 2. Of those that a mesh axis runs over, the one named last changes fastest.
Arguments:
- velocity: float32 [3, 32, 32, 256], P(None, 'gx', 'gy', 'gz'), may hold values from -6 to 6
- cotangent: float32 [3, 32, 32, 256], P(None, 'gx', 'gy', 'gz'), may hold values from -6 to 6
- first_weight: float32 [32, 81], replicated, may hold values from -0.625 to 0.625
- first_bias: float32 [32], replicated, may hold values from -3 to 3
- second_weight: float32 [3, 32], replicated, may hold values from -1 to 1
- second_bias: float32 [3], replicated, may hold values from -3 to 3
- sweeps: int32 [3], replicated, may hold values from 1 to 3, as said below
Outputs:
- updated: float32 [3, 32, 32, 256], P(None, 'gx', 'gy', 'gz')
- grad_velocity: float32 [3, 32, 32, 256], P(None, 'gx', 'gy', 'gz')
The draws below stay inside these ranges and needn't reach their ends.
Inputs may be any that keep to these rules, and one draw needn't show every extreme that they name: `sweeps`: each of 1 to 3 appears exactly once, in an order drawn from the seed.
All inputs are finite; a program needn't handle non-finite values.
Results may differ from the reference program's by a relative error of at most 0.0001.
Values sent between devices are 32-bit elements; how exact they have to be, the bound alone decides.
No kernel may reach another device: no remote copies, remote signals or barrier semaphores. Data moves between devices by JAX's collectives and lax.ppermute only.
A program may use at most 128 MiB of HBM per device.

```python
import jax
import jax.numpy as jnp
from jax import lax

WIDTH = 32
FEATURES = 81
LEVELS = 3
CYCLES = 2
COARSE_SWEEPS = 6
NX = 32
NY = 32
NZ = 256


def draw_sweeps(key, part):
    key = jax.random.fold_in(key, 7)
    return (jax.random.permutation(key, LEVELS) + 1).astype(jnp.int32)


def block_levels(key, dims, split, low, largest):
    level = 1.0
    for position, shards_of in split:
        draws = jax.random.uniform(jax.random.fold_in(jax.random.fold_in(key, 6), position), (shards_of,), jnp.float32, low / len(split), largest / len(split))
        level = level * jnp.repeat(jnp.exp(draws), dims[position] // shards_of).reshape((-1,) + (1,) * (len(dims) - 1 - position))
    return level


def normal_values(own_key, dims, scale, bound, cuts=(), kind=jnp.bfloat16):
    drawn = jax.random.normal(own_key, dims, jnp.float32) * scale
    if len(cuts) > 0:
        drawn = block_levels(own_key, dims, cuts, -0.22, 0.18) * drawn
    return jnp.clip(drawn, min=-bound, max=bound).astype(kind)


def setup_inputs(seed: int = 0) -> dict:
    key_list = jax.random.split(jax.random.key(seed), 8)
    return {
        "velocity": normal_values(key_list[0], (3, NX, NY, NZ), 1.0, 6.0, ((1, 4), (2, 4), (3, 2)), jnp.float32),
        "cotangent": normal_values(key_list[1], (3, NX, NY, NZ), 1.0, 6.0, ((1, 4), (2, 4), (3, 2)), jnp.float32),
        "first_weight": normal_values(key_list[2], (WIDTH, FEATURES), FEATURES ** -0.5, 0.625, (), jnp.float32),
        "first_bias": normal_values(key_list[3], (WIDTH,), 0.5, 3.0, (), jnp.float32),
        "second_weight": normal_values(key_list[4], (3, WIDTH), WIDTH ** -0.5, 1.0, (), jnp.float32),
        "second_bias": normal_values(key_list[5], (3,), 0.5, 3.0, (), jnp.float32),
        "sweeps": draw_sweeps(jax.random.fold_in(key_list[7], 71), 0),
    }


OMEGA = 0.8


def stencil_features(region):
    span_y = region.shape[2] - 2
    span_z = region.shape[3] - 2
    shifted = [region[:, first, second:second + span_y, third:third + span_z]
               for first in range(3) for second in range(3) for third in range(3)]
    return jnp.stack(shifted).reshape(27 * region.shape[0], span_y * span_z)


def six_point(field, padded):
    beside = padded[2:, 1:-1, 1:-1] + padded[:-2, 1:-1, 1:-1]
    beside = beside + padded[1:-1, 2:, 1:-1] + padded[1:-1, :-2, 1:-1]
    beside = beside + padded[1:-1, 1:-1, 2:] + padded[1:-1, 1:-1, :-2]
    return 6.0 * field - beside


def laplace_local(field):
    return six_point(field, jnp.pad(field, 1))


def relax(guess, source):
    return guess + OMEGA * (source - laplace_local(guess)) / 6.0


def restrict(residue):
    half = [extent // 2 for extent in residue.shape]
    return 0.5 * residue.reshape(half[0], 2, half[1], 2, half[2], 2).sum(axis=(1, 3, 5))


def prolong(coarse):
    return jnp.repeat(jnp.repeat(jnp.repeat(coarse, 2, axis=0), 2, axis=1), 2, axis=2)


def vcycle(source, sweeps, level):
    guess = OMEGA * source / 6.0
    if level == LEVELS:
        return lax.fori_loop(1, COARSE_SWEEPS, lambda number, state: relax(state, source), guess)
    repeats = sweeps[level]
    guess = lax.fori_loop(1, repeats, lambda number, state: relax(state, source), guess)
    residue = source - laplace_local(guess)
    guess = guess + prolong(vcycle(restrict(residue), sweeps, level + 1))
    return lax.fori_loop(0, repeats, lambda number, state: relax(state, source), guess)


def divergence(padded):
    total = padded[0, 2:, 1:-1, 1:-1] - padded[0, :-2, 1:-1, 1:-1]
    total = total + padded[1, 1:-1, 2:, 1:-1] - padded[1, 1:-1, :-2, 1:-1]
    total = total + padded[2, 1:-1, 1:-1, 2:] - padded[2, 1:-1, 1:-1, :-2]
    return 0.5 * total


def gradient(padded):
    return 0.5 * jnp.stack([padded[2:, 1:-1, 1:-1] - padded[:-2, 1:-1, 1:-1],
                            padded[1:-1, 2:, 1:-1] - padded[1:-1, :-2, 1:-1],
                            padded[1:-1, 1:-1, 2:] - padded[1:-1, 1:-1, :-2]])


def project(field, sweeps):
    source = divergence(jnp.pad(field, ((0, 0), (1, 1), (1, 1), (1, 1))))
    pressure = vcycle(source, sweeps, 0)
    for repeat_index in range(CYCLES - 1):
        pressure = pressure + vcycle(source - laplace_local(pressure), sweeps, 0)
    return field + gradient(jnp.pad(pressure, 1))


def corrections(near, first_weight, first_bias, second_weight, second_bias, planes):
    span_y = near.shape[2] - 2
    span_z = near.shape[3] - 2

    def one_plane(index):
        region = lax.dynamic_slice_in_dim(near, index, 3, 1)
        feats = stencil_features(region)
        hidden = jax.nn.silu(jnp.dot(first_weight, feats, precision=lax.Precision.HIGHEST) + first_bias[:, None])
        return jnp.dot(second_weight, hidden, precision=lax.Precision.HIGHEST) + second_bias[:, None]

    result = lax.map(one_plane, jnp.arange(planes, dtype=jnp.int32))
    return result.reshape(planes, 3, span_y, span_z).transpose(1, 0, 2, 3)


def back_planes(wide, cot_pad, first_weight, first_bias, second_weight, planes):
    span_y = cot_pad.shape[2] - 2
    span_z = cot_pad.shape[3] - 2

    def one_plane(index):
        region = lax.dynamic_slice_in_dim(wide, index, 3, 1)
        feats = stencil_features(region)
        pre = jnp.dot(first_weight, feats, precision=lax.Precision.HIGHEST) + first_bias[:, None]
        sig = jax.nn.sigmoid(pre)
        slope = sig * (1.0 + pre * (1.0 - sig))
        incoming = lax.dynamic_index_in_dim(cot_pad, index, 1, keepdims=False).reshape(3, -1)
        back = jnp.dot(second_weight.T, incoming, precision=lax.Precision.HIGHEST) * slope
        spread = jnp.dot(first_weight.T, back, precision=lax.Precision.HIGHEST)
        spread = spread.reshape(3, 3, 3, 3, span_y + 2, span_z + 2)
        parts = []
        for first in range(3):
            total = jnp.zeros((3, span_y, span_z), spread.dtype)
            for second in range(3):
                for third in range(3):
                    total = total + spread[first, second, third, :, 2 - second:2 - second + span_y,
                                           2 - third:2 - third + span_z]
            parts.append(total)
        return jnp.stack(parts)

    pieces = lax.map(one_plane, jnp.arange(planes + 2, dtype=jnp.int32))
    return pieces[:-2, 2] + pieces[1:-1, 1] + pieces[2:, 0]


def reference(velocity, cotangent, first_weight, first_bias, second_weight, second_bias, sweeps):
    planes = velocity.shape[1]
    near = jnp.pad(velocity, ((0, 0), (1, 1), (1, 1), (1, 1)))
    closed = velocity + corrections(near, first_weight, first_bias, second_weight, second_bias, planes)
    updated = project(closed, sweeps)
    adjoint_closed = project(cotangent, sweeps)
    wide = jnp.pad(velocity, ((0, 0), (2, 2), (2, 2), (2, 2)))
    cot_pad = jnp.pad(adjoint_closed, ((0, 0), (1, 1), (1, 1), (1, 1)))
    summed = back_planes(wide, cot_pad, first_weight, first_bias, second_weight, planes)
    grad_velocity = adjoint_closed + summed.transpose(1, 0, 2, 3)
    return updated, grad_velocity
```

```python
import functools

import jax
import jax.numpy as jnp
import numpy as np
from jax import lax
from jax.experimental import pallas as pl
from jax.experimental.pallas import tpu as pltpu
from jax.sharding import PartitionSpec as P

LEVELS = 3
COARSE_SWEEPS = 6


OMEGA = 0.8


def with_halo(block, sides, width):
    for axis, dim in sides:
        count = lax.axis_size(axis)
        forward = [(i, i + 1) for i in range(count - 1)]
        backward = [(target, source) for source, target in forward]
        low = lax.ppermute(
            lax.slice_in_dim(block, block.shape[dim] - width, None, axis=dim), axis, forward
        )
        high = lax.ppermute(lax.slice_in_dim(block, 0, width, axis=dim), axis, backward)
        block = jnp.concatenate([low, block, high], axis=dim)
    return block


def stencil_features(region):
    span_y = region.shape[2] - 2
    span_z = region.shape[3] - 2
    shifted = [
        region[:, first, second : second + span_y, third : third + span_z]
        for first in range(3)
        for second in range(3)
        for third in range(3)
    ]
    return jnp.stack(shifted).reshape(27 * region.shape[0], span_y * span_z)


def six_point(field, padded):
    beside = padded[:, 2:, 1:-1, 1:-1] + padded[:, :-2, 1:-1, 1:-1]
    beside = beside + padded[:, 1:-1, 2:, 1:-1] + padded[:, 1:-1, :-2, 1:-1]
    beside = beside + padded[:, 1:-1, 1:-1, 2:] + padded[:, 1:-1, 1:-1, :-2]
    return 6.0 * field - beside


def near_faces(field):
    return with_halo(field, (("gx", 1), ("gy", 2), ("gz", 3)), 1)


def laplace_shared(field):
    return six_point(field, near_faces(field))


def relax(guess, source):
    return guess + OMEGA * (source - laplace_shared(guess)) / 6.0


def restrict(residue):
    batch, size_x, size_y, size_z = residue.shape
    folded = residue.reshape(batch, size_x // 2, 2, size_y // 2, 2, size_z // 2, 2)
    return 0.5 * folded.sum(axis=(2, 4, 6))


def prolong(coarse):
    return jnp.repeat(jnp.repeat(jnp.repeat(coarse, 2, axis=1), 2, axis=2), 2, axis=3)


def coarse_spread(source, sweeps):
    guess = OMEGA * source / 6.0
    return lax.fori_loop(1, COARSE_SWEEPS, lambda number, state: relax(state, source), guess)


def vcycle(source, sweeps, level, coarse_solve, bottom):
    if level == bottom:
        return coarse_solve(source, sweeps)
    repeats = sweeps[level]
    guess = OMEGA * source / 6.0
    guess = lax.fori_loop(1, repeats, lambda number, state: relax(state, source), guess)
    residue = source - laplace_shared(guess)
    guess = guess + prolong(vcycle(restrict(residue), sweeps, level + 1, coarse_solve, bottom))
    return lax.fori_loop(0, repeats, lambda number, state: relax(state, source), guess)


def divergence(padded):
    total = padded[:, 0, 2:, 1:-1, 1:-1] - padded[:, 0, :-2, 1:-1, 1:-1]
    total = total + padded[:, 1, 1:-1, 2:, 1:-1] - padded[:, 1, 1:-1, :-2, 1:-1]
    total = total + padded[:, 2, 1:-1, 1:-1, 2:] - padded[:, 2, 1:-1, 1:-1, :-2]
    return 0.5 * total


def gradient(padded):
    return 0.5 * jnp.stack(
        [
            padded[:, 2:, 1:-1, 1:-1] - padded[:, :-2, 1:-1, 1:-1],
            padded[:, 1:-1, 2:, 1:-1] - padded[:, 1:-1, :-2, 1:-1],
            padded[:, 1:-1, 1:-1, 2:] - padded[:, 1:-1, 1:-1, :-2],
        ],
        axis=1,
    )


def project(fields, sweeps, coarse_solve, bottom):
    batch, comps, size_x, size_y, size_z = fields.shape
    padded = near_faces(fields.reshape(batch * comps, size_x, size_y, size_z))
    padded = padded.reshape(batch, comps, size_x + 2, size_y + 2, size_z + 2)
    source = divergence(padded)
    pressure = vcycle(source, sweeps, 0, coarse_solve, bottom)
    pressure = pressure + vcycle(source - laplace_shared(pressure), sweeps, 0, coarse_solve, bottom)
    return fields + gradient(near_faces(pressure))


def corrections(near, first_weight, first_bias, second_weight, second_bias, planes):
    span_y = near.shape[2] - 2
    span_z = near.shape[3] - 2

    def corrections_one_plane(index):
        region = lax.dynamic_slice_in_dim(near, index, 3, 1)
        feats = stencil_features(region)
        hidden = jax.nn.silu(
            jnp.dot(first_weight, feats, precision=lax.Precision.HIGHEST) + first_bias[:, None]
        )
        return (
            jnp.dot(second_weight, hidden, precision=lax.Precision.HIGHEST) + second_bias[:, None]
        )

    result = lax.map(corrections_one_plane, jnp.arange(planes, dtype=jnp.int32))
    return result.reshape(planes, 3, span_y, span_z).transpose(1, 0, 2, 3)


def back_planes(wide, cot_pad, first_weight, first_bias, second_weight, planes):
    span_y = cot_pad.shape[2] - 2
    span_z = cot_pad.shape[3] - 2

    def back_one_plane(index):
        region = lax.dynamic_slice_in_dim(wide, index, 3, 1)
        feats = stencil_features(region)
        pre = jnp.dot(first_weight, feats, precision=lax.Precision.HIGHEST) + first_bias[:, None]
        sig = jax.nn.sigmoid(pre)
        slope = sig * (1.0 + pre * (1.0 - sig))
        incoming = lax.dynamic_index_in_dim(cot_pad, index, 1, keepdims=False).reshape(3, -1)
        back = jnp.dot(second_weight.T, incoming, precision=lax.Precision.HIGHEST) * slope
        spread = jnp.dot(first_weight.T, back, precision=lax.Precision.HIGHEST)
        spread = spread.reshape(3, 3, 3, 3, span_y + 2, span_z + 2)
        parts = []
        for first in range(3):
            total = jnp.zeros((3, span_y, span_z), jnp.float32)
            for second in range(3):
                for third in range(3):
                    total = (
                        total
                        + spread[
                            first,
                            second,
                            third,
                            :,
                            2 - second : 2 - second + span_y,
                            2 - third : 2 - third + span_z,
                        ]
                    )
            parts.append(total)
        return jnp.stack(parts)

    pieces = lax.map(back_one_plane, jnp.arange(planes + 2, dtype=jnp.int32))
    return pieces[:-2, 2] + pieces[1:-1, 1] + pieces[2:, 0]


def shards(velocity, cotangent, first_weight, first_bias, second_weight, second_bias, sweeps):
    planes = velocity.shape[1]
    near = with_halo(velocity, (("gx", 1), ("gy", 2), ("gz", 3)), 1)
    coarse_solve, bottom = (coarse_spread, LEVELS)
    closed = velocity + corrections(
        near, first_weight, first_bias, second_weight, second_bias, planes
    )
    updated = project(closed[None], sweeps, coarse_solve, bottom)[0]
    adjoint_closed = project(cotangent[None], sweeps, coarse_solve, bottom)[0]
    wide = with_halo(velocity, (("gx", 1), ("gy", 2), ("gz", 3)), 2)
    cot_pad = with_halo(adjoint_closed, (("gx", 1), ("gy", 2), ("gz", 3)), 1)
    summed = back_planes(wide, cot_pad, first_weight, first_bias, second_weight, planes)
    grad_velocity = adjoint_closed + summed.transpose(1, 0, 2, 3)
    return (updated, grad_velocity)


AXES = ("gx", "gy", "gz")
STEP = OMEGA / 6.0
KEEP = 1.0 - OMEGA
WIDTH = 32
SPAN = 10
ROWS = 112
PLANE = 3 * ROWS
DEEP = 1024
HIDDEN = SPAN * WIDTH
SENT = 72
F32 = jnp.float32
BF16 = jnp.bfloat16


def roll(value, shift, axis):
    return pltpu.roll(value, shift, axis)


def lanes(shape=(8, 128)):
    return lax.broadcasted_iota(jnp.int32, shape, len(shape) - 1)


def rows_of(shape=(8, 128)):
    return lax.broadcasted_iota(jnp.int32, shape, len(shape) - 2)


def split(value):
    high = value.astype(BF16)
    return high, (value - high.astype(F32)).astype(BF16)


def exact(left, right):
    return jnp.dot(left, right, precision=lax.Precision.HIGHEST, preferred_element_type=F32)


def once(left, right):
    return jnp.dot(left, right, preferred_element_type=F32)


def tables():
    spread = np.zeros((3, 128, DEEP), np.float32)
    tag = np.full((8, DEEP), -1, np.int32)
    for a in range(3):
        for t in range(3):
            for c in range(3):
                for k in range(3):
                    for y in range(12):
                        column = a * PLANE + t * ROWS + (c * 3 + k) * 12 + y
                        tag[0, column] = y
                        tag[1, column] = t
                        for b in range(3):
                            spread[b, 3 * (9 * a + 3 * b + c) + k, column] = 1.0
    tag[1, 108] = 10
    tag[1, 2 * ROWS + 108] = 12
    tiled = np.zeros((128, DEEP), np.float32)
    for t in range(3):
        for y in range(SPAN):
            for w in range(WIDTH):
                column = t * HIDDEN + y * WIDTH + w
                tiled[w, column] = 1.0
                tag[2, column] = y
                tag[3, column] = t
    lift = np.zeros((3, 216, 128), np.float32)
    height = np.zeros((216, 128), np.int32)
    for a in range(3):
        for c in range(3):
            for k in range(3):
                for y in range(8):
                    row = a * 72 + (c * 3 + k) * 8 + y
                    height[row] = y + 2
                    for b in range(3):
                        lift[b, row, 3 * (9 * a + 3 * b + c) + k] = 1.0
    inner = np.zeros((128, 256), np.float32)
    for t in range(3):
        for k in range(3):
            for y in range(16):
                column = t * 48 + k * 16 + y
                inner[k, column] = 1.0
                tag[4, column] = y
                tag[5, column] = t
    return (jnp.asarray(spread, BF16), jnp.asarray(tag), jnp.asarray(tiled, BF16),
            jnp.asarray(lift, BF16), jnp.asarray(height), jnp.asarray(inner, BF16))


def weights_kernel(first_ref, turned_ref, bias_ref, second_ref, lifted_ref, spread_ref, tag_ref, tiled_ref,
                   lift_ref, height_ref, inner_ref, wide_ref, tall_ref, out_ref, back_ref):
    high, low = split(first_ref[...])
    term = tag_ref[1:2, :]
    bias_high, bias_low = split(bias_ref[...])
    bias = jnp.where(term == 10, bias_high.astype(F32)[:, 0:1], 0.0)
    bias = bias + jnp.where(term == 12, bias_low.astype(F32)[:, 0:1], 0.0)
    parts = []
    for b in range(3):
        chosen = jnp.where(term == 2, once(low, spread_ref[b]), once(high, spread_ref[b]))
        parts.append(chosen)
    for y in range(SPAN):
        total = bias
        for b in range(3):
            total = total + jnp.where(tag_ref[0:1, :] == y + b, parts[b], 0.0)
        wide_ref[y * WIDTH:(y + 1) * WIDTH, :] = total.astype(BF16)
    high, low = split(turned_ref[...])
    term = tag_ref[3:4, :]
    place = tag_ref[2:3, :]
    copies = jnp.where(term == 2, once(low, tiled_ref[...]), once(high, tiled_ref[...])).astype(BF16)
    total = jnp.zeros((216, DEEP), F32)
    for b in range(3):
        here = height_ref[:, 0:1] - b == place
        total = total + jnp.where(here, once(lift_ref[b], copies), 0.0)
    tall_ref[...] = total.astype(BF16)
    high, low = split(second_ref[...])
    copies = jnp.where(term == 2, once(low, tiled_ref[...]), once(high, tiled_ref[...]))
    row = rows_of((16, DEEP))
    for k in range(3):
        out_ref[16 * k:16 * k + 16, :] = jnp.where(row == place, copies[k:k + 1, :], 0.0).astype(BF16)
    high, low = split(lifted_ref[...])
    term = tag_ref[5:6, 0:256]
    copies = jnp.where(term == 2, once(low, inner_ref[...]), once(high, inner_ref[...]))
    for y in range(SPAN):
        back_ref[y * WIDTH:(y + 1) * WIDTH, :] = jnp.where(tag_ref[4:5, 0:256] == y, copies, 0.0).astype(BF16)


def send_rows(get, flat_ref, sent_ref):
    lane = lanes()
    row = rows_of()
    faces = jnp.zeros((8, 128), F32)
    for x in range(8):
        up = get(2, x + 1, 1)
        value = get(0, x + 2, 1) - get(0, x, 1) + get(1, x + 1, 2) - get(1, x + 1, 0)
        value = value + jnp.where(lane == 127, 0.0, roll(up, 127, 1)) - jnp.where(lane == 0, 0.0, roll(up, 1, 1))
        flat_ref[8 * x:8 * x + 8, :] = 0.5 * value
        faces = faces + jnp.where(lane == 8 * x + row, 0.5 * up[:, 0:1], 0.0)
        faces = faces - jnp.where(lane == 64 + 8 * x + row, 0.5 * up[:, 127:128], 0.0)
    first = lax.broadcasted_iota(jnp.int32, (128, 128), 0)
    second = lanes((128, 128))
    order = jnp.where((first % 2) * 64 + first // 2 == second, 1.0, 0.0)
    sent_ref[0:64, :] = exact(flat_ref[...], order)
    sent_ref[64:72, :] = jnp.where(row == 0, jnp.sum(faces, axis=0, keepdims=True), 0.0)


def cot_rows_kernel(ext_ref, sent_ref, flat_ref):
    send_rows(lambda k, x, y: ext_ref[6 + k, x + 1, pl.ds(y + 1, 8), :], flat_ref, sent_ref)


def forward_kernel(ids_ref, bias_ref, ext_ref, wide_ref, out_ref, closed_ref, slope_ref, sent_ref,
                   plane_ref, feat_ref, hid_ref, ce_ref, flat_ref):
    gx, gy, gz = ids_ref[0], ids_ref[1], ids_ref[2]
    low_side = jnp.where(gz == 0, 1.0, 0.0)
    high_side = 1.0 - low_side
    lane = lanes((12, 128))
    pad_row = rows_of((8, 128))
    plane_ref[104:112, :] = jnp.where(pad_row == 4, 1.0, 0.0)
    feat_ref[7 * PLANE:7 * PLANE + 16, :] = jnp.zeros((16, 256), BF16)
    hid_ref[3 * HIDDEN:DEEP, :] = jnp.zeros((DEEP - 3 * HIDDEN, 256), BF16)
    for step in range(7):
        for half in range(2):
            at = step + 5 * half
            for k in range(3):
                here = ext_ref[k, at]
                there = ext_ref[3 + k, at]
                below = roll(jnp.where(lane == 127, there * high_side, here), 1, 1)
                above = roll(jnp.where(lane == 0, there * low_side, here), 127, 1)
                for c, piece in ((0, below), (1, here), (2, above)):
                    plane_ref[pl.ds((c * 3 + k) * 12, 12), :] = piece
            high, low = split(plane_ref[...])
            col = slice(128 * half, 128 * half + 128)
            feat_ref[step * PLANE:step * PLANE + ROWS, col] = high
            feat_ref[step * PLANE + ROWS:step * PLANE + 2 * ROWS, col] = low
            feat_ref[step * PLANE + 2 * ROWS:step * PLANE + 3 * ROWS, col] = high
    row = rows_of((16, 128))
    inside = jnp.where((row == 0) & (gy == 0), 0.0, 1.0)
    inside = jnp.where((row == 9) & (gy == ids_ref[4] - 1), 0.0, inside)
    inside = jnp.where(row > 9, 0.0, inside)
    for x in range(5):
        pre = once(wide_ref[...], feat_ref[x * PLANE:x * PLANE + DEEP, :])
        sig = 0.5 * jnp.tanh(0.5 * pre) + 0.5
        slope_ref[x] = sig * (1.0 + pre * (1.0 - sig))
        high, low = split(pre * sig)
        hid_ref[0:HIDDEN, :] = high
        hid_ref[HIDDEN:2 * HIDDEN, :] = low
        hid_ref[2 * HIDDEN:3 * HIDDEN, :] = high
        result = once(out_ref[...], hid_ref[...])
        for half in range(2):
            e = x + 5 * half
            mask = inside
            if e == 0:
                mask = inside * jnp.where(gx == 0, 0.0, 1.0)
            if e == 9:
                mask = inside * jnp.where(gx == ids_ref[3] - 1, 0.0, 1.0)
            for k in range(3):
                ce_ref[k, e] = (result[16 * k:16 * k + 16, 128 * half:128 * half + 128] + bias_ref[k]) * mask
                ce_ref[k, e, 0:10, :] = ce_ref[k, e, 0:10, :] + ext_ref[k, e + 1, 1:11, :]
    for k in range(3):
        for x in range(8):
            closed_ref[k, x] = ce_ref[k, x + 1, 1:9, :]
    send_rows(lambda k, x, y: ce_ref[k, x, pl.ds(y, 8), :], flat_ref, sent_ref)


def around(grid, wide, masks):
    (x_low, x_high, y_low, y_high) = masks
    lane = lanes()
    size = len(grid[0])
    result = []
    for c in range(2):
        plane = []
        for x in range(size):
            line = []
            for y in range(size):
                here = grid[c][x][y]
                total = jnp.where(lane >= wide, roll(here, wide, 1), 0.0)
                total = total + jnp.where(lane < 128 - wide, roll(here, 128 - wide, 1), 0.0)
                total = total + (grid[c][x - 1][y] if x > 0 else roll(grid[c][size - 1][y], 2, 0) * x_low)
                total = total + (grid[c][x + 1][y] if x < size - 1 else roll(grid[c][0][y], 6, 0) * x_high)
                if y > 0:
                    total = total + grid[c][x][y - 1]
                else:
                    edge = grid[1 - c][x][size - 1]
                    total = total + (edge if c == 1 else roll(edge, 1, 0) * y_low)
                if y < size - 1:
                    total = total + grid[c][x][y + 1]
                else:
                    edge = grid[1 - c][x][0]
                    total = total + (edge if c == 0 else roll(edge, 7, 0) * y_high)
                line.append(total)
            plane.append(line)
        result.append(plane)
    return result


def over(function, *grids):
    size = len(grids[0][0])
    return [[[function(*(g[c][x][y] for g in grids)) for y in range(size)] for x in range(size)] for c in range(2)]


def flat(grid):
    return tuple(v for plane in grid for line in plane for v in line)


def unflat(values, size):
    values = list(values)
    return [[[values[(c * size + x) * size + y] for y in range(size)] for x in range(size)] for c in range(2)]


def relax_level(guess, source, wide, masks):
    return over(lambda g, s, n: KEEP * g + STEP * (s + n), guess, source, around(guess, wide, masks))


def residue_level(guess, source, wide, masks):
    return over(lambda g, s, n: s - 6.0 * g + n, guess, source, around(guess, wide, masks))


def coarser(grid, wide):
    lane = lanes()
    size = len(grid[0]) // 2
    even = (lane // wide) % 2 == 0
    result = []
    for c in range(2):
        plane = []
        for x in range(size):
            line = []
            for y in range(size):
                t = grid[c][2 * x][2 * y] + grid[c][2 * x][2 * y + 1]
                t = t + grid[c][2 * x + 1][2 * y] + grid[c][2 * x + 1][2 * y + 1]
                line.append(0.5 * (t + jnp.where(even, roll(t, 128 - wide, 1), roll(t, wide, 1))))
            plane.append(line)
        result.append(plane)
    return result


def add_coarse(grid, coarse):
    size = len(grid[0])
    return [[[grid[c][x][y] + coarse[c][x // 2][y // 2] for y in range(size)] for x in range(size)] for c in range(2)]


def level_solve(source, level, sweeps_ref, masks):
    wide = 1 << (level - 1)
    size = len(source[0])
    guess = over(lambda s: STEP * s, source)
    if level == LEVELS:
        for _ in range(COARSE_SWEEPS - 1):
            guess = relax_level(guess, source, wide, masks)
        return guess
    repeats = sweeps_ref[level]

    def body(number, state):
        return flat(relax_level(unflat(state, size), source, wide, masks))

    guess = unflat(lax.fori_loop(1, repeats, body, flat(guess)), size)
    coarse = coarser(residue_level(guess, source, wide, masks), wide)
    guess = add_coarse(guess, level_solve(coarse, level + 1, sweeps_ref, masks))
    return unflat(lax.fori_loop(0, repeats, body, flat(guess)), size)


def project_kernel(ext, ids_ref, sweeps_ref, mine_ref, other_ref, field_ref, result_ref,
                   r_ref, q_ref, x_ref, p_ref, c_ref, win_ref, nat_ref):
    gx, gy, gz = ids_ref[0], ids_ref[1], ids_ref[2]
    core = lax.rem(gy, 2)
    lane = lanes()
    sub = rows_of()
    x_low = jnp.where(sub >= 2, 1.0, 0.0)
    x_high = jnp.where(sub < 6, 1.0, 0.0)
    y_low = jnp.where(sub % 2 == 1, 1.0, 0.0)
    y_high = jnp.where(sub % 2 == 0, 1.0, 0.0)
    masks = (x_low, x_high, y_low, y_high)
    z_low = jnp.where(lane != 0, 1.0, 0.0)
    z_high = jnp.where(lane != 127, 1.0, 0.0)
    lower = lane < 64

    for source_ref, slot in ((mine_ref, core), (other_ref, 1 - core)):
        face0 = source_ref[pl.ds(64, 8, stride=2 * SENT), :]
        face1 = source_ref[pl.ds(SENT + 64, 8, stride=2 * SENT), :]

        def place(x, faces, source_ref=source_ref, slot=slot):
            face0, face1 = faces
            for y in range(8):
                first = source_ref[pl.ds(8 * x + y, 8, stride=2 * SENT), :]
                second = source_ref[pl.ds(SENT + 8 * x + y, 8, stride=2 * SENT), :]
                even = jnp.where(lower, first, roll(second, 64, 1))
                odd = jnp.where(lower, roll(first, 64, 1), second)
                even = even + jnp.where(lane == 64, roll(face0, (128 - y) % 128, 1), 0.0)
                odd = odd + jnp.where(lane == 63, roll(face1, 63 - y, 1), 0.0)
                r_ref[slot, 0, x, y] = even
                r_ref[slot, 1, x, y] = odd
            return roll(face0, 120, 1), roll(face1, 120, 1)

        lax.fori_loop(0, 8, place, (face0, face1))

    def fill(now):
        for c in range(2):
            for zi in range(2):
                for y in range(8):
                    x_ref[now, c, zi, 0, y] = roll(x_ref[now, c, zi, 8, y], 2, 0) * x_low
                    x_ref[now, c, zi, 9, y] = roll(x_ref[now, c, zi, 1, y], 6, 0) * x_high

    def near(now, c, x):
        own = [[x_ref[now, c, zi, x, y] for y in range(8)] for zi in range(2)]
        sums = []
        for zi in range(2):
            line = []
            down = x_ref[now, 1 - c, zi, x, 7]
            up = x_ref[now, 1 - c, zi, x, 0]
            if c == 0:
                down = roll(down, 1, 0) * y_low
            else:
                up = roll(up, 7, 0) * y_high
            for y in range(8):
                beside = own[1 - zi][y]
                if zi == 0:
                    total = beside + roll(beside, 1, 1) * z_low
                else:
                    total = beside + roll(beside, 127, 1) * z_high
                total = total + x_ref[now, c, zi, x - 1, y] + x_ref[now, c, zi, x + 1, y]
                total = total + (own[zi][y - 1] if y > 0 else down) + (own[zi][y + 1] if y < 7 else up)
                line.append(total)
            sums.append(line)
        return own, sums

    def sweep(number, now, s_ref):
        def one(x, carry):
            for c in range(2):
                own, sums = near(now, c, x + 1)
                for zi in range(2):
                    for y in range(8):
                        x_ref[1 - now, c, zi, x + 1, y] = KEEP * own[zi][y] + STEP * (s_ref[c, zi, x, y] + sums[zi][y])
            return carry

        lax.fori_loop(0, 8, one, 0)
        fill(1 - now)
        return 1 - now

    def vcycle0(s_ref):
        def start(x, carry):
            for c in range(2):
                for zi in range(2):
                    for y in range(8):
                        x_ref[0, c, zi, x + 1, y] = STEP * s_ref[c, zi, x, y]
            return carry

        lax.fori_loop(0, 8, start, 0)
        fill(0)
        repeats = sweeps_ref[0]
        now = lax.fori_loop(1, repeats, lambda n, s: sweep(n, s, s_ref), jnp.int32(0))

        def down(pair, carry):
            for c in range(2):
                total = [None] * 4
                for step in range(2):
                    x = 2 * pair + step
                    own, sums = near(now, c, x + 1)
                    for zi in range(2):
                        for y in range(8):
                            e = s_ref[c, zi, x, y] - 6.0 * own[zi][y] + sums[zi][y]
                            total[y // 2] = e if total[y // 2] is None else total[y // 2] + e
                for y in range(4):
                    c_ref[c, pair, y] = 0.5 * total[y]
            return carry

        lax.fori_loop(0, 4, down, 0)
        coarse = [[[c_ref[c, x, y] for y in range(4)] for x in range(4)] for c in range(2)]
        coarse = level_solve(coarse, 1, sweeps_ref, masks)
        for c in range(2):
            for x in range(4):
                for y in range(4):
                    c_ref[c, x, y] = coarse[c][x][y]

        def up(x, carry):
            for c in range(2):
                for y in range(4):
                    value = c_ref[c, x // 2, y]
                    for zi in range(2):
                        for step in range(2):
                            at = 2 * y + step
                            x_ref[now, c, zi, x + 1, at] = x_ref[now, c, zi, x + 1, at] + value
            return carry

        lax.fori_loop(0, 8, up, 0)
        fill(now)
        return lax.fori_loop(0, repeats, lambda n, s: sweep(n, s, s_ref), now)

    now = vcycle0(r_ref)

    def between(x, carry):
        for c in range(2):
            own, sums = near(now, c, x + 1)
            for zi in range(2):
                for y in range(8):
                    p_ref[c, zi, x, y] = own[zi][y]
                    q_ref[c, zi, x, y] = r_ref[c, zi, x, y] - 6.0 * own[zi][y] + sums[zi][y]
        return carry

    lax.fori_loop(0, 8, between, 0)
    now = vcycle0(q_ref)

    x_rows = x_ref.reshape(2 * 2 * 2 * 10 * 8 * 8, 128)
    p_rows = p_ref.reshape(2 * 2 * 8 * 8 * 8, 128)
    last_x, last_y = ids_ref[3] - 1, ids_ref[4] - 1
    for wx in range(12):
        dx = -1 if wx < 2 else (1 if wx > 9 else 0)
        xi = (wx - 2) % 8
        bx = gx + dx
        for dy in (-1, 0, 1):
            by = gy + dy
            ok = (bx >= 0) & (bx <= last_x) & (by >= 0) & (by <= last_y)
            ax = jnp.clip(bx, 0, last_x)
            ay = jnp.clip(by, 0, last_y)
            at = ax * 2 + ay // 2
            c = lax.rem(ay, 2)
            for zi in range(2):
                first = x_rows[pl.ds((((now * 2 + c) * 2 + zi) * 10 + xi + 1) * 64 + at, 8, stride=8), :]
                second = p_rows[pl.ds(((c * 2 + zi) * 8 + xi) * 64 + at, 8, stride=8), :]
                win_ref[wx * 24 + 8 * (dy + 1):wx * 24 + 8 * (dy + 1) + 8, 128 * zi:128 * zi + 128] = jnp.where(
                    ok, first + second, 0.0)
    source = lax.broadcasted_iota(jnp.int32, (256, 256), 0)
    target = lanes((256, 256))
    depth = 2 * (source % 128) + source // 128
    wanted = jnp.where(target == 255, -1, target) + gz * 128
    pick = jnp.where((depth == wanted) & ((target <= 128) | (target == 255)), 1.0, 0.0)
    nat_ref[...] = exact(win_ref[...], pick)

    size = 16 if ext else 8
    count = 10 if ext else 8
    lane = lanes((count, 128))
    row = rows_of((count, 128))
    for i in range(count):
        x = i - 1 if ext else i
        top = 7 if ext else 8
        base = (x + 2) * 24 + top
        mid = nat_ref[pl.ds(base, count), 0:128]
        tail = nat_ref[pl.ds(base, count), 128:256]
        sx = nat_ref[pl.ds(base + 24, count), 0:128] - nat_ref[pl.ds(base - 24, count), 0:128]
        sy = nat_ref[pl.ds(base + 1, count), 0:128] - nat_ref[pl.ds(base - 1, count), 0:128]
        sz = roll(jnp.where(lane == 0, tail, mid), 127, 1) - roll(jnp.where(lane == 127, tail, mid), 1, 1)
        for k, s in enumerate((sx, sy, sz)):
            if ext:
                value = field_ref[6 + k, x + 2, 1:11, :] + 0.5 * s
                good = jnp.where((row == 0) & (gy == 0), 0.0, 1.0)
                good = jnp.where((row == 9) & (gy == last_y), 0.0, good)
                if i == 0:
                    good = good * jnp.where(gx == 0, 0.0, 1.0)
                if i == 9:
                    good = good * jnp.where(gx == last_x, 0.0, 1.0)
                result_ref[k, i] = jnp.zeros((16, 128), F32)
                result_ref[k, i, 0:10, :] = value * good
            else:
                result_ref[k, i] = field_ref[k, i] + 0.5 * s


def backward_kernel(ids_ref, adj_ref, slope_ref, tall_ref, back_ref, grad_ref, over_ref, in_ref, bb_ref, acc_ref):
    gz = ids_ref[2]
    in_ref[144:256, :] = jnp.zeros((112, 256), BF16)
    bb_ref[3 * HIDDEN:DEEP, :] = jnp.zeros((DEEP - 3 * HIDDEN, 256), BF16)
    acc_ref[...] = jnp.zeros(acc_ref.shape, F32)
    for x in range(5):
        for half in range(2):
            col = slice(128 * half, 128 * half + 128)
            for k in range(3):
                high, low = split(adj_ref[k, x + 5 * half])
                in_ref[16 * k:16 * k + 16, col] = high
                in_ref[48 + 16 * k:64 + 16 * k, col] = low
                in_ref[96 + 16 * k:112 + 16 * k, col] = high
        high, low = split(once(back_ref[...], in_ref[...]) * slope_ref[x])
        bb_ref[0:HIDDEN, :] = high
        bb_ref[HIDDEN:2 * HIDDEN, :] = low
        bb_ref[2 * HIDDEN:3 * HIDDEN, :] = high
        total = once(tall_ref[...], bb_ref[...])
        for half in range(2):
            for a in range(3):
                at = x + 5 * half + a
                acc_ref[at] = acc_ref[at] + total[72 * a:72 * a + 72, 128 * half:128 * half + 128]
    lane = lanes()
    row = rows_of()
    for k in range(3):
        packed = jnp.zeros((8, 128), F32)
        for x in range(8):
            low = acc_ref[x + 2, 8 * k:8 * k + 8, :]
            mid = acc_ref[x + 2, 24 + 8 * k:32 + 8 * k, :]
            high = acc_ref[x + 2, 48 + 8 * k:56 + 8 * k, :]
            value = adj_ref[k, x + 1, 1:9, :] + mid
            value = value + jnp.where(lane == 127, 0.0, roll(low, 127, 1))
            grad_ref[k, x] = value + jnp.where(lane == 0, 0.0, roll(high, 1, 1))
            out = jnp.where(gz == 0, high[:, 127:128], low[:, 0:1])
            packed = packed + jnp.where(lane == 8 * x + row, out, 0.0)
        over_ref[k:k + 1, :] = jnp.sum(packed, axis=0, keepdims=True)
    over_ref[3:8, :] = jnp.zeros((5, 128), F32)


def join_kernel(ids_ref, part_ref, over_ref, grad_ref):
    gz = ids_ref[2]
    lane = lanes()
    row = rows_of()
    edge = jnp.where(gz == 0, 127, 0)
    for k in range(3):
        for x in range(8):
            column = jnp.sum(jnp.where(lane == 8 * x + row, over_ref[k:k + 1, :], 0.0), axis=1, keepdims=True)
            grad_ref[k, x] = part_ref[k, x] + jnp.where(lane == edge, column, 0.0)


VMEM = pl.BlockSpec(memory_space=pltpu.VMEM)
SMEM = pl.BlockSpec(memory_space=pltpu.SMEM)


def call(kernel, specs, shapes, scratch, *operands, flops=0, size=1 << 20):
    return pl.pallas_call(
        kernel,
        in_specs=specs,
        out_specs=[VMEM] * len(shapes),
        out_shape=[jax.ShapeDtypeStruct(s, t) for s, t in shapes],
        scratch_shapes=scratch,
        compiler_params=pltpu.CompilerParams(vmem_limit_bytes=40 * 2**20),
        cost_estimate=pl.CostEstimate(flops=flops, bytes_accessed=size, transcendentals=0),
    )(*operands)


def trade(block, axis, dim, width):
    count = lax.axis_size(axis)
    odd = lax.rem(lax.axis_index(axis), 2) == 1
    low = lax.slice_in_dim(block, 0, width, axis=dim)
    high = lax.slice_in_dim(block, block.shape[dim] - width, None, axis=dim)
    pairs = [(i, i ^ 1) for i in range(count)]
    gaps = [(i, i + 1) for i in range(1, count - 1, 2)]
    gaps = gaps + [(j, i) for i, j in gaps]
    first = lax.ppermute(jnp.where(odd, low, high), axis, pairs)
    second = lax.ppermute(jnp.where(odd, high, low), axis, gaps)
    return jnp.concatenate([jnp.where(odd, first, second), block, jnp.where(odd, second, first)], axis=dim)


def gather_rows(rows):
    nx, ny, nz = (lax.axis_size(a) for a in AXES)
    groups = [[(x * ny + 2 * y + c) * nz + z for x in range(nx) for y in range(ny // 2) for z in range(nz)]
              for c in range(2)]
    count = len(groups[0])
    spread = jnp.broadcast_to(rows[None], (count,) + rows.shape)
    mine = lax.all_to_all(spread, AXES, 0, 0, axis_index_groups=groups)
    mine = mine.reshape(count * rows.shape[0], rows.shape[1])
    return mine, lax.ppermute(mine, "gy", [(i, i ^ 1) for i in range(ny)])


def project_rows(ext, ids, sweeps, mine, other, field):
    shape = (3, 10, 16, 128) if ext else (3, 8, 8, 128)
    scratch = [
        pltpu.VMEM((2, 2, 8, 8, 8, 128), F32),
        pltpu.VMEM((2, 2, 8, 8, 8, 128), F32),
        pltpu.VMEM((2, 2, 2, 10, 8, 8, 128), F32),
        pltpu.VMEM((2, 2, 8, 8, 8, 128), F32),
        pltpu.VMEM((2, 4, 4, 8, 128), F32),
        pltpu.VMEM((288, 256), F32),
        pltpu.VMEM((288, 256), F32),
    ]
    return call(functools.partial(project_kernel, ext), [SMEM, SMEM, VMEM, VMEM, VMEM], [(shape, F32)], scratch,
                ids, sweeps, mine, other, field, flops=10**9)[0]


def gathered(velocity, cotangent, first_weight, first_bias, second_weight, second_bias, sweeps):
    ids = jnp.stack([lax.axis_index("gx"), lax.axis_index("gy"), lax.axis_index("gz"),
                     jnp.int32(lax.axis_size("gx")), jnp.int32(lax.axis_size("gy"))]).astype(jnp.int32)
    partner = lax.ppermute(velocity, "gz", [(0, 1), (1, 0)])
    ext = jnp.concatenate([velocity, partner, cotangent], axis=0)
    ext = trade(ext, "gy", 2, 2)
    ext = trade(ext, "gx", 1, 2)
    features = first_weight.shape[1]
    padded = jnp.pad(first_weight, ((0, 0), (0, 128 - features)))
    turned = jnp.pad(first_weight.T, ((0, 128 - features), (0, 128 - WIDTH)))
    second = jnp.pad(second_weight, ((0, 5), (0, 128 - WIDTH)))
    lifted = jnp.pad(second_weight.T, ((0, 0), (0, 125)))
    bias = jnp.broadcast_to(first_bias[:, None], (WIDTH, 128))
    wide, tall, out, back = call(
        weights_kernel, [VMEM] * 11,
        [((HIDDEN, DEEP), BF16), ((216, DEEP), BF16), ((48, DEEP), BF16), ((HIDDEN, 256), BF16)], [],
        padded, turned, bias, second, lifted, *tables(), flops=10**8)
    cot_rows = call(cot_rows_kernel, [VMEM], [((SENT, 128), F32)], [pltpu.VMEM((64, 128), F32)], ext)[0]
    cot_mine, cot_other = gather_rows(cot_rows)
    closed, slope, rows = call(
        forward_kernel, [SMEM, SMEM, VMEM, VMEM, VMEM],
        [((3, 8, 8, 128), F32), ((5, HIDDEN, 256), F32), ((SENT, 128), F32)],
        [pltpu.VMEM((ROWS, 128), F32), pltpu.VMEM((7 * PLANE + 16, 256), BF16), pltpu.VMEM((DEEP, 256), BF16),
         pltpu.VMEM((3, 10, 16, 128), F32), pltpu.VMEM((64, 128), F32)],
        ids, second_bias, ext, wide, out, flops=10**9)
    mine, other = gather_rows(rows)
    adjoint = project_rows(True, ids, sweeps, cot_mine, cot_other, ext)
    part, over_rows = call(
        backward_kernel, [SMEM, VMEM, VMEM, VMEM, VMEM], [((3, 8, 8, 128), F32), ((8, 128), F32)],
        [pltpu.VMEM((256, 256), BF16), pltpu.VMEM((DEEP, 256), BF16), pltpu.VMEM((12, 72, 128), F32)],
        ids, adjoint, slope, tall, back, flops=10**9)
    over_rows = lax.ppermute(over_rows, "gz", [(0, 1), (1, 0)])
    updated = project_rows(False, ids, sweeps, mine, other, closed)
    grad = call(join_kernel, [SMEM, VMEM, VMEM], [((3, 8, 8, 128), F32)], [], ids, part, over_rows)[0]
    return updated, grad


def one_gather(velocity, first_weight):
    nx, ny, nz = (lax.axis_size(a) for a in AXES)
    return (velocity.shape == (3, 8, 8, 128) and nx == 4 and ny == 4 and nz == 2
            and first_weight.shape == (WIDTH, 81))


def dispatch(velocity, cotangent, first_weight, first_bias, second_weight, second_bias, sweeps):
    path = gathered if one_gather(velocity, first_weight) else shards
    return path(velocity, cotangent, first_weight, first_bias, second_weight, second_bias, sweeps)


def solution(mesh):
    return jax.shard_map(
        dispatch,
        mesh=mesh,
        in_specs=(P(None, "gx", "gy", "gz"), P(None, "gx", "gy", "gz"), P(), P(), P(), P(), P()),
        out_specs=(P(None, "gx", "gy", "gz"), P(None, "gx", "gy", "gz")),
        check_vma=False,
    )
```

```python
import functools

import jax
import jax.numpy as jnp
import numpy as np
from jax import lax
from jax.experimental import pallas as pl
from jax.experimental.pallas import tpu as pltpu
from jax.sharding import PartitionSpec as P

LEVELS = 3
COARSE_SWEEPS = 6
CYCLES = 2


OMEGA = 0.8


def with_halo(block, sides, width):
    for axis, dim in sides:
        count = lax.axis_size(axis)
        forward = [(i, i + 1) for i in range(count - 1)]
        backward = [(target, source) for source, target in forward]
        low = lax.ppermute(
            lax.slice_in_dim(block, block.shape[dim] - width, None, axis=dim), axis, forward
        )
        high = lax.ppermute(lax.slice_in_dim(block, 0, width, axis=dim), axis, backward)
        block = jnp.concatenate([low, block, high], axis=dim)
    return block


def stencil_features(region):
    span_y = region.shape[2] - 2
    span_z = region.shape[3] - 2
    shifted = [
        region[:, first, second : second + span_y, third : third + span_z]
        for first in range(3)
        for second in range(3)
        for third in range(3)
    ]
    return jnp.stack(shifted).reshape(27 * region.shape[0], span_y * span_z)


def six_point(field, padded):
    beside = padded[:, 2:, 1:-1, 1:-1] + padded[:, :-2, 1:-1, 1:-1]
    beside = beside + padded[:, 1:-1, 2:, 1:-1] + padded[:, 1:-1, :-2, 1:-1]
    beside = beside + padded[:, 1:-1, 1:-1, 2:] + padded[:, 1:-1, 1:-1, :-2]
    return 6.0 * field - beside


def near_faces(field):
    return with_halo(field, (("gx", 1), ("gy", 2), ("gz", 3)), 1)


def laplace_shared(field):
    return six_point(field, near_faces(field))


def relax(guess, source):
    return guess + OMEGA * (source - laplace_shared(guess)) / 6.0


def restrict(residue):
    batch, size_x, size_y, size_z = residue.shape
    folded = residue.reshape(batch, size_x // 2, 2, size_y // 2, 2, size_z // 2, 2)
    return 0.5 * folded.sum(axis=(2, 4, 6))


def prolong(coarse):
    return jnp.repeat(jnp.repeat(jnp.repeat(coarse, 2, axis=1), 2, axis=2), 2, axis=3)


def coarse_spread(source, sweeps):
    guess = OMEGA * source / 6.0
    return lax.fori_loop(1, COARSE_SWEEPS, lambda number, state: relax(state, source), guess)


def vcycle(source, sweeps, level, coarse_solve, bottom):
    if level == bottom:
        return coarse_solve(source, sweeps)
    repeats = sweeps[level]
    guess = OMEGA * source / 6.0
    guess = lax.fori_loop(1, repeats, lambda number, state: relax(state, source), guess)
    residue = source - laplace_shared(guess)
    guess = guess + prolong(vcycle(restrict(residue), sweeps, level + 1, coarse_solve, bottom))
    return lax.fori_loop(0, repeats, lambda number, state: relax(state, source), guess)


def divergence(padded):
    total = padded[:, 0, 2:, 1:-1, 1:-1] - padded[:, 0, :-2, 1:-1, 1:-1]
    total = total + padded[:, 1, 1:-1, 2:, 1:-1] - padded[:, 1, 1:-1, :-2, 1:-1]
    total = total + padded[:, 2, 1:-1, 1:-1, 2:] - padded[:, 2, 1:-1, 1:-1, :-2]
    return 0.5 * total


def gradient(padded):
    return 0.5 * jnp.stack(
        [
            padded[:, 2:, 1:-1, 1:-1] - padded[:, :-2, 1:-1, 1:-1],
            padded[:, 1:-1, 2:, 1:-1] - padded[:, 1:-1, :-2, 1:-1],
            padded[:, 1:-1, 1:-1, 2:] - padded[:, 1:-1, 1:-1, :-2],
        ],
        axis=1,
    )


def project(fields, sweeps, coarse_solve, bottom):
    batch, comps, size_x, size_y, size_z = fields.shape
    padded = near_faces(fields.reshape(batch * comps, size_x, size_y, size_z))
    padded = padded.reshape(batch, comps, size_x + 2, size_y + 2, size_z + 2)
    source = divergence(padded)
    pressure = vcycle(source, sweeps, 0, coarse_solve, bottom)
    pressure = pressure + vcycle(source - laplace_shared(pressure), sweeps, 0, coarse_solve, bottom)
    return fields + gradient(near_faces(pressure))


def corrections(near, first_weight, first_bias, second_weight, second_bias, planes):
    span_y = near.shape[2] - 2
    span_z = near.shape[3] - 2

    def corrections_one_plane(index):
        region = lax.dynamic_slice_in_dim(near, index, 3, 1)
        feats = stencil_features(region)
        hidden = jax.nn.silu(
            jnp.dot(first_weight, feats, precision=lax.Precision.HIGHEST) + first_bias[:, None]
        )
        return (
            jnp.dot(second_weight, hidden, precision=lax.Precision.HIGHEST) + second_bias[:, None]
        )

    result = lax.map(corrections_one_plane, jnp.arange(planes, dtype=jnp.int32))
    return result.reshape(planes, 3, span_y, span_z).transpose(1, 0, 2, 3)


def back_planes(wide, cot_pad, first_weight, first_bias, second_weight, planes):
    span_y = cot_pad.shape[2] - 2
    span_z = cot_pad.shape[3] - 2

    def back_one_plane(index):
        region = lax.dynamic_slice_in_dim(wide, index, 3, 1)
        feats = stencil_features(region)
        pre = jnp.dot(first_weight, feats, precision=lax.Precision.HIGHEST) + first_bias[:, None]
        sig = jax.nn.sigmoid(pre)
        slope = sig * (1.0 + pre * (1.0 - sig))
        incoming = lax.dynamic_index_in_dim(cot_pad, index, 1, keepdims=False).reshape(3, -1)
        back = jnp.dot(second_weight.T, incoming, precision=lax.Precision.HIGHEST) * slope
        spread = jnp.dot(first_weight.T, back, precision=lax.Precision.HIGHEST)
        spread = spread.reshape(3, 3, 3, 3, span_y + 2, span_z + 2)
        parts = []
        for first in range(3):
            total = jnp.zeros((3, span_y, span_z), jnp.float32)
            for second in range(3):
                for third in range(3):
                    total = (
                        total
                        + spread[
                            first,
                            second,
                            third,
                            :,
                            2 - second : 2 - second + span_y,
                            2 - third : 2 - third + span_z,
                        ]
                    )
            parts.append(total)
        return jnp.stack(parts)

    pieces = lax.map(back_one_plane, jnp.arange(planes + 2, dtype=jnp.int32))
    return pieces[:-2, 2] + pieces[1:-1, 1] + pieces[2:, 0]


def shards(velocity, cotangent, first_weight, first_bias, second_weight, second_bias, sweeps):
    planes = velocity.shape[1]
    near = with_halo(velocity, (("gx", 1), ("gy", 2), ("gz", 3)), 1)
    coarse_solve, bottom = (coarse_spread, LEVELS)
    closed = velocity + corrections(
        near, first_weight, first_bias, second_weight, second_bias, planes
    )
    updated = project(closed[None], sweeps, coarse_solve, bottom)[0]
    adjoint_closed = project(cotangent[None], sweeps, coarse_solve, bottom)[0]
    wide = with_halo(velocity, (("gx", 1), ("gy", 2), ("gz", 3)), 2)
    cot_pad = with_halo(adjoint_closed, (("gx", 1), ("gy", 2), ("gz", 3)), 1)
    summed = back_planes(wide, cot_pad, first_weight, first_bias, second_weight, planes)
    grad_velocity = adjoint_closed + summed.transpose(1, 0, 2, 3)
    return (updated, grad_velocity)


AXES = ("gx", "gy", "gz")
STEP = OMEGA / 6.0
KEEP = 1.0 - OMEGA
WIDTH = 32
SPAN = 10
ROWS = 112
PLANE = 3 * ROWS
DEEP = 1024
HIDDEN = SPAN * WIDTH
SENT = 72
SENT_OWN = 88
F32 = jnp.float32
BF16 = jnp.bfloat16


def roll(value, shift, axis):
    return pltpu.roll(value, shift, axis)


def lanes(shape=(8, 128)):
    return lax.broadcasted_iota(jnp.int32, shape, len(shape) - 1)


def rows_of(shape=(8, 128)):
    return lax.broadcasted_iota(jnp.int32, shape, len(shape) - 2)


def split(value):
    high = value.astype(BF16)
    return high, (value - high.astype(F32)).astype(BF16)


def exact(left, right):
    return jnp.dot(left, right, precision=lax.Precision.HIGHEST, preferred_element_type=F32)


def once(left, right):
    return jnp.dot(left, right, preferred_element_type=F32)


def tables():
    spread = np.zeros((3, 128, DEEP), np.float32)
    tag = np.full((8, DEEP), -1, np.int32)
    for a in range(3):
        for t in range(3):
            for c in range(3):
                for k in range(3):
                    for y in range(12):
                        column = a * PLANE + t * ROWS + (c * 3 + k) * 12 + y
                        tag[0, column] = y
                        tag[1, column] = t
                        for b in range(3):
                            spread[b, 3 * (9 * a + 3 * b + c) + k, column] = 1.0
    tag[1, 108] = 10
    tag[1, 2 * ROWS + 108] = 12
    tiled = np.zeros((128, DEEP), np.float32)
    for t in range(3):
        for y in range(SPAN):
            for w in range(WIDTH):
                column = t * HIDDEN + y * WIDTH + w
                tiled[w, column] = 1.0
                tag[2, column] = y
                tag[3, column] = t
    lift = np.zeros((3, 216, 128), np.float32)
    height = np.zeros((216, 128), np.int32)
    for a in range(3):
        for c in range(3):
            for k in range(3):
                for y in range(8):
                    row = a * 72 + (c * 3 + k) * 8 + y
                    height[row] = y + 2
                    for b in range(3):
                        lift[b, row, 3 * (9 * a + 3 * b + c) + k] = 1.0
    inner = np.zeros((128, 256), np.float32)
    for t in range(3):
        for k in range(3):
            for y in range(16):
                column = t * 48 + k * 16 + y
                inner[k, column] = 1.0
                tag[4, column] = y
                tag[5, column] = t
    return (jnp.asarray(spread, BF16), jnp.asarray(tag), jnp.asarray(tiled, BF16),
            jnp.asarray(lift, BF16), jnp.asarray(height), jnp.asarray(inner, BF16))


def weights_kernel(first_ref, turned_ref, bias_ref, second_ref, lifted_ref, spread_ref, tag_ref, tiled_ref,
                   lift_ref, height_ref, inner_ref, wide_ref, tall_ref, out_ref, back_ref):
    high, low = split(first_ref[...])
    term = tag_ref[1:2, :]
    bias_high, bias_low = split(bias_ref[...])
    bias = jnp.where(term == 10, bias_high.astype(F32)[:, 0:1], 0.0)
    bias = bias + jnp.where(term == 12, bias_low.astype(F32)[:, 0:1], 0.0)
    parts = []
    for b in range(3):
        chosen = jnp.where(term == 2, once(low, spread_ref[b]), once(high, spread_ref[b]))
        parts.append(chosen)
    for y in range(SPAN):
        total = bias
        for b in range(3):
            total = total + jnp.where(tag_ref[0:1, :] == y + b, parts[b], 0.0)
        wide_ref[y * WIDTH:(y + 1) * WIDTH, :] = total.astype(BF16)
    high, low = split(turned_ref[...])
    term = tag_ref[3:4, :]
    place = tag_ref[2:3, :]
    copies = jnp.where(term == 2, once(low, tiled_ref[...]), once(high, tiled_ref[...])).astype(BF16)
    total = jnp.zeros((216, DEEP), F32)
    for b in range(3):
        here = height_ref[:, 0:1] - b == place
        total = total + jnp.where(here, once(lift_ref[b], copies), 0.0)
    tall_ref[...] = total.astype(BF16)
    high, low = split(second_ref[...])
    copies = jnp.where(term == 2, once(low, tiled_ref[...]), once(high, tiled_ref[...]))
    row = rows_of((16, DEEP))
    for k in range(3):
        out_ref[16 * k:16 * k + 16, :] = jnp.where(row == place, copies[k:k + 1, :], 0.0).astype(BF16)
    high, low = split(lifted_ref[...])
    term = tag_ref[5:6, 0:256]
    copies = jnp.where(term == 2, once(low, inner_ref[...]), once(high, inner_ref[...]))
    for y in range(SPAN):
        back_ref[y * WIDTH:(y + 1) * WIDTH, :] = jnp.where(tag_ref[4:5, 0:256] == y, copies, 0.0).astype(BF16)


def depth_order():
    first = lax.broadcasted_iota(jnp.int32, (128, 128), 0)
    return jnp.where((first % 2) * 64 + first // 2 == lanes((128, 128)), 1.0, 0.0)


def send_rows(get, flat_ref, sent_ref):
    lane = lanes()
    row = rows_of()
    faces = jnp.zeros((8, 128), F32)
    for x in range(8):
        up = get(2, x + 1, 1)
        value = get(0, x + 2, 1) - get(0, x, 1) + get(1, x + 1, 2) - get(1, x + 1, 0)
        value = value + jnp.where(lane == 127, 0.0, roll(up, 127, 1)) - jnp.where(lane == 0, 0.0, roll(up, 1, 1))
        flat_ref[8 * x:8 * x + 8, :] = 0.5 * value
        faces = faces + jnp.where(lane == 8 * x + row, 0.5 * up[:, 0:1], 0.0)
        faces = faces - jnp.where(lane == 64 + 8 * x + row, 0.5 * up[:, 127:128], 0.0)
    sent_ref[0:64, :] = exact(flat_ref[...], depth_order())
    sent_ref[64:72, :] = jnp.where(row == 0, jnp.sum(faces, axis=0, keepdims=True), 0.0)


def own_rows_kernel(field_ref, sent_ref, flat_ref):
    lane = lanes()
    row = rows_of()
    faces = jnp.zeros((8, 128), F32)
    for x in range(8):
        along = field_ref[1, x + 1]
        up = field_ref[2, x + 1]
        value = jnp.where(row == 7, 0.0, roll(along, 7, 0)) - jnp.where(row == 0, 0.0, roll(along, 1, 0))
        value = value + jnp.where(lane == 127, 0.0, roll(up, 127, 1)) - jnp.where(lane == 0, 0.0, roll(up, 1, 1))
        flat_ref[8 * x:8 * x + 8, :] = 0.5 * (value + field_ref[0, x + 2] - field_ref[0, x])
        flat_ref[64 + x:65 + x, :] = 0.5 * along[0:1, :]
        flat_ref[72 + x:73 + x, :] = -0.5 * along[7:8, :]
        faces = faces + jnp.where(lane == 8 * x + row, 0.5 * up[:, 0:1], 0.0)
        faces = faces - jnp.where(lane == 64 + 8 * x + row, 0.5 * up[:, 127:128], 0.0)
    turned = exact(flat_ref[...], depth_order())
    sent_ref[0:64, :] = turned[0:64]
    sent_ref[64:72, :] = jnp.where(row == 0, jnp.sum(faces, axis=0, keepdims=True), 0.0)
    sent_ref[72:88, :] = turned[64:80]


def forward_kernel(ids_ref, bias_ref, ext_ref, col_ref, wide_ref, out_ref, closed_ref, slope_ref, sent_ref,
                   plane_ref, feat_ref, hid_ref, ce_ref, flat_ref):
    gx, gy, gz = ids_ref[0], ids_ref[1], ids_ref[2]
    low_side = jnp.where(gz == 0, 1.0, 0.0)
    high_side = 1.0 - low_side
    lane = lanes((12, 128))
    pad_row = rows_of((8, 128))
    plane_ref[104:112, :] = jnp.where(pad_row == 4, 1.0, 0.0)
    feat_ref[7 * PLANE:7 * PLANE + 16, :] = jnp.zeros((16, 256), BF16)
    hid_ref[3 * HIDDEN:DEEP, :] = jnp.zeros((DEEP - 3 * HIDDEN, 256), BF16)
    corner = rows_of((12, 12)) == lanes((12, 12))
    beyond = [[jnp.sum(jnp.where(corner, col_ref[k, at:at + 1, :], 0.0), axis=1, keepdims=True) for at in range(12)]
              for k in range(3)]
    for step in range(7):
        for half in range(2):
            at = step + 5 * half
            for k in range(3):
                here = ext_ref[k, at]
                below = jnp.where(lane == 0, beyond[k][at] * high_side, roll(here, 1, 1))
                above = jnp.where(lane == 127, beyond[k][at] * low_side, roll(here, 127, 1))
                for c, piece in ((0, below), (1, here), (2, above)):
                    plane_ref[pl.ds((c * 3 + k) * 12, 12), :] = piece
            high, low = split(plane_ref[...])
            col = slice(128 * half, 128 * half + 128)
            feat_ref[step * PLANE:step * PLANE + ROWS, col] = high
            feat_ref[step * PLANE + ROWS:step * PLANE + 2 * ROWS, col] = low
            feat_ref[step * PLANE + 2 * ROWS:step * PLANE + 3 * ROWS, col] = high
    row = rows_of((16, 128))
    inside = jnp.where((row == 0) & (gy == 0), 0.0, 1.0)
    inside = jnp.where((row == 9) & (gy == ids_ref[4] - 1), 0.0, inside)
    inside = jnp.where(row > 9, 0.0, inside)
    for x in range(5):
        pre = once(wide_ref[...], feat_ref[x * PLANE:x * PLANE + DEEP, :])
        sig = 0.5 * jnp.tanh(0.5 * pre) + 0.5
        slope_ref[x] = sig * (1.0 + pre * (1.0 - sig))
        high, low = split(pre * sig)
        hid_ref[0:HIDDEN, :] = high
        hid_ref[HIDDEN:2 * HIDDEN, :] = low
        hid_ref[2 * HIDDEN:3 * HIDDEN, :] = high
        result = once(out_ref[...], hid_ref[...])
        for half in range(2):
            e = x + 5 * half
            mask = inside
            if e == 0:
                mask = inside * jnp.where(gx == 0, 0.0, 1.0)
            if e == 9:
                mask = inside * jnp.where(gx == ids_ref[3] - 1, 0.0, 1.0)
            for k in range(3):
                ce_ref[k, e] = (result[16 * k:16 * k + 16, 128 * half:128 * half + 128] + bias_ref[k]) * mask
                ce_ref[k, e, 0:10, :] = ce_ref[k, e, 0:10, :] + ext_ref[k, e + 1, 1:11, :]
    for k in range(3):
        for x in range(8):
            closed_ref[k, x] = ce_ref[k, x + 1, 1:9, :]
    send_rows(lambda k, x, y: ce_ref[k, x, pl.ds(y, 8), :], flat_ref, sent_ref)


def around(grid, wide, masks):
    (x_low, x_high, y_low, y_high) = masks
    lane = lanes()
    size = len(grid[0])
    result = []
    for c in range(2):
        plane = []
        for x in range(size):
            line = []
            for y in range(size):
                here = grid[c][x][y]
                total = jnp.where(lane >= wide, roll(here, wide, 1), 0.0)
                total = total + jnp.where(lane < 128 - wide, roll(here, 128 - wide, 1), 0.0)
                total = total + (grid[c][x - 1][y] if x > 0 else roll(grid[c][size - 1][y], 2, 0) * x_low)
                total = total + (grid[c][x + 1][y] if x < size - 1 else roll(grid[c][0][y], 6, 0) * x_high)
                if y > 0:
                    total = total + grid[c][x][y - 1]
                else:
                    edge = grid[1 - c][x][size - 1]
                    total = total + (edge if c == 1 else roll(edge, 1, 0) * y_low)
                if y < size - 1:
                    total = total + grid[c][x][y + 1]
                else:
                    edge = grid[1 - c][x][0]
                    total = total + (edge if c == 0 else roll(edge, 7, 0) * y_high)
                line.append(total)
            plane.append(line)
        result.append(plane)
    return result


def over(function, *grids):
    size = len(grids[0][0])
    return [[[function(*(g[c][x][y] for g in grids)) for y in range(size)] for x in range(size)] for c in range(2)]


def flat(grid):
    return tuple(v for plane in grid for line in plane for v in line)


def unflat(values, size):
    values = list(values)
    return [[[values[(c * size + x) * size + y] for y in range(size)] for x in range(size)] for c in range(2)]


def relax_level(guess, source, wide, masks):
    return over(lambda g, s, n: KEEP * g + STEP * (s + n), guess, source, around(guess, wide, masks))


def residue_level(guess, source, wide, masks):
    return over(lambda g, s, n: s - 6.0 * g + n, guess, source, around(guess, wide, masks))


def coarser(grid, wide):
    lane = lanes()
    size = len(grid[0]) // 2
    even = (lane // wide) % 2 == 0
    result = []
    for c in range(2):
        plane = []
        for x in range(size):
            line = []
            for y in range(size):
                t = grid[c][2 * x][2 * y] + grid[c][2 * x][2 * y + 1]
                t = t + grid[c][2 * x + 1][2 * y] + grid[c][2 * x + 1][2 * y + 1]
                line.append(0.5 * (t + jnp.where(even, roll(t, 128 - wide, 1), roll(t, wide, 1))))
            plane.append(line)
        result.append(plane)
    return result


def add_coarse(grid, coarse):
    size = len(grid[0])
    return [[[grid[c][x][y] + coarse[c][x // 2][y // 2] for y in range(size)] for x in range(size)] for c in range(2)]


def level_solve(source, level, sweeps_ref, masks):
    wide = 1 << (level - 1)
    size = len(source[0])
    guess = over(lambda s: STEP * s, source)
    if level == LEVELS:
        for _ in range(COARSE_SWEEPS - 1):
            guess = relax_level(guess, source, wide, masks)
        return guess
    repeats = sweeps_ref[level]

    def body(number, state):
        return flat(relax_level(unflat(state, size), source, wide, masks))

    guess = unflat(lax.fori_loop(1, repeats, body, flat(guess)), size)
    coarse = coarser(residue_level(guess, source, wide, masks), wide)
    guess = add_coarse(guess, level_solve(coarse, level + 1, sweeps_ref, masks))
    return unflat(lax.fori_loop(0, repeats, body, flat(guess)), size)


def project_kernel(ext, ids_ref, sweeps_ref, mine_ref, other_ref, field_ref, *refs):
    if ext:
        result_ref, s_ref, x_ref, p_ref, wrap_ref, edge_ref, win_ref, nat_ref = refs
    else:
        part_ref, over_ref, result_ref, grad_ref, s_ref, x_ref, p_ref, wrap_ref, edge_ref, win_ref, nat_ref = refs
        join(ids_ref, part_ref, over_ref, grad_ref)
    sent = SENT_OWN if ext else SENT
    gx, gy, gz = ids_ref[0], ids_ref[1], ids_ref[2]
    core = lax.rem(gy, 2)
    lane = lanes()
    sub = rows_of()
    x_low = jnp.where(sub >= 2, 1.0, 0.0)
    x_high = jnp.where(sub < 6, 1.0, 0.0)
    y_low = jnp.where(sub % 2 == 1, 1.0, 0.0)
    y_high = jnp.where(sub % 2 == 0, 1.0, 0.0)
    masks = (x_low, x_high, y_low, y_high)
    z_low = jnp.where(lane != 0, 1.0, 0.0)
    z_high = jnp.where(lane != 127, 1.0, 0.0)
    lower = lane < 64

    def halves(source_ref, i):
        first = source_ref[pl.ds(i, 8, stride=2 * sent), :]
        second = source_ref[pl.ds(sent + i, 8, stride=2 * sent), :]
        return jnp.where(lower, first, roll(second, 64, 1)), jnp.where(lower, roll(first, 64, 1), second)

    for source_ref, slot in ((mine_ref, core), (other_ref, 1 - core)):
        face0 = source_ref[pl.ds(64, 8, stride=2 * sent), :]
        face1 = source_ref[pl.ds(sent + 64, 8, stride=2 * sent), :]
        for x in range(8):
            for y in range(8):
                i = 8 * x + y
                even, odd = halves(source_ref, i)
                even = even + jnp.where(lane == 64, roll(face0, (128 - i) % 128, 1), 0.0)
                odd = odd + jnp.where(lane == 63, roll(face1, (63 - i) % 128, 1), 0.0)
                for zi, value in ((0, even), (1, odd)):
                    s_ref[slot, zi, x, y] = value
                    x_ref[slot, zi, x, y] = STEP * value

    def also(slot, zi, x, y, value):
        s_ref[slot, zi, x, y] = s_ref[slot, zi, x, y] + value
        x_ref[slot, zi, x, y] = x_ref[slot, zi, x, y] + STEP * value

    if ext:
        for source_ref, slot in ((mine_ref, core), (other_ref, 1 - core)):
            for at in range(8):
                for zi, value in enumerate(halves(source_ref, 72 + at)):
                    also(1 - slot, zi, at, 7, jnp.where(slot == 1, value, roll(value, 7, 0) * y_high))
                for zi, value in enumerate(halves(source_ref, 80 + at)):
                    also(1 - slot, zi, at, 0, jnp.where(slot == 0, value, roll(value, 1, 0) * y_low))

    every = [(zi, y) for zi in range(2) for y in range(8)]

    def visit(use):
        for c in range(2):
            first = {at: x_ref[c, at[0], 0, at[1]] for at in every}
            before = {at: roll(x_ref[c, at[0], 7, at[1]], 2, 0) * x_low for at in every}
            for at in every:
                wrap_ref[at[0], at[1]] = roll(first[at], 6, 0) * x_high
            own = first
            for x in range(8):
                after = {at: x_ref[c, at[0], x + 1, at[1]] if x < 7 else wrap_ref[at[0], at[1]] for at in every}
                for zi in range(2):
                    if c == 0:
                        down = roll(x_ref[1, zi, x, 7], 1, 0) * y_low
                        up = x_ref[1, zi, x, 0]
                        edge_ref[zi, x, 0] = own[zi, 7]
                        edge_ref[zi, x, 1] = roll(own[zi, 0], 7, 0) * y_high
                    else:
                        down = edge_ref[zi, x, 0]
                        up = edge_ref[zi, x, 1]
                    for y in range(8):
                        beside = own[1 - zi, y]
                        total = before[zi, y] + after[zi, y] + beside
                        total = total + (own[zi, y - 1] if y > 0 else down) + (own[zi, y + 1] if y < 7 else up)
                        if zi == 0:
                            total = total + roll(beside, 1, 1) * z_low
                        else:
                            total = total + roll(beside, 127, 1) * z_high
                        value = use(c, zi, x, y, own[zi, y], total)
                        if value is not None:
                            x_ref[c, zi, x, y] = value
                before, own = own, after

    def sweep(number, carry):
        visit(lambda c, zi, x, y, own, total: KEEP * own + STEP * (s_ref[c, zi, x, y] + total))
        return carry

    repeats = sweeps_ref[0]

    def cycle(number, carry):
        lax.fori_loop(1, repeats, sweep, 0)
        sums = {}

        def gather(c, zi, x, y, own, total):
            e = s_ref[c, zi, x, y] - 6.0 * own + total
            at = (c, x // 2, y // 2)
            sums[at] = sums[at] + e if at in sums else e

        visit(gather)
        coarse = [[[0.5 * sums[c, x, y] for y in range(4)] for x in range(4)] for c in range(2)]
        coarse = level_solve(coarse, 1, sweeps_ref, masks)
        for c in range(2):
            for zi in range(2):
                for x in range(8):
                    for y in range(8):
                        x_ref[c, zi, x, y] = x_ref[c, zi, x, y] + coarse[c][x // 2][y // 2]
        lax.fori_loop(0, repeats, sweep, 0)

        @pl.when(number == 0)
        def _():
            def restart(c, zi, x, y, own, total):
                p_ref[c, zi, x, y] = own
                rest = s_ref[c, zi, x, y] - 6.0 * own + total
                s_ref[c, zi, x, y] = rest
                return STEP * rest

            visit(restart)

        return carry

    lax.fori_loop(0, CYCLES, cycle, 0)

    x_rows = x_ref.reshape(2 * 2 * 8 * 8 * 8, 128)
    p_rows = p_ref.reshape(2 * 2 * 8 * 8 * 8, 128)
    last_x, last_y = ids_ref[3] - 1, ids_ref[4] - 1
    for wx in range(12):
        dx = -1 if wx < 2 else (1 if wx > 9 else 0)
        xi = (wx - 2) % 8
        bx = gx + dx
        for dy in (-1, 0, 1):
            by = gy + dy
            ok = (bx >= 0) & (bx <= last_x) & (by >= 0) & (by <= last_y)
            ax = jnp.clip(bx, 0, last_x)
            ay = jnp.clip(by, 0, last_y)
            at = ax * 2 + ay // 2
            c = lax.rem(ay, 2)
            for zi in range(2):
                start = ((c * 2 + zi) * 8 + xi) * 64 + at
                first = x_rows[pl.ds(start, 8, stride=8), :]
                second = p_rows[pl.ds(start, 8, stride=8), :]
                win_ref[wx * 24 + 8 * (dy + 1):wx * 24 + 8 * (dy + 1) + 8, 128 * zi:128 * zi + 128] = jnp.where(
                    ok, first + second, 0.0)
    source = lax.broadcasted_iota(jnp.int32, (256, 256), 0)
    target = lanes((256, 256))
    depth = 2 * (source % 128) + source // 128
    wanted = jnp.where(target == 255, -1, target) + gz * 128
    pick = jnp.where((depth == wanted) & ((target <= 128) | (target == 255)), 1.0, 0.0)
    nat_ref[...] = exact(win_ref[...], pick)

    size = 16 if ext else 8
    count = 10 if ext else 8
    lane = lanes((count, 128))
    row = rows_of((count, 128))
    for i in range(count):
        x = i - 1 if ext else i
        top = 7 if ext else 8
        base = (x + 2) * 24 + top
        mid = nat_ref[pl.ds(base, count), 0:128]
        tail = nat_ref[pl.ds(base, count), 128:256]
        sx = nat_ref[pl.ds(base + 24, count), 0:128] - nat_ref[pl.ds(base - 24, count), 0:128]
        sy = nat_ref[pl.ds(base + 1, count), 0:128] - nat_ref[pl.ds(base - 1, count), 0:128]
        sz = roll(jnp.where(lane == 0, tail, mid), 127, 1) - roll(jnp.where(lane == 127, tail, mid), 1, 1)
        for k, s in enumerate((sx, sy, sz)):
            if ext:
                value = field_ref[k, i] + 0.5 * s
                good = jnp.where((row == 0) & (gy == 0), 0.0, 1.0)
                good = jnp.where((row == 9) & (gy == last_y), 0.0, good)
                if i == 0:
                    good = good * jnp.where(gx == 0, 0.0, 1.0)
                if i == 9:
                    good = good * jnp.where(gx == last_x, 0.0, 1.0)
                result_ref[k, i] = jnp.zeros((16, 128), F32)
                result_ref[k, i, 0:10, :] = value * good
            else:
                result_ref[k, i] = field_ref[k, i] + 0.5 * s


def backward_kernel(ids_ref, adj_ref, slope_ref, tall_ref, back_ref, grad_ref, over_ref, in_ref, bb_ref, acc_ref):
    gz = ids_ref[2]
    in_ref[144:256, :] = jnp.zeros((112, 256), BF16)
    bb_ref[3 * HIDDEN:DEEP, :] = jnp.zeros((DEEP - 3 * HIDDEN, 256), BF16)
    acc_ref[...] = jnp.zeros(acc_ref.shape, F32)
    for x in range(5):
        for half in range(2):
            col = slice(128 * half, 128 * half + 128)
            for k in range(3):
                high, low = split(adj_ref[k, x + 5 * half])
                in_ref[16 * k:16 * k + 16, col] = high
                in_ref[48 + 16 * k:64 + 16 * k, col] = low
                in_ref[96 + 16 * k:112 + 16 * k, col] = high
        high, low = split(once(back_ref[...], in_ref[...]) * slope_ref[x])
        bb_ref[0:HIDDEN, :] = high
        bb_ref[HIDDEN:2 * HIDDEN, :] = low
        bb_ref[2 * HIDDEN:3 * HIDDEN, :] = high
        total = once(tall_ref[...], bb_ref[...])
        for half in range(2):
            for a in range(3):
                at = x + 5 * half + a
                acc_ref[at] = acc_ref[at] + total[72 * a:72 * a + 72, 128 * half:128 * half + 128]
    lane = lanes()
    row = rows_of()
    for k in range(3):
        packed = jnp.zeros((8, 128), F32)
        for x in range(8):
            low = acc_ref[x + 2, 8 * k:8 * k + 8, :]
            mid = acc_ref[x + 2, 24 + 8 * k:32 + 8 * k, :]
            high = acc_ref[x + 2, 48 + 8 * k:56 + 8 * k, :]
            value = adj_ref[k, x + 1, 1:9, :] + mid
            value = value + jnp.where(lane == 127, 0.0, roll(low, 127, 1))
            grad_ref[k, x] = value + jnp.where(lane == 0, 0.0, roll(high, 1, 1))
            out = jnp.where(gz == 0, high[:, 127:128], low[:, 0:1])
            packed = packed + jnp.where(lane == 8 * x + row, out, 0.0)
        over_ref[k:k + 1, :] = jnp.sum(packed, axis=0, keepdims=True)
    over_ref[3:8, :] = jnp.zeros((5, 128), F32)


def join(ids_ref, part_ref, over_ref, grad_ref):
    gz = ids_ref[2]
    lane = lanes()
    row = rows_of()
    edge = jnp.where(gz == 0, 127, 0)
    for k in range(3):
        for x in range(8):
            column = jnp.sum(jnp.where(lane == 8 * x + row, over_ref[k:k + 1, :], 0.0), axis=1, keepdims=True)
            grad_ref[k, x] = part_ref[k, x] + jnp.where(lane == edge, column, 0.0)


VMEM = pl.BlockSpec(memory_space=pltpu.VMEM)
SMEM = pl.BlockSpec(memory_space=pltpu.SMEM)


def call(kernel, specs, shapes, scratch, *operands, flops=0, size=1 << 20):
    return pl.pallas_call(
        kernel,
        in_specs=specs,
        out_specs=[VMEM] * len(shapes),
        out_shape=[jax.ShapeDtypeStruct(s, t) for s, t in shapes],
        scratch_shapes=scratch,
        compiler_params=pltpu.CompilerParams(vmem_limit_bytes=12 * 2**20),
        cost_estimate=pl.CostEstimate(flops=flops, bytes_accessed=size, transcendentals=0),
    )(*operands)


def trade(velocity, cotangent, axis, dim):
    count = lax.axis_size(axis)
    odd = lax.rem(lax.axis_index(axis), 2) == 1
    size = velocity.shape[dim]

    def cut(array, start, stop):
        return lax.slice_in_dim(array, start, stop, axis=dim)

    other = 3 - dim
    grow = [(0, 0)] * 4
    grow[other] = (0, velocity.shape[other] - cotangent.shape[other])
    low = jnp.concatenate([cut(velocity, 0, 2), jnp.pad(cut(cotangent, 0, 1), grow)], axis=dim)
    high = jnp.concatenate([cut(velocity, size - 2, size), jnp.pad(cut(cotangent, size - 1, size), grow)], axis=dim)
    pairs = [(i, i ^ 1) for i in range(count)]
    gaps = [(i, i + 1) for i in range(1, count - 1, 2)]
    gaps = gaps + [(j, i) for i, j in gaps]
    second = lax.ppermute(jnp.where(odd, high, low), axis, gaps)
    first = lax.ppermute(jnp.where(odd, low, high), axis, pairs)
    below, above = jnp.where(odd, first, second), jnp.where(odd, second, first)
    wide = jnp.concatenate([cut(below, 0, 2), velocity, cut(above, 0, 2)], axis=dim)
    kept = cotangent.shape[other]
    narrow = jnp.concatenate([lax.slice_in_dim(cut(below, 2, 3), 0, kept, axis=other), cotangent,
                              lax.slice_in_dim(cut(above, 2, 3), 0, kept, axis=other)], axis=dim)
    return wide, narrow


def gather_own(rows):
    nx, ny, nz = (lax.axis_size(a) for a in AXES)
    groups = [[(x * ny + 2 * y + c) * nz + z for x in range(nx) for y in range(ny // 2) for z in range(nz)]
              for c in range(2)]
    count = len(groups[0])
    spread = jnp.broadcast_to(rows[None], (count,) + rows.shape)
    mine = lax.all_to_all(spread, AXES, 0, 0, axis_index_groups=groups)
    return mine.reshape(count * rows.shape[0], rows.shape[1])


def twin(mine):
    return lax.ppermute(mine, "gy", [(i, i ^ 1) for i in range(lax.axis_size("gy"))])


def project_rows(ids, sweeps, mine, other, field, *more):
    ext = len(more) == 0
    block = ((3, 8, 8, 128), F32)
    scratch = [
        pltpu.VMEM((2, 2, 8, 8, 8, 128), F32),
        pltpu.VMEM((2, 2, 8, 8, 8, 128), F32),
        pltpu.VMEM((2, 2, 8, 8, 8, 128), F32),
        pltpu.VMEM((2, 8, 8, 128), F32),
        pltpu.VMEM((2, 8, 2, 8, 128), F32),
        pltpu.VMEM((288, 256), F32),
        pltpu.VMEM((288, 256), F32),
    ]
    return call(functools.partial(project_kernel, ext), [SMEM, SMEM] + [VMEM] * (3 + len(more)),
                [((3, 10, 16, 128), F32)] if ext else [block, block], scratch,
                ids, sweeps, mine, other, field, *more, flops=10**10)


def gathered(velocity, cotangent, first_weight, first_bias, second_weight, second_bias, sweeps):
    swap = [(0, 1), (1, 0)]
    ids = jnp.stack([lax.axis_index("gx"), lax.axis_index("gy"), lax.axis_index("gz"),
                     jnp.int32(lax.axis_size("gx")), jnp.int32(lax.axis_size("gy"))]).astype(jnp.int32)
    near, cot_near = trade(velocity, cotangent, "gx", 1)
    cot_rows = call(own_rows_kernel, [VMEM], [((SENT_OWN, 128), F32)], [pltpu.VMEM((80, 128), F32)], cot_near)[0]
    cot_mine = gather_own(cot_rows)
    near, cot_near = trade(near, cot_near, "gy", 2)
    face = jnp.where(ids[2] == 0, near[:, :, :, 127], near[:, :, :, 0])
    face = lax.ppermute(face, "gz", swap)
    features = first_weight.shape[1]
    padded = jnp.pad(first_weight, ((0, 0), (0, 128 - features)))
    turned = jnp.pad(first_weight.T, ((0, 128 - features), (0, 128 - WIDTH)))
    second = jnp.pad(second_weight, ((0, 5), (0, 128 - WIDTH)))
    lifted = jnp.pad(second_weight.T, ((0, 0), (0, 125)))
    bias = jnp.broadcast_to(first_bias[:, None], (WIDTH, 128))
    wide, tall, out, back = call(
        weights_kernel, [VMEM] * 11,
        [((HIDDEN, DEEP), BF16), ((216, DEEP), BF16), ((48, DEEP), BF16), ((HIDDEN, 256), BF16)], [],
        padded, turned, bias, second, lifted, *tables(), flops=10**9)
    closed, slope, rows = call(
        forward_kernel, [SMEM, SMEM] + [VMEM] * 4,
        [((3, 8, 8, 128), F32), ((5, HIDDEN, 256), F32), ((SENT, 128), F32)],
        [pltpu.VMEM((ROWS, 128), F32), pltpu.VMEM((7 * PLANE + 16, 256), BF16), pltpu.VMEM((DEEP, 256), BF16),
         pltpu.VMEM((3, 10, 16, 128), F32), pltpu.VMEM((64, 128), F32)],
        ids, second_bias, near, face, wide, out, flops=4 * 10**9)
    cot_mine, rows = lax.optimization_barrier((cot_mine, rows))
    cot_other = twin(cot_mine)
    mine = gather_own(rows)
    adjoint = project_rows(ids, sweeps, cot_mine, cot_other, cot_near)[0]
    part, over_rows = call(
        backward_kernel, [SMEM] + [VMEM] * 4, [((3, 8, 8, 128), F32), ((8, 128), F32)],
        [pltpu.VMEM((256, 256), BF16), pltpu.VMEM((DEEP, 256), BF16), pltpu.VMEM((12, 72, 128), F32)],
        ids, adjoint, slope, tall, back, flops=3 * 10**9)
    over_rows = lax.ppermute(over_rows, "gz", swap)
    mine, part, over_rows = lax.optimization_barrier((mine, part, over_rows))
    updated, grad = project_rows(ids, sweeps, mine, twin(mine), closed, part, over_rows)
    return updated, grad


def one_gather(velocity, first_weight):
    nx, ny, nz = (lax.axis_size(a) for a in AXES)
    return (velocity.shape == (3, 8, 8, 128) and nx == 4 and ny == 4 and nz == 2
            and first_weight.shape == (WIDTH, 81))


def dispatch(velocity, cotangent, first_weight, first_bias, second_weight, second_bias, sweeps):
    path = gathered if one_gather(velocity, first_weight) else shards
    return path(velocity, cotangent, first_weight, first_bias, second_weight, second_bias, sweeps)


def solution(mesh):
    return jax.shard_map(
        dispatch,
        mesh=mesh,
        in_specs=(P(None, "gx", "gy", "gz"), P(None, "gx", "gy", "gz"), P(), P(), P(), P(), P()),
        out_specs=(P(None, "gx", "gy", "gz"), P(None, "gx", "gy", "gz")),
        check_vma=False,
    )
```

```python
import functools

import jax
import jax.numpy as jnp
from jax import lax
from jax.experimental import pallas as pl
from jax.experimental.pallas import tpu as pltpu
from jax.sharding import PartitionSpec as P

LEVELS = 3
COARSE_SWEEPS = 6
CYCLES = 2


OMEGA = 0.8


def with_halo(block, sides, width):
    for axis, dim in sides:
        count = lax.axis_size(axis)
        forward = [(i, i + 1) for i in range(count - 1)]
        backward = [(target, source) for source, target in forward]
        low = lax.ppermute(
            lax.slice_in_dim(block, block.shape[dim] - width, None, axis=dim), axis, forward
        )
        high = lax.ppermute(lax.slice_in_dim(block, 0, width, axis=dim), axis, backward)
        block = jnp.concatenate([low, block, high], axis=dim)
    return block


def stencil_features(region):
    span_y = region.shape[2] - 2
    span_z = region.shape[3] - 2
    shifted = [
        region[:, first, second : second + span_y, third : third + span_z]
        for first in range(3)
        for second in range(3)
        for third in range(3)
    ]
    return jnp.stack(shifted).reshape(27 * region.shape[0], span_y * span_z)


def six_point(field, padded):
    beside = padded[:, 2:, 1:-1, 1:-1] + padded[:, :-2, 1:-1, 1:-1]
    beside = beside + padded[:, 1:-1, 2:, 1:-1] + padded[:, 1:-1, :-2, 1:-1]
    beside = beside + padded[:, 1:-1, 1:-1, 2:] + padded[:, 1:-1, 1:-1, :-2]
    return 6.0 * field - beside


def near_faces(field):
    return with_halo(field, (("gx", 1), ("gy", 2), ("gz", 3)), 1)


def laplace_shared(field):
    return six_point(field, near_faces(field))


def relax(guess, source):
    return guess + OMEGA * (source - laplace_shared(guess)) / 6.0


def restrict(residue):
    batch, size_x, size_y, size_z = residue.shape
    folded = residue.reshape(batch, size_x // 2, 2, size_y // 2, 2, size_z // 2, 2)
    return 0.5 * folded.sum(axis=(2, 4, 6))


def prolong(coarse):
    return jnp.repeat(jnp.repeat(jnp.repeat(coarse, 2, axis=1), 2, axis=2), 2, axis=3)


def coarse_spread(source, sweeps):
    guess = OMEGA * source / 6.0
    return lax.fori_loop(1, COARSE_SWEEPS, lambda number, state: relax(state, source), guess)


def vcycle(source, sweeps, level, coarse_solve, bottom):
    if level == bottom:
        return coarse_solve(source, sweeps)
    repeats = sweeps[level]
    guess = OMEGA * source / 6.0
    guess = lax.fori_loop(1, repeats, lambda number, state: relax(state, source), guess)
    residue = source - laplace_shared(guess)
    guess = guess + prolong(vcycle(restrict(residue), sweeps, level + 1, coarse_solve, bottom))
    return lax.fori_loop(0, repeats, lambda number, state: relax(state, source), guess)


def divergence(padded):
    total = padded[:, 0, 2:, 1:-1, 1:-1] - padded[:, 0, :-2, 1:-1, 1:-1]
    total = total + padded[:, 1, 1:-1, 2:, 1:-1] - padded[:, 1, 1:-1, :-2, 1:-1]
    total = total + padded[:, 2, 1:-1, 1:-1, 2:] - padded[:, 2, 1:-1, 1:-1, :-2]
    return 0.5 * total


def gradient(padded):
    return 0.5 * jnp.stack(
        [
            padded[:, 2:, 1:-1, 1:-1] - padded[:, :-2, 1:-1, 1:-1],
            padded[:, 1:-1, 2:, 1:-1] - padded[:, 1:-1, :-2, 1:-1],
            padded[:, 1:-1, 1:-1, 2:] - padded[:, 1:-1, 1:-1, :-2],
        ],
        axis=1,
    )


def project(fields, sweeps, coarse_solve, bottom):
    batch, comps, size_x, size_y, size_z = fields.shape
    padded = near_faces(fields.reshape(batch * comps, size_x, size_y, size_z))
    padded = padded.reshape(batch, comps, size_x + 2, size_y + 2, size_z + 2)
    source = divergence(padded)
    pressure = vcycle(source, sweeps, 0, coarse_solve, bottom)
    pressure = pressure + vcycle(source - laplace_shared(pressure), sweeps, 0, coarse_solve, bottom)
    return fields + gradient(near_faces(pressure))


def corrections(near, first_weight, first_bias, second_weight, second_bias, planes):
    span_y = near.shape[2] - 2
    span_z = near.shape[3] - 2

    def corrections_one_plane(index):
        region = lax.dynamic_slice_in_dim(near, index, 3, 1)
        feats = stencil_features(region)
        hidden = jax.nn.silu(
            jnp.dot(first_weight, feats, precision=lax.Precision.HIGHEST) + first_bias[:, None]
        )
        return (
            jnp.dot(second_weight, hidden, precision=lax.Precision.HIGHEST) + second_bias[:, None]
        )

    result = lax.map(corrections_one_plane, jnp.arange(planes, dtype=jnp.int32))
    return result.reshape(planes, 3, span_y, span_z).transpose(1, 0, 2, 3)


def back_planes(wide, cot_pad, first_weight, first_bias, second_weight, planes):
    span_y = cot_pad.shape[2] - 2
    span_z = cot_pad.shape[3] - 2

    def back_one_plane(index):
        region = lax.dynamic_slice_in_dim(wide, index, 3, 1)
        feats = stencil_features(region)
        pre = jnp.dot(first_weight, feats, precision=lax.Precision.HIGHEST) + first_bias[:, None]
        sig = jax.nn.sigmoid(pre)
        slope = sig * (1.0 + pre * (1.0 - sig))
        incoming = lax.dynamic_index_in_dim(cot_pad, index, 1, keepdims=False).reshape(3, -1)
        back = jnp.dot(second_weight.T, incoming, precision=lax.Precision.HIGHEST) * slope
        spread = jnp.dot(first_weight.T, back, precision=lax.Precision.HIGHEST)
        spread = spread.reshape(3, 3, 3, 3, span_y + 2, span_z + 2)
        parts = []
        for first in range(3):
            total = jnp.zeros((3, span_y, span_z), jnp.float32)
            for second in range(3):
                for third in range(3):
                    total = (
                        total
                        + spread[
                            first,
                            second,
                            third,
                            :,
                            2 - second : 2 - second + span_y,
                            2 - third : 2 - third + span_z,
                        ]
                    )
            parts.append(total)
        return jnp.stack(parts)

    pieces = lax.map(back_one_plane, jnp.arange(planes + 2, dtype=jnp.int32))
    return pieces[:-2, 2] + pieces[1:-1, 1] + pieces[2:, 0]


def shards(velocity, cotangent, first_weight, first_bias, second_weight, second_bias, sweeps):
    planes = velocity.shape[1]
    near = with_halo(velocity, (("gx", 1), ("gy", 2), ("gz", 3)), 1)
    coarse_solve, bottom = (coarse_spread, LEVELS)
    closed = velocity + corrections(
        near, first_weight, first_bias, second_weight, second_bias, planes
    )
    updated = project(closed[None], sweeps, coarse_solve, bottom)[0]
    adjoint_closed = project(cotangent[None], sweeps, coarse_solve, bottom)[0]
    wide = with_halo(velocity, (("gx", 1), ("gy", 2), ("gz", 3)), 2)
    cot_pad = with_halo(adjoint_closed, (("gx", 1), ("gy", 2), ("gz", 3)), 1)
    summed = back_planes(wide, cot_pad, first_weight, first_bias, second_weight, planes)
    grad_velocity = adjoint_closed + summed.transpose(1, 0, 2, 3)
    return (updated, grad_velocity)


AXES = ("gx", "gy", "gz")
STEP = OMEGA / 6.0
KEEP = 1.0 - OMEGA
WIDTH = 32
SPAN = 10
ROWS = 112
PLANE = 2 * ROWS
REACH = 768
DEEP = 1024
HIDDEN = SPAN * WIDTH
SENT = 72
SENT_OWN = 88
F32 = jnp.float32
BF16 = jnp.bfloat16


def roll(value, shift, axis):
    return pltpu.roll(value, shift, axis)


def lanes(shape=(8, 128)):
    return lax.broadcasted_iota(jnp.int32, shape, len(shape) - 1)


def rows_of(shape=(8, 128)):
    return lax.broadcasted_iota(jnp.int32, shape, len(shape) - 2)


def split(value):
    high = value.astype(BF16)
    return high, (value - high.astype(F32)).astype(BF16)


def exact(left, right):
    return jnp.dot(left, right, precision=lax.Precision.HIGHEST, preferred_element_type=F32)


def once(left, right):
    return jnp.dot(left, right, preferred_element_type=F32)


def one_hot(condition):
    return jnp.where(condition, 1.0, 0.0).astype(BF16)


def column_of(line, size):
    square = (size, size)
    return jnp.sum(jnp.where(rows_of(square) == lanes(square), line, 0.0), axis=1, keepdims=True)


def weights_kernel(first_ref, bias_ref, second_ref, wide_ref, tall_ref, out_ref, back_ref, pad_ref):
    count = first_ref.shape[1]
    pad_ref[...] = jnp.zeros((256, 128), F32)
    pad_ref[0:WIDTH, 0:count] = first_ref[...]
    pad_ref[128:131, 0:WIDTH] = second_ref[...]
    first = pad_ref[0:128, :]
    second = pad_ref[128:256, :]
    high, low = split(first[0:WIDTH])
    column = lanes((1, REACH))
    rest = column % ROWS
    real = (rest < 108) & (column < 3 * PLANE)
    height = jnp.where(real, rest % 12, -1)
    feature = jnp.where(real, 27 * (column // PLANE) + rest // 12, -1000)
    upper = (column % PLANE) < ROWS
    bias_high, bias_low = split(column_of(bias_ref[...], WIDTH))
    totals = [jnp.where(column == 108, part.astype(F32), 0.0) for part in (bias_high, bias_low)]
    row = rows_of((128, REACH))
    parts = []
    for b in range(3):
        chosen = one_hot(row - 9 * b == feature)
        parts.append((once(high, chosen), jnp.where(upper, once(low, chosen), 0.0)))
    for y in range(SPAN):
        for half in range(2):
            total = totals[half]
            for b in range(3):
                total = total + jnp.where(height == y + b, parts[b][half], 0.0)
            wide_ref[half * HIDDEN + y * WIDTH:half * HIDDEN + (y + 1) * WIDTH, :] = total.astype(BF16)
    high, low = split(first.T)
    column = lanes((1, DEEP))
    row = rows_of((128, DEEP))
    place = (column % HIDDEN) // WIDTH
    term = column // HIDDEN
    tiled = one_hot((row == column % WIDTH) & (column < 3 * HIDDEN))
    copies = jnp.where(term == 2, once(low, tiled), once(high, tiled)).astype(BF16)
    line = lax.broadcasted_iota(jnp.int32, (216, 128), 0)
    lane = lanes((216, 128))
    tops = line[:, 0:1] % 8 + 2
    total = jnp.zeros((216, DEEP), F32)
    for b in range(3):
        lift = one_hot(lane - 9 * b == 27 * (line // 72) + (line % 72) // 8)
        total = total + jnp.where(tops - b == place, once(lift, copies), 0.0)
    tall_ref[...] = total.astype(BF16)
    for k in range(3):
        line = second[k:k + 1, 0:WIDTH]
        out_ref[WIDTH * k:WIDTH * (k + 1), :] = jnp.broadcast_to(column_of(line, WIDTH), (WIDTH, 128))
    high, low = split(second.T[0:WIDTH])
    column = lanes((1, 256))
    row = rows_of((128, 256))
    inner = one_hot((row == (column % 48) // 16) & (column < 144))
    copies = jnp.where(column // 48 == 2, once(low, inner), once(high, inner))
    for y in range(SPAN):
        back_ref[y * WIDTH:(y + 1) * WIDTH, :] = jnp.where(column % 16 == y, copies, 0.0).astype(BF16)


def depth_order():
    first = lax.broadcasted_iota(jnp.int32, (128, 128), 0)
    return jnp.where((first % 2) * 64 + first // 2 == lanes((128, 128)), 1.0, 0.0)


def send_rows(get, flat_ref, sent_ref):
    lane = lanes()
    row = rows_of()
    faces = jnp.zeros((8, 128), F32)
    for x in range(8):
        up = get(2, x + 1, 1)
        value = get(0, x + 2, 1) - get(0, x, 1) + get(1, x + 1, 2) - get(1, x + 1, 0)
        value = value + jnp.where(lane == 127, 0.0, roll(up, 127, 1)) - jnp.where(lane == 0, 0.0, roll(up, 1, 1))
        flat_ref[8 * x:8 * x + 8, :] = 0.5 * value
        faces = faces + jnp.where(lane == 8 * x + row, 0.5 * up[:, 0:1], 0.0)
        faces = faces - jnp.where(lane == 64 + 8 * x + row, 0.5 * up[:, 127:128], 0.0)
    sent_ref[0:64, :] = exact(flat_ref[...], depth_order())
    sent_ref[64:72, :] = jnp.where(row == 0, jnp.sum(faces, axis=0, keepdims=True), 0.0)


def own_rows_kernel(field_ref, sent_ref, flat_ref):
    lane = lanes()
    row = rows_of()
    faces = jnp.zeros((8, 128), F32)
    for x in range(8):
        along = field_ref[1, x + 1]
        up = field_ref[2, x + 1]
        value = jnp.where(row == 7, 0.0, roll(along, 7, 0)) - jnp.where(row == 0, 0.0, roll(along, 1, 0))
        value = value + jnp.where(lane == 127, 0.0, roll(up, 127, 1)) - jnp.where(lane == 0, 0.0, roll(up, 1, 1))
        flat_ref[8 * x:8 * x + 8, :] = 0.5 * (value + field_ref[0, x + 2] - field_ref[0, x])
        flat_ref[64 + x:65 + x, :] = 0.5 * along[0:1, :]
        flat_ref[72 + x:73 + x, :] = -0.5 * along[7:8, :]
        faces = faces + jnp.where(lane == 8 * x + row, 0.5 * up[:, 0:1], 0.0)
        faces = faces - jnp.where(lane == 64 + 8 * x + row, 0.5 * up[:, 127:128], 0.0)
    turned = exact(flat_ref[...], depth_order())
    sent_ref[0:64, :] = turned[0:64]
    sent_ref[64:72, :] = jnp.where(row == 0, jnp.sum(faces, axis=0, keepdims=True), 0.0)
    sent_ref[72:88, :] = turned[64:80]


def fold(values):
    row = rows_of()
    low = row < 4
    values = [jnp.where(low, a, b) + roll(jnp.where(low, b, a), 4, 0) for a, b in zip(values[:4], values[4:])]
    for step in (2, 1):
        low = (row // step) % 2 == 0
        values = [jnp.where(low, a + roll(a, 8 - step, 0), b + roll(b, step, 0))
                  for a, b in zip(values[:step], values[step:])]
    return values[0]


def forward_kernel(ids_ref, bias_ref, ext_ref, col_ref, wide_ref, out_ref, closed_ref, slope_ref, sent_ref,
                   plane_ref, feat_ref, hid_ref, ce_ref, flat_ref, kept_ref, sems):
    gx, gy, gz = ids_ref[0], ids_ref[1], ids_ref[2]
    low_side = jnp.where(gz == 0, 1.0, 0.0)
    high_side = 1.0 - low_side
    lane = lanes((12, 128))
    pad_row = rows_of((8, 128))
    plane_ref[104:112, :] = jnp.where(pad_row == 4, 1.0, 0.0)
    feat_ref[7 * PLANE:, :] = jnp.zeros((REACH - 3 * PLANE, 256), BF16)
    corner = rows_of((12, 12)) == lanes((12, 12))
    beyond = [[jnp.sum(jnp.where(corner, col_ref[k, at:at + 1, :], 0.0), axis=1, keepdims=True) for at in range(12)]
              for k in range(3)]
    for step in range(7):
        for half in range(2):
            at = step + 5 * half
            for k in range(3):
                here = ext_ref[k, at]
                below = jnp.where(lane == 0, beyond[k][at] * high_side, roll(here, 1, 1))
                above = jnp.where(lane == 127, beyond[k][at] * low_side, roll(here, 127, 1))
                for c, piece in ((0, below), (1, here), (2, above)):
                    plane_ref[pl.ds((c * 3 + k) * 12, 12), :] = piece
            high, low = split(plane_ref[...])
            col = slice(128 * half, 128 * half + 128)
            feat_ref[step * PLANE:step * PLANE + ROWS, col] = high
            feat_ref[step * PLANE + ROWS:step * PLANE + 2 * ROWS, col] = low
    row = rows_of((10, 128))
    inside = jnp.where((row == 0) & (gy == 0), 0.0, 1.0)
    inside = jnp.where((row == 9) & (gy == ids_ref[4] - 1), 0.0, inside)
    for x in range(5):
        both = once(wide_ref[...], feat_ref[x * PLANE:x * PLANE + REACH, :])
        pre = both[0:HIDDEN] + both[HIDDEN:]
        sig = 0.5 * jnp.tanh(0.5 * pre) + 0.5
        kept_ref[x] = sig * (1.0 + pre * (1.0 - sig))
        pltpu.make_async_copy(kept_ref.at[x], slope_ref.at[x], sems.at[x]).start()
        hid_ref[...] = pre * sig
        for half in range(2):
            e = x + 5 * half
            mask = inside
            if e == 0:
                mask = inside * jnp.where(gx == 0, 0.0, 1.0)
            if e == 9:
                mask = inside * jnp.where(gx == ids_ref[3] - 1, 0.0, 1.0)
            sums = []
            for y in range(SPAN):
                here = [hid_ref[y * WIDTH + 8 * i:y * WIDTH + 8 * i + 8, 128 * half:128 * half + 128] for i in range(4)]
                for k in range(3):
                    terms = [out_ref[WIDTH * k + 8 * i:WIDTH * k + 8 * i + 8, :] * here[i] for i in range(4)]
                    sums.append((terms[0] + terms[1]) + (terms[2] + terms[3]))
            rest = fold([sums[3 * y + k] for k in range(3) for y in (8, 9)] + [sums[0]] * 2)
            for k in range(3):
                ce_ref[k, e, 0:8, :] = fold([sums[3 * y + k] for y in range(8)])
                ce_ref[k, e, 8:10, :] = rest[2 * k:2 * k + 2, :]
                ce_ref[k, e, 0:10, :] = (ce_ref[k, e, 0:10, :] + bias_ref[k] + ext_ref[k, e + 1, 1:11, :]) * mask
    for k in range(3):
        for x in range(8):
            closed_ref[k, x] = ce_ref[k, x + 1, 1:9, :]
    send_rows(lambda k, x, y: ce_ref[k, x, pl.ds(y, 8), :], flat_ref, sent_ref)
    for x in range(5):
        pltpu.make_async_copy(kept_ref.at[x], slope_ref.at[x], sems.at[x]).wait()


def around(grid, wide, masks):
    (x_low, x_high, y_low, y_high) = masks
    lane = lanes()
    size = len(grid[0])
    result = []
    for c in range(2):
        plane = []
        for x in range(size):
            line = []
            for y in range(size):
                here = grid[c][x][y]
                total = jnp.where(lane >= wide, roll(here, wide, 1), 0.0)
                total = total + jnp.where(lane < 128 - wide, roll(here, 128 - wide, 1), 0.0)
                total = total + (grid[c][x - 1][y] if x > 0 else roll(grid[c][size - 1][y], 1, 0) * x_low)
                total = total + (grid[c][x + 1][y] if x < size - 1 else roll(grid[c][0][y], 7, 0) * x_high)
                if y > 0:
                    total = total + grid[c][x][y - 1]
                else:
                    edge = grid[1 - c][x][size - 1]
                    total = total + (edge if c == 1 else roll(edge, 4, 0) * y_low)
                if y < size - 1:
                    total = total + grid[c][x][y + 1]
                else:
                    edge = grid[1 - c][x][0]
                    total = total + (edge if c == 0 else roll(edge, 4, 0) * y_high)
                line.append(total)
            plane.append(line)
        result.append(plane)
    return result


def over(function, *grids):
    size = len(grids[0][0])
    return [[[function(*(g[c][x][y] for g in grids)) for y in range(size)] for x in range(size)] for c in range(2)]


def flat(grid):
    return tuple(v for plane in grid for line in plane for v in line)


def unflat(values, size):
    values = list(values)
    return [[[values[(c * size + x) * size + y] for y in range(size)] for x in range(size)] for c in range(2)]


def relax_level(guess, source, wide, masks):
    return over(lambda g, s, n: KEEP * g + STEP * (s + n), guess, source, around(guess, wide, masks))


def residue_level(guess, source, wide, masks):
    return over(lambda g, s, n: s - 6.0 * g + n, guess, source, around(guess, wide, masks))


def coarser(grid, wide):
    lane = lanes()
    size = len(grid[0]) // 2
    even = (lane // wide) % 2 == 0
    result = []
    for c in range(2):
        plane = []
        for x in range(size):
            line = []
            for y in range(size):
                t = grid[c][2 * x][2 * y] + grid[c][2 * x][2 * y + 1]
                t = t + grid[c][2 * x + 1][2 * y] + grid[c][2 * x + 1][2 * y + 1]
                line.append(0.5 * (t + jnp.where(even, roll(t, 128 - wide, 1), roll(t, wide, 1))))
            plane.append(line)
        result.append(plane)
    return result


def add_coarse(grid, coarse):
    size = len(grid[0])
    return [[[grid[c][x][y] + coarse[c][x // 2][y // 2] for y in range(size)] for x in range(size)] for c in range(2)]


def level_solve(source, level, sweeps_ref, masks):
    wide = 1 << (level - 1)
    size = len(source[0])
    guess = over(lambda s: STEP * s, source)
    if level == LEVELS:
        for _ in range(COARSE_SWEEPS - 1):
            guess = relax_level(guess, source, wide, masks)
        return guess
    repeats = sweeps_ref[level]

    def body(number, state):
        return flat(relax_level(unflat(state, size), source, wide, masks))

    guess = unflat(lax.fori_loop(1, repeats, body, flat(guess)), size)
    coarse = coarser(residue_level(guess, source, wide, masks), wide)
    guess = add_coarse(guess, level_solve(coarse, level + 1, sweeps_ref, masks))
    return unflat(lax.fori_loop(0, repeats, body, flat(guess)), size)


def project_kernel(ext, ids_ref, sweeps_ref, field_ref, *refs):
    source_refs, refs = refs[:4 if ext else 2], refs[4 if ext else 2:]
    if ext:
        result_ref, s_ref, x_ref, p_ref, wrap_ref, edge_ref, win_ref, nat_ref = refs
    else:
        part_ref, over_ref, result_ref, grad_ref, s_ref, x_ref, p_ref, wrap_ref, edge_ref, win_ref, nat_ref = refs
        join(ids_ref, part_ref, over_ref, grad_ref)
    sent = SENT_OWN if ext else SENT
    gx, gy, gz = ids_ref[0], ids_ref[1], ids_ref[2]
    core = lax.rem(gy, 2)
    lane = lanes()
    sub = rows_of()
    x_low = jnp.where(sub % 4 != 0, 1.0, 0.0)
    x_high = jnp.where(sub % 4 != 3, 1.0, 0.0)
    y_low = jnp.where(sub >= 4, 1.0, 0.0)
    y_high = jnp.where(sub < 4, 1.0, 0.0)
    masks = (x_low, x_high, y_low, y_high)
    z_low = jnp.where(lane != 0, 1.0, 0.0)
    z_high = jnp.where(lane != 127, 1.0, 0.0)
    lower = lane < 64

    if ext:
        near_ref, far_ref, near_twin_ref, far_twin_ref = source_refs
        sources = ((near_ref, far_ref, core), (near_twin_ref, far_twin_ref, 1 - core))
    else:
        mine_ref, other_ref = source_refs
        sources = ((mine_ref, mine_ref.at[pl.ds(8 * sent, 8 * sent)], core),
                   (other_ref, other_ref.at[pl.ds(8 * sent, 8 * sent)], 1 - core))

    def both(near_ref, far_ref, i):
        near = near_ref[pl.ds(i, 8, stride=sent), :]
        far = far_ref[pl.ds(i, 8, stride=sent), :]
        if ext:
            return jnp.where(gz == 0, near, far), jnp.where(gz == 0, far, near)
        return near, far

    def halves(near_ref, far_ref, i):
        first, second = both(near_ref, far_ref, i)
        return jnp.where(lower, first, roll(second, 64, 1)), jnp.where(lower, roll(first, 64, 1), second)

    for near_ref, far_ref, slot in sources:
        face0, face1 = both(near_ref, far_ref, 64)
        for x in range(8):
            for y in range(8):
                i = 8 * x + y
                even, odd = halves(near_ref, far_ref, i)
                even = even + jnp.where(lane == 64, roll(face0, (128 - i) % 128, 1), 0.0)
                odd = odd + jnp.where(lane == 63, roll(face1, (63 - i) % 128, 1), 0.0)
                for zi, value in ((0, even), (1, odd)):
                    s_ref[slot, zi, x, y] = value
                    x_ref[slot, zi, x, y] = STEP * value

    def also(slot, zi, x, y, value):
        s_ref[slot, zi, x, y] = s_ref[slot, zi, x, y] + value
        x_ref[slot, zi, x, y] = x_ref[slot, zi, x, y] + STEP * value

    if ext:
        for near_ref, far_ref, slot in sources:
            for at in range(8):
                for zi, value in enumerate(halves(near_ref, far_ref, 72 + at)):
                    also(1 - slot, zi, at, 7, jnp.where(slot == 1, value, roll(value, 4, 0) * y_high))
                for zi, value in enumerate(halves(near_ref, far_ref, 80 + at)):
                    also(1 - slot, zi, at, 0, jnp.where(slot == 0, value, roll(value, 4, 0) * y_low))

    every = [(zi, y) for zi in range(2) for y in range(8)]

    def visit(use):
        for c in range(2):
            first = {at: x_ref[c, at[0], 0, at[1]] for at in every}
            before = {at: roll(x_ref[c, at[0], 7, at[1]], 1, 0) * x_low for at in every}
            for at in every:
                wrap_ref[at[0], at[1]] = roll(first[at], 7, 0) * x_high
            own = first
            for x in range(8):
                after = {at: x_ref[c, at[0], x + 1, at[1]] if x < 7 else wrap_ref[at[0], at[1]] for at in every}
                for zi in range(2):
                    if c == 0:
                        down = roll(x_ref[1, zi, x, 7], 4, 0) * y_low
                        up = x_ref[1, zi, x, 0]
                        edge_ref[zi, x, 0] = own[zi, 7]
                        edge_ref[zi, x, 1] = roll(own[zi, 0], 4, 0) * y_high
                    else:
                        down = edge_ref[zi, x, 0]
                        up = edge_ref[zi, x, 1]
                    for y in range(8):
                        beside = own[1 - zi, y]
                        total = before[zi, y] + after[zi, y] + beside
                        total = total + (own[zi, y - 1] if y > 0 else down) + (own[zi, y + 1] if y < 7 else up)
                        if zi == 0:
                            total = total + roll(beside, 1, 1) * z_low
                        else:
                            total = total + roll(beside, 127, 1) * z_high
                        value = use(c, zi, x, y, own[zi, y], total)
                        if value is not None:
                            x_ref[c, zi, x, y] = value
                before, own = own, after

    def sweep(number, carry):
        visit(lambda c, zi, x, y, own, total: KEEP * own + STEP * (s_ref[c, zi, x, y] + total))
        return carry

    repeats = sweeps_ref[0]

    def cycle(number, carry):
        lax.fori_loop(1, repeats, sweep, 0)
        sums = {}

        def gather(c, zi, x, y, own, total):
            e = s_ref[c, zi, x, y] - 6.0 * own + total
            at = (c, x // 2, y // 2)
            sums[at] = sums[at] + e if at in sums else e

        visit(gather)
        coarse = [[[0.5 * sums[c, x, y] for y in range(4)] for x in range(4)] for c in range(2)]
        coarse = level_solve(coarse, 1, sweeps_ref, masks)
        for c in range(2):
            for zi in range(2):
                for x in range(8):
                    for y in range(8):
                        x_ref[c, zi, x, y] = x_ref[c, zi, x, y] + coarse[c][x // 2][y // 2]
        lax.fori_loop(0, repeats, sweep, 0)

        @pl.when(number == 0)
        def _():
            def restart(c, zi, x, y, own, total):
                p_ref[c, zi, x, y] = own
                rest = s_ref[c, zi, x, y] - 6.0 * own + total
                s_ref[c, zi, x, y] = rest
                return STEP * rest

            visit(restart)

        return carry

    lax.fori_loop(0, CYCLES, cycle, 0)

    x_rows = x_ref.reshape(2 * 2 * 8 * 8 * 8, 128)
    p_rows = p_ref.reshape(2 * 2 * 8 * 8 * 8, 128)
    last_x, last_y = ids_ref[3] - 1, ids_ref[4] - 1
    for wx in range(12):
        dx = -1 if wx < 2 else (1 if wx > 9 else 0)
        xi = (wx - 2) % 8
        bx = gx + dx
        for dy in (-1, 0, 1):
            by = gy + dy
            ok = (bx >= 0) & (bx <= last_x) & (by >= 0) & (by <= last_y)
            ax = jnp.clip(bx, 0, last_x)
            ay = jnp.clip(by, 0, last_y)
            at = (ay // 2) * 4 + ax
            c = lax.rem(ay, 2)
            for zi in range(2):
                start = ((c * 2 + zi) * 8 + xi) * 64 + at
                first = x_rows[pl.ds(start, 8, stride=8), :]
                second = p_rows[pl.ds(start, 8, stride=8), :]
                win_ref[wx * 24 + 8 * (dy + 1):wx * 24 + 8 * (dy + 1) + 8, 128 * zi:128 * zi + 128] = jnp.where(
                    ok, first + second, 0.0)
    source = lax.broadcasted_iota(jnp.int32, (256, 256), 0)
    target = lanes((256, 256))
    depth = 2 * (source % 128) + source // 128
    wanted = jnp.where(target == 255, -1, target) + gz * 128
    pick = jnp.where((depth == wanted) & ((target <= 128) | (target == 255)), 1.0, 0.0)
    nat_ref[...] = exact(win_ref[...], pick)

    size = 16 if ext else 8
    count = 10 if ext else 8
    lane = lanes((count, 128))
    row = rows_of((count, 128))
    for i in range(count):
        x = i - 1 if ext else i
        top = 7 if ext else 8
        base = (x + 2) * 24 + top
        mid = nat_ref[pl.ds(base, count), 0:128]
        tail = nat_ref[pl.ds(base, count), 128:256]
        sx = nat_ref[pl.ds(base + 24, count), 0:128] - nat_ref[pl.ds(base - 24, count), 0:128]
        sy = nat_ref[pl.ds(base + 1, count), 0:128] - nat_ref[pl.ds(base - 1, count), 0:128]
        sz = roll(jnp.where(lane == 0, tail, mid), 127, 1) - roll(jnp.where(lane == 127, tail, mid), 1, 1)
        for k, s in enumerate((sx, sy, sz)):
            if ext:
                value = field_ref[k, i] + 0.5 * s
                good = jnp.where((row == 0) & (gy == 0), 0.0, 1.0)
                good = jnp.where((row == 9) & (gy == last_y), 0.0, good)
                if i == 0:
                    good = good * jnp.where(gx == 0, 0.0, 1.0)
                if i == 9:
                    good = good * jnp.where(gx == last_x, 0.0, 1.0)
                result_ref[k, i] = jnp.zeros((16, 128), F32)
                result_ref[k, i, 0:10, :] = value * good
            else:
                result_ref[k, i] = field_ref[k, i] + 0.5 * s


def backward_kernel(ids_ref, adj_ref, slope_ref, tall_ref, back_ref, grad_ref, over_ref, in_ref, bb_ref, acc_ref):
    gz = ids_ref[2]
    in_ref[144:256, :] = jnp.zeros((112, 256), BF16)
    bb_ref[3 * HIDDEN:DEEP, :] = jnp.zeros((DEEP - 3 * HIDDEN, 256), BF16)
    acc_ref[...] = jnp.zeros(acc_ref.shape, F32)
    for x in range(5):
        for half in range(2):
            col = slice(128 * half, 128 * half + 128)
            for k in range(3):
                high, low = split(adj_ref[k, x + 5 * half])
                in_ref[16 * k:16 * k + 16, col] = high
                in_ref[48 + 16 * k:64 + 16 * k, col] = low
                in_ref[96 + 16 * k:112 + 16 * k, col] = high
        high, low = split(once(back_ref[...], in_ref[...]) * slope_ref[x])
        bb_ref[0:HIDDEN, :] = high
        bb_ref[HIDDEN:2 * HIDDEN, :] = low
        bb_ref[2 * HIDDEN:3 * HIDDEN, :] = high
        total = once(tall_ref[...], bb_ref[...])
        for half in range(2):
            for a in range(3):
                at = x + 5 * half + a
                acc_ref[at] = acc_ref[at] + total[72 * a:72 * a + 72, 128 * half:128 * half + 128]
    lane = lanes()
    row = rows_of()
    for k in range(3):
        packed = jnp.zeros((8, 128), F32)
        for x in range(8):
            low = acc_ref[x + 2, 8 * k:8 * k + 8, :]
            mid = acc_ref[x + 2, 24 + 8 * k:32 + 8 * k, :]
            high = acc_ref[x + 2, 48 + 8 * k:56 + 8 * k, :]
            value = adj_ref[k, x + 1, 1:9, :] + mid
            value = value + jnp.where(lane == 127, 0.0, roll(low, 127, 1))
            grad_ref[k, x] = value + jnp.where(lane == 0, 0.0, roll(high, 1, 1))
            out = jnp.where(gz == 0, high[:, 127:128], low[:, 0:1])
            packed = packed + jnp.where(lane == 8 * x + row, out, 0.0)
        over_ref[k:k + 1, :] = jnp.sum(packed, axis=0, keepdims=True)
    over_ref[3:8, :] = jnp.zeros((5, 128), F32)


def join(ids_ref, part_ref, over_ref, grad_ref):
    gz = ids_ref[2]
    lane = lanes()
    row = rows_of()
    edge = jnp.where(gz == 0, 127, 0)
    for k in range(3):
        for x in range(8):
            column = jnp.sum(jnp.where(lane == 8 * x + row, over_ref[k:k + 1, :], 0.0), axis=1, keepdims=True)
            grad_ref[k, x] = part_ref[k, x] + jnp.where(lane == edge, column, 0.0)


VMEM = pl.BlockSpec(memory_space=pltpu.VMEM)
SMEM = pl.BlockSpec(memory_space=pltpu.SMEM)


def call(kernel, specs, shapes, scratch, *operands, flops=0, size=1 << 20, outs=None):
    return pl.pallas_call(
        kernel,
        in_specs=specs,
        out_specs=outs or [VMEM] * len(shapes),
        out_shape=[s if hasattr(s, "memory_space") else jax.ShapeDtypeStruct(*s) for s in shapes],
        scratch_shapes=scratch,
        compiler_params=pltpu.CompilerParams(vmem_limit_bytes=12 * 2**20),
        cost_estimate=pl.CostEstimate(flops=flops, bytes_accessed=size, transcendentals=0),
    )(*operands)


def trade(velocity, cotangent, axis, dim):
    count = lax.axis_size(axis)
    odd = lax.rem(lax.axis_index(axis), 2) == 1
    size = velocity.shape[dim]

    def cut(array, start, stop):
        return lax.slice_in_dim(array, start, stop, axis=dim)

    other = 3 - dim
    grow = [(0, 0)] * 4
    grow[other] = (0, velocity.shape[other] - cotangent.shape[other])
    low = jnp.concatenate([cut(velocity, 0, 2), jnp.pad(cut(cotangent, 0, 1), grow)], axis=dim)
    high = jnp.concatenate([cut(velocity, size - 2, size), jnp.pad(cut(cotangent, size - 1, size), grow)], axis=dim)
    pairs = [(i, i ^ 1) for i in range(count)]
    gaps = [(i, i + 1) for i in range(1, count - 1, 2)]
    gaps = gaps + [(j, i) for i, j in gaps]
    second = lax.ppermute(jnp.where(odd, high, low), axis, gaps)
    first = lax.ppermute(jnp.where(odd, low, high), axis, pairs)
    below, above = jnp.where(odd, first, second), jnp.where(odd, second, first)
    wide = jnp.concatenate([cut(below, 0, 2), velocity, cut(above, 0, 2)], axis=dim)
    kept = cotangent.shape[other]
    narrow = jnp.concatenate([lax.slice_in_dim(cut(below, 2, 3), 0, kept, axis=other), cotangent,
                              lax.slice_in_dim(cut(above, 2, 3), 0, kept, axis=other)], axis=dim)
    return wide, narrow


def gather_own(rows):
    nx, ny, nz = (lax.axis_size(a) for a in AXES)
    groups = [[(x * ny + 2 * y + c) * nz + z for z in range(nz) for y in range(ny // 2) for x in range(nx)]
              for c in range(2)]
    count = len(groups[0])
    spread = jnp.broadcast_to(rows[None], (count,) + rows.shape)
    mine = lax.all_to_all(spread, AXES, 0, 0, axis_index_groups=groups)
    return mine.reshape(count * rows.shape[0], rows.shape[1])


def twin(mine):
    return lax.ppermute(mine, "gy", [(i, i ^ 1) for i in range(lax.axis_size("gy"))])


def collect(rows):
    x = lax.axis_index("gx")
    odd, upper = lax.rem(x, 2) == 1, x >= 2
    one, two, three = (lax.ppermute(rows, "gx", [(i, i ^ d) for i in range(4)]) for d in (1, 2, 3))
    a, b = jnp.where(odd, one, rows), jnp.where(odd, rows, one)
    c, d = jnp.where(odd, three, two), jnp.where(odd, two, three)
    line = jnp.concatenate([jnp.where(upper, c, a), jnp.where(upper, d, b),
                            jnp.where(upper, a, c), jnp.where(upper, b, d)], axis=0)
    across = lax.ppermute(line, "gy", [(i, i ^ 2) for i in range(4)])
    upper = lax.axis_index("gy") >= 2
    near = jnp.concatenate([jnp.where(upper, across, line), jnp.where(upper, line, across)], axis=0)
    return near, lax.ppermute(near, "gz", [(0, 1), (1, 0)])


def project_rows(ext, ids, sweeps, field, *more):
    block = ((3, 8, 8, 128), F32)
    scratch = [
        pltpu.VMEM((2, 2, 8, 8, 8, 128), F32),
        pltpu.VMEM((2, 2, 8, 8, 8, 128), F32),
        pltpu.VMEM((2, 2, 8, 8, 8, 128), F32),
        pltpu.VMEM((2, 8, 8, 128), F32),
        pltpu.VMEM((2, 8, 2, 8, 128), F32),
        pltpu.VMEM((288, 256), F32),
        pltpu.VMEM((288, 256), F32),
    ]
    return call(functools.partial(project_kernel, ext), [SMEM, SMEM] + [VMEM] * (1 + len(more)),
                [((3, 10, 16, 128), F32)] if ext else [block, block], scratch,
                ids, sweeps, field, *more, flops=6 * 10**9)


def weights(first_weight, first_bias, second_weight):
    return call(
        weights_kernel, [VMEM] * 3,
        [((2 * HIDDEN, REACH), BF16), ((216, DEEP), BF16), ((3 * WIDTH, 128), F32), ((HIDDEN, 256), BF16)],
        [pltpu.VMEM((256, 128), F32)], first_weight, first_bias[None], second_weight, flops=10**9)


def forward(ids, second_bias, near, face, wide, out):
    return call(
        forward_kernel, [SMEM, SMEM] + [VMEM] * 4,
        [((3, 8, 8, 128), F32), pltpu.HBM((5, HIDDEN, 256), F32), ((SENT, 128), F32)],
        [pltpu.VMEM((ROWS, 128), F32), pltpu.VMEM((4 * PLANE + REACH, 256), BF16), pltpu.VMEM((HIDDEN, 256), F32),
         pltpu.VMEM((3, 10, 16, 128), F32), pltpu.VMEM((64, 128), F32), pltpu.VMEM((5, HIDDEN, 256), F32),
         pltpu.SemaphoreType.DMA((5,))],
        ids, second_bias, near, face, wide, out, flops=4 * 10**9,
        outs=[VMEM, pl.BlockSpec(memory_space=pltpu.HBM), VMEM])


def gathered(velocity, cotangent, first_weight, first_bias, second_weight, second_bias, sweeps):
    swap = [(0, 1), (1, 0)]
    ids = jnp.stack([lax.axis_index("gx"), lax.axis_index("gy"), lax.axis_index("gz"),
                     jnp.int32(lax.axis_size("gx")), jnp.int32(lax.axis_size("gy"))]).astype(jnp.int32)
    near, cot_near = trade(velocity, cotangent, "gx", 1)
    cot_rows = call(own_rows_kernel, [VMEM], [((SENT_OWN, 128), F32)], [pltpu.VMEM((80, 128), F32)], cot_near)[0]
    cot_own, cot_far = collect(cot_rows)
    near, cot_near = trade(near, cot_near, "gy", 2)
    face = jnp.where(ids[2] == 0, near[:, :, :, 127], near[:, :, :, 0])
    face = lax.ppermute(face, "gz", swap)
    wide, tall, out, back = weights(first_weight, first_bias, second_weight)
    closed, slope, rows = forward(ids, second_bias, near, face, wide, out)
    mine = gather_own(rows)
    cot_far, rows = lax.optimization_barrier((cot_far, rows))
    adjoint = project_rows(True, ids, sweeps, cot_near, cot_own, cot_far, twin(cot_own), twin(cot_far))[0]
    part, over_rows = call(
        backward_kernel, [SMEM] + [VMEM] * 4, [((3, 8, 8, 128), F32), ((8, 128), F32)],
        [pltpu.VMEM((256, 256), BF16), pltpu.VMEM((DEEP, 256), BF16), pltpu.VMEM((12, 72, 128), F32)],
        ids, adjoint, slope, tall, back, flops=10**6)
    over_rows = lax.ppermute(over_rows, "gz", swap)
    mine, part, over_rows = lax.optimization_barrier((mine, part, over_rows))
    updated, grad = project_rows(False, ids, sweeps, closed, mine, twin(mine), part, over_rows)
    return updated, grad


def one_gather(velocity, first_weight):
    nx, ny, nz = (lax.axis_size(a) for a in AXES)
    return (velocity.shape == (3, 8, 8, 128) and nx == 4 and ny == 4 and nz == 2
            and first_weight.shape == (WIDTH, 81))


def dispatch(velocity, cotangent, first_weight, first_bias, second_weight, second_bias, sweeps):
    path = gathered if one_gather(velocity, first_weight) else shards
    return path(velocity, cotangent, first_weight, first_bias, second_weight, second_bias, sweeps)


def solution(mesh):
    return jax.shard_map(
        dispatch,
        mesh=mesh,
        in_specs=(P(None, "gx", "gy", "gz"), P(None, "gx", "gy", "gz"), P(), P(), P(), P(), P()),
        out_specs=(P(None, "gx", "gy", "gz"), P(None, "gx", "gy", "gz")),
        check_vma=False,
    )
```

```python
import functools

import jax
import jax.numpy as jnp
from jax import lax
from jax.experimental import pallas as pl
from jax.experimental.pallas import tpu as pltpu
from jax.sharding import PartitionSpec as P

LEVELS = 3
COARSE_SWEEPS = 6
CYCLES = 2


OMEGA = 0.8


def with_halo(block, sides, width):
    for axis, dim in sides:
        count = lax.axis_size(axis)
        forward = [(i, i + 1) for i in range(count - 1)]
        backward = [(target, source) for source, target in forward]
        low = lax.ppermute(
            lax.slice_in_dim(block, block.shape[dim] - width, None, axis=dim), axis, forward
        )
        high = lax.ppermute(lax.slice_in_dim(block, 0, width, axis=dim), axis, backward)
        block = jnp.concatenate([low, block, high], axis=dim)
    return block


def stencil_features(region):
    span_y = region.shape[2] - 2
    span_z = region.shape[3] - 2
    shifted = [
        region[:, first, second : second + span_y, third : third + span_z]
        for first in range(3)
        for second in range(3)
        for third in range(3)
    ]
    return jnp.stack(shifted).reshape(27 * region.shape[0], span_y * span_z)


def six_point(field, padded):
    beside = padded[:, 2:, 1:-1, 1:-1] + padded[:, :-2, 1:-1, 1:-1]
    beside = beside + padded[:, 1:-1, 2:, 1:-1] + padded[:, 1:-1, :-2, 1:-1]
    beside = beside + padded[:, 1:-1, 1:-1, 2:] + padded[:, 1:-1, 1:-1, :-2]
    return 6.0 * field - beside


def near_faces(field):
    return with_halo(field, (("gx", 1), ("gy", 2), ("gz", 3)), 1)


def laplace_shared(field):
    return six_point(field, near_faces(field))


def relax(guess, source):
    return guess + OMEGA * (source - laplace_shared(guess)) / 6.0


def restrict(residue):
    batch, size_x, size_y, size_z = residue.shape
    folded = residue.reshape(batch, size_x // 2, 2, size_y // 2, 2, size_z // 2, 2)
    return 0.5 * folded.sum(axis=(2, 4, 6))


def prolong(coarse):
    return jnp.repeat(jnp.repeat(jnp.repeat(coarse, 2, axis=1), 2, axis=2), 2, axis=3)


def coarse_spread(source, sweeps):
    guess = OMEGA * source / 6.0
    return lax.fori_loop(1, COARSE_SWEEPS, lambda number, state: relax(state, source), guess)


def vcycle(source, sweeps, level, coarse_solve, bottom):
    if level == bottom:
        return coarse_solve(source, sweeps)
    repeats = sweeps[level]
    guess = OMEGA * source / 6.0
    guess = lax.fori_loop(1, repeats, lambda number, state: relax(state, source), guess)
    residue = source - laplace_shared(guess)
    guess = guess + prolong(vcycle(restrict(residue), sweeps, level + 1, coarse_solve, bottom))
    return lax.fori_loop(0, repeats, lambda number, state: relax(state, source), guess)


def divergence(padded):
    total = padded[:, 0, 2:, 1:-1, 1:-1] - padded[:, 0, :-2, 1:-1, 1:-1]
    total = total + padded[:, 1, 1:-1, 2:, 1:-1] - padded[:, 1, 1:-1, :-2, 1:-1]
    total = total + padded[:, 2, 1:-1, 1:-1, 2:] - padded[:, 2, 1:-1, 1:-1, :-2]
    return 0.5 * total


def gradient(padded):
    return 0.5 * jnp.stack(
        [
            padded[:, 2:, 1:-1, 1:-1] - padded[:, :-2, 1:-1, 1:-1],
            padded[:, 1:-1, 2:, 1:-1] - padded[:, 1:-1, :-2, 1:-1],
            padded[:, 1:-1, 1:-1, 2:] - padded[:, 1:-1, 1:-1, :-2],
        ],
        axis=1,
    )


def project(fields, sweeps, coarse_solve, bottom):
    batch, comps, size_x, size_y, size_z = fields.shape
    padded = near_faces(fields.reshape(batch * comps, size_x, size_y, size_z))
    padded = padded.reshape(batch, comps, size_x + 2, size_y + 2, size_z + 2)
    source = divergence(padded)
    pressure = vcycle(source, sweeps, 0, coarse_solve, bottom)
    pressure = pressure + vcycle(source - laplace_shared(pressure), sweeps, 0, coarse_solve, bottom)
    return fields + gradient(near_faces(pressure))


def corrections(near, first_weight, first_bias, second_weight, second_bias, planes):
    span_y = near.shape[2] - 2
    span_z = near.shape[3] - 2

    def corrections_one_plane(index):
        region = lax.dynamic_slice_in_dim(near, index, 3, 1)
        feats = stencil_features(region)
        hidden = jax.nn.silu(
            jnp.dot(first_weight, feats, precision=lax.Precision.HIGHEST) + first_bias[:, None]
        )
        return (
            jnp.dot(second_weight, hidden, precision=lax.Precision.HIGHEST) + second_bias[:, None]
        )

    result = lax.map(corrections_one_plane, jnp.arange(planes, dtype=jnp.int32))
    return result.reshape(planes, 3, span_y, span_z).transpose(1, 0, 2, 3)


def back_planes(wide, cot_pad, first_weight, first_bias, second_weight, planes):
    span_y = cot_pad.shape[2] - 2
    span_z = cot_pad.shape[3] - 2

    def back_one_plane(index):
        region = lax.dynamic_slice_in_dim(wide, index, 3, 1)
        feats = stencil_features(region)
        pre = jnp.dot(first_weight, feats, precision=lax.Precision.HIGHEST) + first_bias[:, None]
        sig = jax.nn.sigmoid(pre)
        slope = sig * (1.0 + pre * (1.0 - sig))
        incoming = lax.dynamic_index_in_dim(cot_pad, index, 1, keepdims=False).reshape(3, -1)
        back = jnp.dot(second_weight.T, incoming, precision=lax.Precision.HIGHEST) * slope
        spread = jnp.dot(first_weight.T, back, precision=lax.Precision.HIGHEST)
        spread = spread.reshape(3, 3, 3, 3, span_y + 2, span_z + 2)
        parts = []
        for first in range(3):
            total = jnp.zeros((3, span_y, span_z), jnp.float32)
            for second in range(3):
                for third in range(3):
                    total = (
                        total
                        + spread[
                            first,
                            second,
                            third,
                            :,
                            2 - second : 2 - second + span_y,
                            2 - third : 2 - third + span_z,
                        ]
                    )
            parts.append(total)
        return jnp.stack(parts)

    pieces = lax.map(back_one_plane, jnp.arange(planes + 2, dtype=jnp.int32))
    return pieces[:-2, 2] + pieces[1:-1, 1] + pieces[2:, 0]


def shards(velocity, cotangent, first_weight, first_bias, second_weight, second_bias, sweeps):
    planes = velocity.shape[1]
    near = with_halo(velocity, (("gx", 1), ("gy", 2), ("gz", 3)), 1)
    coarse_solve, bottom = (coarse_spread, LEVELS)
    closed = velocity + corrections(
        near, first_weight, first_bias, second_weight, second_bias, planes
    )
    updated = project(closed[None], sweeps, coarse_solve, bottom)[0]
    adjoint_closed = project(cotangent[None], sweeps, coarse_solve, bottom)[0]
    wide = with_halo(velocity, (("gx", 1), ("gy", 2), ("gz", 3)), 2)
    cot_pad = with_halo(adjoint_closed, (("gx", 1), ("gy", 2), ("gz", 3)), 1)
    summed = back_planes(wide, cot_pad, first_weight, first_bias, second_weight, planes)
    grad_velocity = adjoint_closed + summed.transpose(1, 0, 2, 3)
    return (updated, grad_velocity)


AXES = ("gx", "gy", "gz")
STEP = OMEGA / 6.0
KEEP = 1.0 - OMEGA
WIDTH = 32
SPAN = 10
ROWS = 112
PLANE = 2 * ROWS
REACH = 768
DEEP = 1024
HIDDEN = SPAN * WIDTH
SENT = 72
SENT_OWN = 88
F32 = jnp.float32
BF16 = jnp.bfloat16


def roll(value, shift, axis):
    return pltpu.roll(value, shift, axis)


def lanes(shape=(8, 128)):
    return lax.broadcasted_iota(jnp.int32, shape, len(shape) - 1)


def rows_of(shape=(8, 128)):
    return lax.broadcasted_iota(jnp.int32, shape, len(shape) - 2)


def split(value):
    high = value.astype(BF16)
    return high, (value - high.astype(F32)).astype(BF16)


def exact(left, right):
    high = left.astype(BF16)
    rest = left - high.astype(F32)
    middle, low = split(rest)
    right = right.astype(BF16)
    return (once(high, right) + once(middle, right)) + once(low, right)


def once(left, right):
    return jnp.dot(left, right, preferred_element_type=F32)


def one_hot(condition):
    return jnp.where(condition, 1.0, 0.0).astype(BF16)


def column_of(line, size):
    square = (size, size)
    return jnp.sum(jnp.where(rows_of(square) == lanes(square), line, 0.0), axis=1, keepdims=True)


def weights_kernel(first_ref, bias_ref, second_ref, wide_ref, tall_ref, out_ref, back_ref, pad_ref):
    count = first_ref.shape[1]
    pad_ref[...] = jnp.zeros((256, 128), F32)
    pad_ref[0:WIDTH, 0:count] = first_ref[...]
    pad_ref[128:131, 0:WIDTH] = second_ref[...]
    first = pad_ref[0:128, :]
    second = pad_ref[128:256, :]
    high, low = split(first[0:WIDTH])
    column = lanes((1, REACH))
    rest = column % ROWS
    real = (rest < 108) & (column < 3 * PLANE)
    height = jnp.where(real, rest % 12, -1)
    feature = jnp.where(real, 27 * (column // PLANE) + rest // 12, -1000)
    upper = (column % PLANE) < ROWS
    bias_high, bias_low = split(column_of(bias_ref[...], WIDTH))
    totals = [jnp.where(column == 108, part.astype(F32), 0.0) for part in (bias_high, bias_low)]
    row = rows_of((128, REACH))
    parts = []
    for b in range(3):
        chosen = one_hot(row - 9 * b == feature)
        parts.append((once(high, chosen), jnp.where(upper, once(low, chosen), 0.0)))
    for y in range(SPAN):
        for half in range(2):
            total = totals[half]
            for b in range(3):
                total = total + jnp.where(height == y + b, parts[b][half], 0.0)
            wide_ref[half * HIDDEN + y * WIDTH:half * HIDDEN + (y + 1) * WIDTH, :] = total.astype(BF16)
    high, low = split(first.T)
    column = lanes((1, DEEP))
    row = rows_of((128, DEEP))
    place = (column % HIDDEN) // WIDTH
    term = column // HIDDEN
    tiled = one_hot((row == column % WIDTH) & (column < 3 * HIDDEN))
    copies = jnp.where(term == 2, once(low, tiled), once(high, tiled)).astype(BF16)
    line = lax.broadcasted_iota(jnp.int32, (216, 128), 0)
    lane = lanes((216, 128))
    tops = line[:, 0:1] % 8 + 2
    total = jnp.zeros((216, DEEP), F32)
    for b in range(3):
        lift = one_hot(lane - 9 * b == 27 * (line // 72) + (line % 72) // 8)
        total = total + jnp.where(tops - b == place, once(lift, copies), 0.0)
    tall_ref[...] = total.astype(BF16)
    for k in range(3):
        line = second[k:k + 1, 0:WIDTH]
        out_ref[WIDTH * k:WIDTH * (k + 1), :] = jnp.broadcast_to(column_of(line, WIDTH), (WIDTH, 128))
    high, low = split(second.T[0:WIDTH])
    column = lanes((1, 256))
    row = rows_of((128, 256))
    inner = one_hot((row == (column % 48) // 16) & (column < 144))
    copies = jnp.where(column // 48 == 2, once(low, inner), once(high, inner))
    for y in range(SPAN):
        back_ref[y * WIDTH:(y + 1) * WIDTH, :] = jnp.where(column % 16 == y, copies, 0.0).astype(BF16)


def depth_order():
    first = lax.broadcasted_iota(jnp.int32, (128, 128), 0)
    return jnp.where((first % 2) * 64 + first // 2 == lanes((128, 128)), 1.0, 0.0)


def send_rows(get, flat_ref, sent_ref):
    lane = lanes()
    row = rows_of()
    faces = jnp.zeros((8, 128), F32)
    for x in range(8):
        up = get(2, x + 1, 1)
        value = get(0, x + 2, 1) - get(0, x, 1) + get(1, x + 1, 2) - get(1, x + 1, 0)
        value = value + jnp.where(lane == 127, 0.0, roll(up, 127, 1)) - jnp.where(lane == 0, 0.0, roll(up, 1, 1))
        flat_ref[8 * x:8 * x + 8, :] = 0.5 * value
        faces = faces + jnp.where(lane == 8 * x + row, 0.5 * up[:, 0:1], 0.0)
        faces = faces - jnp.where(lane == 64 + 8 * x + row, 0.5 * up[:, 127:128], 0.0)
    sent_ref[0:64, :] = exact(flat_ref[...], depth_order())
    sent_ref[64:72, :] = jnp.where(row == 0, jnp.sum(faces, axis=0, keepdims=True), 0.0)


def own_rows_kernel(field_ref, sent_ref, flat_ref):
    lane = lanes()
    row = rows_of()
    faces = jnp.zeros((8, 128), F32)
    for x in range(8):
        along = field_ref[1, x + 1]
        up = field_ref[2, x + 1]
        value = jnp.where(row == 7, 0.0, roll(along, 7, 0)) - jnp.where(row == 0, 0.0, roll(along, 1, 0))
        value = value + jnp.where(lane == 127, 0.0, roll(up, 127, 1)) - jnp.where(lane == 0, 0.0, roll(up, 1, 1))
        flat_ref[8 * x:8 * x + 8, :] = 0.5 * (value + field_ref[0, x + 2] - field_ref[0, x])
        flat_ref[64 + x:65 + x, :] = 0.5 * along[0:1, :]
        flat_ref[72 + x:73 + x, :] = -0.5 * along[7:8, :]
        faces = faces + jnp.where(lane == 8 * x + row, 0.5 * up[:, 0:1], 0.0)
        faces = faces - jnp.where(lane == 64 + 8 * x + row, 0.5 * up[:, 127:128], 0.0)
    turned = exact(flat_ref[...], depth_order())
    sent_ref[0:64, :] = turned[0:64]
    sent_ref[64:72, :] = jnp.where(row == 0, jnp.sum(faces, axis=0, keepdims=True), 0.0)
    sent_ref[72:88, :] = turned[64:80]


def fold(values):
    row = rows_of()
    low = row < 4
    values = [jnp.where(low, a, b) + roll(jnp.where(low, b, a), 4, 0) for a, b in zip(values[:4], values[4:])]
    for step in (2, 1):
        low = (row // step) % 2 == 0
        values = [jnp.where(low, a + roll(a, 8 - step, 0), b + roll(b, step, 0))
                  for a, b in zip(values[:step], values[step:])]
    return values[0]


def forward_kernel(ids_ref, bias_ref, ext_ref, col_ref, wide_ref, out_ref, closed_ref, slope_ref, sent_ref,
                   plane_ref, feat_ref, hid_ref, ce_ref, flat_ref, kept_ref, sems):
    gx, gy, gz = ids_ref[0], ids_ref[1], ids_ref[2]
    low_side = jnp.where(gz == 0, 1.0, 0.0)
    high_side = 1.0 - low_side
    lane = lanes((12, 128))
    pad_row = rows_of((8, 128))
    plane_ref[104:112, :] = jnp.where(pad_row == 4, 1.0, 0.0)
    feat_ref[7 * PLANE:, :] = jnp.zeros((REACH - 3 * PLANE, 256), BF16)
    corner = rows_of((12, 12)) == lanes((12, 12))
    beyond = [[jnp.sum(jnp.where(corner, col_ref[k, at:at + 1, :], 0.0), axis=1, keepdims=True) for at in range(12)]
              for k in range(3)]
    for step in range(7):
        for half in range(2):
            at = step + 5 * half
            for k in range(3):
                here = ext_ref[k, at]
                below = jnp.where(lane == 0, beyond[k][at] * high_side, roll(here, 1, 1))
                above = jnp.where(lane == 127, beyond[k][at] * low_side, roll(here, 127, 1))
                for c, piece in ((0, below), (1, here), (2, above)):
                    plane_ref[pl.ds((c * 3 + k) * 12, 12), :] = piece
            high, low = split(plane_ref[...])
            col = slice(128 * half, 128 * half + 128)
            feat_ref[step * PLANE:step * PLANE + ROWS, col] = high
            feat_ref[step * PLANE + ROWS:step * PLANE + 2 * ROWS, col] = low
    row = rows_of((10, 128))
    inside = jnp.where((row == 0) & (gy == 0), 0.0, 1.0)
    inside = jnp.where((row == 9) & (gy == ids_ref[4] - 1), 0.0, inside)
    for x in range(5):
        both = once(wide_ref[...], feat_ref[x * PLANE:x * PLANE + REACH, :])
        pre = both[0:HIDDEN] + both[HIDDEN:]
        sig = 0.5 * jnp.tanh(0.5 * pre) + 0.5
        kept_ref[x] = sig * (1.0 + pre * (1.0 - sig))
        pltpu.make_async_copy(kept_ref.at[x], slope_ref.at[x], sems.at[x]).start()
        hid_ref[...] = pre * sig
        for half in range(2):
            e = x + 5 * half
            mask = inside
            if e == 0:
                mask = inside * jnp.where(gx == 0, 0.0, 1.0)
            if e == 9:
                mask = inside * jnp.where(gx == ids_ref[3] - 1, 0.0, 1.0)
            sums = []
            for y in range(SPAN):
                here = [hid_ref[y * WIDTH + 8 * i:y * WIDTH + 8 * i + 8, 128 * half:128 * half + 128] for i in range(4)]
                for k in range(3):
                    terms = [out_ref[WIDTH * k + 8 * i:WIDTH * k + 8 * i + 8, :] * here[i] for i in range(4)]
                    sums.append((terms[0] + terms[1]) + (terms[2] + terms[3]))
            rest = fold([sums[3 * y + k] for k in range(3) for y in (8, 9)] + [sums[0]] * 2)
            for k in range(3):
                ce_ref[k, e, 0:8, :] = fold([sums[3 * y + k] for y in range(8)])
                ce_ref[k, e, 8:10, :] = rest[2 * k:2 * k + 2, :]
                ce_ref[k, e, 0:10, :] = (ce_ref[k, e, 0:10, :] + bias_ref[k] + ext_ref[k, e + 1, 1:11, :]) * mask
    for k in range(3):
        for x in range(8):
            closed_ref[k, x] = ce_ref[k, x + 1, 1:9, :]
    send_rows(lambda k, x, y: ce_ref[k, x, pl.ds(y, 8), :], flat_ref, sent_ref)
    for x in range(5):
        pltpu.make_async_copy(kept_ref.at[x], slope_ref.at[x], sems.at[x]).wait()


def around(grid, wide, masks):
    (x_low, x_high, y_low, y_high) = masks
    lane = lanes()
    size = len(grid[0])
    result = []
    for c in range(2):
        plane = []
        for x in range(size):
            line = []
            for y in range(size):
                here = grid[c][x][y]
                total = jnp.where(lane >= wide, roll(here, wide, 1), 0.0)
                total = total + jnp.where(lane < 128 - wide, roll(here, 128 - wide, 1), 0.0)
                total = total + (grid[c][x - 1][y] if x > 0 else roll(grid[c][size - 1][y], 1, 0) * x_low)
                total = total + (grid[c][x + 1][y] if x < size - 1 else roll(grid[c][0][y], 7, 0) * x_high)
                if y > 0:
                    total = total + grid[c][x][y - 1]
                else:
                    edge = grid[1 - c][x][size - 1]
                    total = total + (edge if c == 1 else roll(edge, 4, 0) * y_low)
                if y < size - 1:
                    total = total + grid[c][x][y + 1]
                else:
                    edge = grid[1 - c][x][0]
                    total = total + (edge if c == 0 else roll(edge, 4, 0) * y_high)
                line.append(total)
            plane.append(line)
        result.append(plane)
    return result


def over(function, *grids):
    size = len(grids[0][0])
    return [[[function(*(g[c][x][y] for g in grids)) for y in range(size)] for x in range(size)] for c in range(2)]


def flat(grid):
    return tuple(v for plane in grid for line in plane for v in line)


def unflat(values, size):
    values = list(values)
    return [[[values[(c * size + x) * size + y] for y in range(size)] for x in range(size)] for c in range(2)]


def relax_level(guess, source, wide, masks):
    return over(lambda g, s, n: KEEP * g + STEP * (s + n), guess, source, around(guess, wide, masks))


def residue_level(guess, source, wide, masks):
    return over(lambda g, s, n: s - 6.0 * g + n, guess, source, around(guess, wide, masks))


def coarser(grid, wide):
    lane = lanes()
    size = len(grid[0]) // 2
    even = (lane // wide) % 2 == 0
    result = []
    for c in range(2):
        plane = []
        for x in range(size):
            line = []
            for y in range(size):
                t = grid[c][2 * x][2 * y] + grid[c][2 * x][2 * y + 1]
                t = t + grid[c][2 * x + 1][2 * y] + grid[c][2 * x + 1][2 * y + 1]
                line.append(0.5 * (t + jnp.where(even, roll(t, 128 - wide, 1), roll(t, wide, 1))))
            plane.append(line)
        result.append(plane)
    return result


def add_coarse(grid, coarse):
    size = len(grid[0])
    return [[[grid[c][x][y] + coarse[c][x // 2][y // 2] for y in range(size)] for x in range(size)] for c in range(2)]


def coarsest(source, wide, masks):
    (x_low, x_high, y_low, y_high) = masks
    lane = lanes()
    reach = COARSE_SWEEPS - 1
    moved, inside = {}, {}
    for j in range(-reach, reach + 1):
        at = lane + wide * j
        inside[j] = jnp.where((at >= 0) & (at < 128), 1.0, 0.0)
        for c in range(2):
            here = source[c][0][0]
            moved[j, c] = here if j == 0 else roll(here, (-wide * j) % 128, 1) * inside[j]
    guess = {at: STEP * value for at, value in moved.items()}
    for k in range(1, reach + 1):
        after = {}
        for j in range(k - reach, reach - k + 1):
            for c in range(2):
                here, other = guess[j, c], guess[j, 1 - c]
                across = roll(other, 4, 0) * (y_low if c == 0 else y_high)
                total = (guess[j - 1, c] + guess[j + 1, c]) + (other + moved[j, c])
                total = total + ((roll(here, 1, 0) * x_low + roll(here, 7, 0) * x_high) + across)
                value = KEEP * here + STEP * total
                after[j, c] = value if j == 0 else value * inside[j]
        guess = after
    return [[[guess[0, c]]] for c in range(2)]


def level_solve(source, level, sweeps_ref, masks):
    wide = 1 << (level - 1)
    if level == LEVELS:
        return coarsest(source, wide, masks)
    size = len(source[0])
    guess = over(lambda s: STEP * s, source)
    repeats = sweeps_ref[level]

    def body(number, state):
        return flat(relax_level(unflat(state, size), source, wide, masks))

    guess = unflat(lax.fori_loop(1, repeats, body, flat(guess)), size)
    coarse = coarser(residue_level(guess, source, wide, masks), wide)
    guess = add_coarse(guess, level_solve(coarse, level + 1, sweeps_ref, masks))
    return unflat(lax.fori_loop(0, repeats, body, flat(guess)), size)


def project_kernel(ext, ids_ref, sweeps_ref, field_ref, *refs):
    source_refs, refs = refs[:4 if ext else 2], refs[4 if ext else 2:]
    if ext:
        result_ref, s_ref, x_ref, p_ref, wrap_ref, edge_ref, win_ref, nat_ref = refs
    else:
        part_ref, over_ref, result_ref, grad_ref, s_ref, x_ref, p_ref, wrap_ref, edge_ref, win_ref, nat_ref = refs
        join(ids_ref, part_ref, over_ref, grad_ref)
    sent = SENT_OWN if ext else SENT
    gx, gy, gz = ids_ref[0], ids_ref[1], ids_ref[2]
    core = lax.rem(gy, 2)
    lane = lanes()
    sub = rows_of()
    x_low = jnp.where(sub % 4 != 0, 1.0, 0.0)
    x_high = jnp.where(sub % 4 != 3, 1.0, 0.0)
    y_low = jnp.where(sub >= 4, 1.0, 0.0)
    y_high = jnp.where(sub < 4, 1.0, 0.0)
    masks = (x_low, x_high, y_low, y_high)
    z_low = jnp.where(lane != 0, 1.0, 0.0)
    z_high = jnp.where(lane != 127, 1.0, 0.0)
    lower = lane < 64

    if ext:
        near_ref, far_ref, near_twin_ref, far_twin_ref = source_refs
        sources = ((near_ref, far_ref, core), (near_twin_ref, far_twin_ref, 1 - core))
    else:
        mine_ref, other_ref = source_refs
        sources = ((mine_ref, mine_ref.at[pl.ds(8 * sent, 8 * sent)], core),
                   (other_ref, other_ref.at[pl.ds(8 * sent, 8 * sent)], 1 - core))

    def both(near_ref, far_ref, i):
        near = near_ref[pl.ds(i, 8, stride=sent), :]
        far = far_ref[pl.ds(i, 8, stride=sent), :]
        if ext:
            return jnp.where(gz == 0, near, far), jnp.where(gz == 0, far, near)
        return near, far

    def halves(near_ref, far_ref, i):
        first, second = both(near_ref, far_ref, i)
        return jnp.where(lower, first, roll(second, 64, 1)), jnp.where(lower, roll(first, 64, 1), second)

    for near_ref, far_ref, slot in sources:
        face0, face1 = both(near_ref, far_ref, 64)
        for x in range(8):
            for y in range(8):
                i = 8 * x + y
                even, odd = halves(near_ref, far_ref, i)
                even = even + jnp.where(lane == 64, roll(face0, (128 - i) % 128, 1), 0.0)
                odd = odd + jnp.where(lane == 63, roll(face1, (63 - i) % 128, 1), 0.0)
                for zi, value in ((0, even), (1, odd)):
                    s_ref[slot, zi, x, y] = value
                    x_ref[slot, zi, x, y] = STEP * value

    def also(slot, zi, x, y, value):
        s_ref[slot, zi, x, y] = s_ref[slot, zi, x, y] + value
        x_ref[slot, zi, x, y] = x_ref[slot, zi, x, y] + STEP * value

    if ext:
        for near_ref, far_ref, slot in sources:
            for at in range(8):
                for zi, value in enumerate(halves(near_ref, far_ref, 72 + at)):
                    also(1 - slot, zi, at, 7, jnp.where(slot == 1, value, roll(value, 4, 0) * y_high))
                for zi, value in enumerate(halves(near_ref, far_ref, 80 + at)):
                    also(1 - slot, zi, at, 0, jnp.where(slot == 0, value, roll(value, 4, 0) * y_low))

    every = [(zi, y) for zi in range(2) for y in range(8)]

    def visit(use):
        for c in range(2):
            first = {at: x_ref[c, at[0], 0, at[1]] for at in every}
            before = {at: roll(x_ref[c, at[0], 7, at[1]], 1, 0) * x_low for at in every}
            for at in every:
                wrap_ref[at[0], at[1]] = roll(first[at], 7, 0) * x_high
            own = first
            for x in range(8):
                after = {at: x_ref[c, at[0], x + 1, at[1]] if x < 7 else wrap_ref[at[0], at[1]] for at in every}
                for zi in range(2):
                    if c == 0:
                        down = roll(x_ref[1, zi, x, 7], 4, 0) * y_low
                        up = x_ref[1, zi, x, 0]
                        edge_ref[zi, x, 0] = own[zi, 7]
                        edge_ref[zi, x, 1] = roll(own[zi, 0], 4, 0) * y_high
                    else:
                        down = edge_ref[zi, x, 0]
                        up = edge_ref[zi, x, 1]
                    for y in range(8):
                        beside = own[1 - zi, y]
                        total = before[zi, y] + after[zi, y] + beside
                        total = total + (own[zi, y - 1] if y > 0 else down) + (own[zi, y + 1] if y < 7 else up)
                        if zi == 0:
                            total = total + roll(beside, 1, 1) * z_low
                        else:
                            total = total + roll(beside, 127, 1) * z_high
                        value = use(c, zi, x, y, own[zi, y], total)
                        if value is not None:
                            x_ref[c, zi, x, y] = value
                before, own = own, after

    def sweep(number, carry):
        visit(lambda c, zi, x, y, own, total: KEEP * own + STEP * (s_ref[c, zi, x, y] + total))
        return carry

    repeats = sweeps_ref[0]

    def cycle(number, carry):
        lax.fori_loop(1, repeats, sweep, 0)
        sums = {}

        def gather(c, zi, x, y, own, total):
            e = s_ref[c, zi, x, y] - 6.0 * own + total
            at = (c, x // 2, y // 2)
            sums[at] = sums[at] + e if at in sums else e

        visit(gather)
        coarse = [[[0.5 * sums[c, x, y] for y in range(4)] for x in range(4)] for c in range(2)]
        coarse = level_solve(coarse, 1, sweeps_ref, masks)
        for c in range(2):
            for zi in range(2):
                for x in range(8):
                    for y in range(8):
                        x_ref[c, zi, x, y] = x_ref[c, zi, x, y] + coarse[c][x // 2][y // 2]
        lax.fori_loop(0, repeats, sweep, 0)

        @pl.when(number == 0)
        def _():
            def restart(c, zi, x, y, own, total):
                p_ref[c, zi, x, y] = own
                rest = s_ref[c, zi, x, y] - 6.0 * own + total
                s_ref[c, zi, x, y] = rest
                return STEP * rest

            visit(restart)

        return carry

    lax.fori_loop(0, CYCLES, cycle, 0)

    x_rows = x_ref.reshape(2 * 2 * 8 * 8 * 8, 128)
    p_rows = p_ref.reshape(2 * 2 * 8 * 8 * 8, 128)
    last_x, last_y = ids_ref[3] - 1, ids_ref[4] - 1
    for wx in range(12):
        dx = -1 if wx < 2 else (1 if wx > 9 else 0)
        xi = (wx - 2) % 8
        bx = gx + dx
        for dy in (-1, 0, 1):
            by = gy + dy
            ok = (bx >= 0) & (bx <= last_x) & (by >= 0) & (by <= last_y)
            ax = jnp.clip(bx, 0, last_x)
            ay = jnp.clip(by, 0, last_y)
            at = (ay // 2) * 4 + ax
            c = lax.rem(ay, 2)
            for zi in range(2):
                start = ((c * 2 + zi) * 8 + xi) * 64 + at
                first = x_rows[pl.ds(start, 8, stride=8), :]
                second = p_rows[pl.ds(start, 8, stride=8), :]
                win_ref[wx * 24 + 8 * (dy + 1):wx * 24 + 8 * (dy + 1) + 8, 128 * zi:128 * zi + 128] = jnp.where(
                    ok, first + second, 0.0)
    source = lax.broadcasted_iota(jnp.int32, (256, 256), 0)
    target = lanes((256, 256))
    depth = 2 * (source % 128) + source // 128
    wanted = jnp.where(target == 255, -1, target) + gz * 128
    pick = jnp.where((depth == wanted) & ((target <= 128) | (target == 255)), 1.0, 0.0)
    nat_ref[...] = exact(win_ref[...], pick)

    size = 16 if ext else 8
    count = 10 if ext else 8
    lane = lanes((count, 128))
    row = rows_of((count, 128))
    for i in range(count):
        x = i - 1 if ext else i
        top = 7 if ext else 8
        base = (x + 2) * 24 + top
        mid = nat_ref[pl.ds(base, count), 0:128]
        tail = nat_ref[pl.ds(base, count), 128:256]
        sx = nat_ref[pl.ds(base + 24, count), 0:128] - nat_ref[pl.ds(base - 24, count), 0:128]
        sy = nat_ref[pl.ds(base + 1, count), 0:128] - nat_ref[pl.ds(base - 1, count), 0:128]
        sz = roll(jnp.where(lane == 0, tail, mid), 127, 1) - roll(jnp.where(lane == 127, tail, mid), 1, 1)
        for k, s in enumerate((sx, sy, sz)):
            if ext:
                value = field_ref[k, i] + 0.5 * s
                good = jnp.where((row == 0) & (gy == 0), 0.0, 1.0)
                good = jnp.where((row == 9) & (gy == last_y), 0.0, good)
                if i == 0:
                    good = good * jnp.where(gx == 0, 0.0, 1.0)
                if i == 9:
                    good = good * jnp.where(gx == last_x, 0.0, 1.0)
                result_ref[k, i] = jnp.zeros((16, 128), F32)
                result_ref[k, i, 0:10, :] = value * good
            else:
                result_ref[k, i] = field_ref[k, i] + 0.5 * s


def backward_kernel(ids_ref, adj_ref, slope_ref, tall_ref, back_ref, grad_ref, over_ref, in_ref, bb_ref, acc_ref):
    gz = ids_ref[2]
    in_ref[144:256, :] = jnp.zeros((112, 256), BF16)
    bb_ref[3 * HIDDEN:DEEP, :] = jnp.zeros((DEEP - 3 * HIDDEN, 256), BF16)
    acc_ref[...] = jnp.zeros(acc_ref.shape, F32)
    for x in range(5):
        for half in range(2):
            col = slice(128 * half, 128 * half + 128)
            for k in range(3):
                high, low = split(adj_ref[k, x + 5 * half])
                in_ref[16 * k:16 * k + 16, col] = high
                in_ref[48 + 16 * k:64 + 16 * k, col] = low
                in_ref[96 + 16 * k:112 + 16 * k, col] = high
        high, low = split(once(back_ref[...], in_ref[...]) * slope_ref[x])
        bb_ref[0:HIDDEN, :] = high
        bb_ref[HIDDEN:2 * HIDDEN, :] = low
        bb_ref[2 * HIDDEN:3 * HIDDEN, :] = high
        total = once(tall_ref[...], bb_ref[...])
        for half in range(2):
            for a in range(3):
                at = x + 5 * half + a
                acc_ref[at] = acc_ref[at] + total[72 * a:72 * a + 72, 128 * half:128 * half + 128]
    lane = lanes()
    row = rows_of()
    for k in range(3):
        packed = jnp.zeros((8, 128), F32)
        for x in range(8):
            low = acc_ref[x + 2, 8 * k:8 * k + 8, :]
            mid = acc_ref[x + 2, 24 + 8 * k:32 + 8 * k, :]
            high = acc_ref[x + 2, 48 + 8 * k:56 + 8 * k, :]
            value = adj_ref[k, x + 1, 1:9, :] + mid
            value = value + jnp.where(lane == 127, 0.0, roll(low, 127, 1))
            grad_ref[k, x] = value + jnp.where(lane == 0, 0.0, roll(high, 1, 1))
            out = jnp.where(gz == 0, high[:, 127:128], low[:, 0:1])
            packed = packed + jnp.where(lane == 8 * x + row, out, 0.0)
        over_ref[k:k + 1, :] = jnp.sum(packed, axis=0, keepdims=True)
    over_ref[3:8, :] = jnp.zeros((5, 128), F32)


def join(ids_ref, part_ref, over_ref, grad_ref):
    gz = ids_ref[2]
    lane = lanes()
    row = rows_of()
    edge = jnp.where(gz == 0, 127, 0)
    for k in range(3):
        for x in range(8):
            column = jnp.sum(jnp.where(lane == 8 * x + row, over_ref[k:k + 1, :], 0.0), axis=1, keepdims=True)
            grad_ref[k, x] = part_ref[k, x] + jnp.where(lane == edge, column, 0.0)


VMEM = pl.BlockSpec(memory_space=pltpu.VMEM)
SMEM = pl.BlockSpec(memory_space=pltpu.SMEM)


def call(kernel, specs, shapes, scratch, *operands, flops=0, size=1 << 20, outs=None):
    return pl.pallas_call(
        kernel,
        in_specs=specs,
        out_specs=outs or [VMEM] * len(shapes),
        out_shape=[s if hasattr(s, "memory_space") else jax.ShapeDtypeStruct(*s) for s in shapes],
        scratch_shapes=scratch,
        compiler_params=pltpu.CompilerParams(vmem_limit_bytes=12 * 2**20),
        cost_estimate=pl.CostEstimate(flops=flops, bytes_accessed=size, transcendentals=0),
    )(*operands)


def trade(velocity, cotangent, axis, dim):
    count = lax.axis_size(axis)
    odd = lax.rem(lax.axis_index(axis), 2) == 1
    size = velocity.shape[dim]

    def cut(array, start, stop):
        return lax.slice_in_dim(array, start, stop, axis=dim)

    other = 3 - dim
    grow = [(0, 0)] * 4
    grow[other] = (0, velocity.shape[other] - cotangent.shape[other])
    low = jnp.concatenate([cut(velocity, 0, 2), jnp.pad(cut(cotangent, 0, 1), grow)], axis=dim)
    high = jnp.concatenate([cut(velocity, size - 2, size), jnp.pad(cut(cotangent, size - 1, size), grow)], axis=dim)
    pairs = [(i, i ^ 1) for i in range(count)]
    gaps = [(i, i + 1) for i in range(1, count - 1, 2)]
    gaps = gaps + [(j, i) for i, j in gaps]
    second = lax.ppermute(jnp.where(odd, high, low), axis, gaps)
    first = lax.ppermute(jnp.where(odd, low, high), axis, pairs)
    below, above = jnp.where(odd, first, second), jnp.where(odd, second, first)
    wide = jnp.concatenate([cut(below, 0, 2), velocity, cut(above, 0, 2)], axis=dim)
    kept = cotangent.shape[other]
    narrow = jnp.concatenate([lax.slice_in_dim(cut(below, 2, 3), 0, kept, axis=other), cotangent,
                              lax.slice_in_dim(cut(above, 2, 3), 0, kept, axis=other)], axis=dim)
    return wide, narrow


def gather_own(rows):
    nx, ny, nz = (lax.axis_size(a) for a in AXES)
    groups = [[(x * ny + 2 * y + c) * nz + z for z in range(nz) for y in range(ny // 2) for x in range(nx)]
              for c in range(2)]
    count = len(groups[0])
    spread = jnp.broadcast_to(rows[None], (count,) + rows.shape)
    mine = lax.all_to_all(spread, AXES, 0, 0, axis_index_groups=groups)
    return mine.reshape(count * rows.shape[0], rows.shape[1])


def twin(mine):
    return lax.ppermute(mine, "gy", [(i, i ^ 1) for i in range(lax.axis_size("gy"))])


def collect(rows):
    x = lax.axis_index("gx")
    odd, upper = lax.rem(x, 2) == 1, x >= 2
    one, two, three = (lax.ppermute(rows, "gx", [(i, i ^ d) for i in range(4)]) for d in (1, 2, 3))
    a, b = jnp.where(odd, one, rows), jnp.where(odd, rows, one)
    c, d = jnp.where(odd, three, two), jnp.where(odd, two, three)
    line = jnp.concatenate([jnp.where(upper, c, a), jnp.where(upper, d, b),
                            jnp.where(upper, a, c), jnp.where(upper, b, d)], axis=0)
    across = lax.ppermute(line, "gy", [(i, i ^ 2) for i in range(4)])
    upper = lax.axis_index("gy") >= 2
    near = jnp.concatenate([jnp.where(upper, across, line), jnp.where(upper, line, across)], axis=0)
    return near, lax.ppermute(near, "gz", [(0, 1), (1, 0)])


def project_rows(ext, ids, sweeps, field, *more):
    block = ((3, 8, 8, 128), F32)
    scratch = [
        pltpu.VMEM((2, 2, 8, 8, 8, 128), F32),
        pltpu.VMEM((2, 2, 8, 8, 8, 128), F32),
        pltpu.VMEM((2, 2, 8, 8, 8, 128), F32),
        pltpu.VMEM((2, 8, 8, 128), F32),
        pltpu.VMEM((2, 8, 2, 8, 128), F32),
        pltpu.VMEM((288, 256), F32),
        pltpu.VMEM((288, 256), F32),
    ]
    return call(functools.partial(project_kernel, ext), [SMEM, SMEM] + [VMEM] * (1 + len(more)),
                [((3, 10, 16, 128), F32)] if ext else [block, block], scratch,
                ids, sweeps, field, *more, flops=6 * 10**9)


def weights(first_weight, first_bias, second_weight):
    return call(
        weights_kernel, [VMEM] * 3,
        [((2 * HIDDEN, REACH), BF16), ((216, DEEP), BF16), ((3 * WIDTH, 128), F32), ((HIDDEN, 256), BF16)],
        [pltpu.VMEM((256, 128), F32)], first_weight, first_bias[None], second_weight, flops=10**9)


def forward(ids, second_bias, near, face, wide, out):
    return call(
        forward_kernel, [SMEM, SMEM] + [VMEM] * 4,
        [((3, 8, 8, 128), F32), pltpu.HBM((5, HIDDEN, 256), F32), ((SENT, 128), F32)],
        [pltpu.VMEM((ROWS, 128), F32), pltpu.VMEM((4 * PLANE + REACH, 256), BF16), pltpu.VMEM((HIDDEN, 256), F32),
         pltpu.VMEM((3, 10, 16, 128), F32), pltpu.VMEM((64, 128), F32), pltpu.VMEM((5, HIDDEN, 256), F32),
         pltpu.SemaphoreType.DMA((5,))],
        ids, second_bias, near, face, wide, out, flops=4 * 10**9,
        outs=[VMEM, pl.BlockSpec(memory_space=pltpu.HBM), VMEM])


def gathered(velocity, cotangent, first_weight, first_bias, second_weight, second_bias, sweeps):
    swap = [(0, 1), (1, 0)]
    ids = jnp.stack([lax.axis_index("gx"), lax.axis_index("gy"), lax.axis_index("gz"),
                     jnp.int32(lax.axis_size("gx")), jnp.int32(lax.axis_size("gy"))]).astype(jnp.int32)
    near, cot_near = trade(velocity, cotangent, "gx", 1)
    cot_rows = call(own_rows_kernel, [VMEM], [((SENT_OWN, 128), F32)], [pltpu.VMEM((80, 128), F32)], cot_near)[0]
    cot_own, cot_far = collect(cot_rows)
    near, cot_near = trade(near, cot_near, "gy", 2)
    face = jnp.where(ids[2] == 0, near[:, :, :, 127], near[:, :, :, 0])
    face = lax.ppermute(face, "gz", swap)
    wide, tall, out, back = weights(first_weight, first_bias, second_weight)
    closed, slope, rows = forward(ids, second_bias, near, face, wide, out)
    mine = gather_own(rows)
    cot_far, rows = lax.optimization_barrier((cot_far, rows))
    adjoint = project_rows(True, ids, sweeps, cot_near, cot_own, cot_far, twin(cot_own), twin(cot_far))[0]
    part, over_rows = call(
        backward_kernel, [SMEM] + [VMEM] * 4, [((3, 8, 8, 128), F32), ((8, 128), F32)],
        [pltpu.VMEM((256, 256), BF16), pltpu.VMEM((DEEP, 256), BF16), pltpu.VMEM((12, 72, 128), F32)],
        ids, adjoint, slope, tall, back, flops=10**6)
    over_rows = lax.ppermute(over_rows, "gz", swap)
    mine, part, over_rows = lax.optimization_barrier((mine, part, over_rows))
    updated, grad = project_rows(False, ids, sweeps, closed, mine, twin(mine), part, over_rows)
    return updated, grad


def one_gather(velocity, first_weight):
    nx, ny, nz = (lax.axis_size(a) for a in AXES)
    return (velocity.shape == (3, 8, 8, 128) and nx == 4 and ny == 4 and nz == 2
            and first_weight.shape == (WIDTH, 81))


def dispatch(velocity, cotangent, first_weight, first_bias, second_weight, second_bias, sweeps):
    path = gathered if one_gather(velocity, first_weight) else shards
    return path(velocity, cotangent, first_weight, first_bias, second_weight, second_bias, sweeps)


def solution(mesh):
    return jax.shard_map(
        dispatch,
        mesh=mesh,
        in_specs=(P(None, "gx", "gy", "gz"), P(None, "gx", "gy", "gz"), P(), P(), P(), P(), P()),
        out_specs=(P(None, "gx", "gy", "gz"), P(None, "gx", "gy", "gz")),
        check_vma=False,
    )
```

```python
import functools

import jax
import jax.numpy as jnp
from jax import lax
from jax.experimental import pallas as pl
from jax.experimental.pallas import tpu as pltpu
from jax.sharding import PartitionSpec as P

LEVELS = 3
COARSE_SWEEPS = 6
CYCLES = 2


OMEGA = 0.8


def with_halo(block, sides, width):
    for axis, dim in sides:
        count = lax.axis_size(axis)
        forward = [(i, i + 1) for i in range(count - 1)]
        backward = [(target, source) for source, target in forward]
        low = lax.ppermute(
            lax.slice_in_dim(block, block.shape[dim] - width, None, axis=dim), axis, forward
        )
        high = lax.ppermute(lax.slice_in_dim(block, 0, width, axis=dim), axis, backward)
        block = jnp.concatenate([low, block, high], axis=dim)
    return block


def stencil_features(region):
    span_y = region.shape[2] - 2
    span_z = region.shape[3] - 2
    shifted = [
        region[:, first, second : second + span_y, third : third + span_z]
        for first in range(3)
        for second in range(3)
        for third in range(3)
    ]
    return jnp.stack(shifted).reshape(27 * region.shape[0], span_y * span_z)


def six_point(field, padded):
    beside = padded[:, 2:, 1:-1, 1:-1] + padded[:, :-2, 1:-1, 1:-1]
    beside = beside + padded[:, 1:-1, 2:, 1:-1] + padded[:, 1:-1, :-2, 1:-1]
    beside = beside + padded[:, 1:-1, 1:-1, 2:] + padded[:, 1:-1, 1:-1, :-2]
    return 6.0 * field - beside


def near_faces(field):
    return with_halo(field, (("gx", 1), ("gy", 2), ("gz", 3)), 1)


def laplace_shared(field):
    return six_point(field, near_faces(field))


def relax(guess, source):
    return guess + OMEGA * (source - laplace_shared(guess)) / 6.0


def restrict(residue):
    batch, size_x, size_y, size_z = residue.shape
    folded = residue.reshape(batch, size_x // 2, 2, size_y // 2, 2, size_z // 2, 2)
    return 0.5 * folded.sum(axis=(2, 4, 6))


def prolong(coarse):
    return jnp.repeat(jnp.repeat(jnp.repeat(coarse, 2, axis=1), 2, axis=2), 2, axis=3)


def coarse_spread(source, sweeps):
    guess = OMEGA * source / 6.0
    return lax.fori_loop(1, COARSE_SWEEPS, lambda number, state: relax(state, source), guess)


def vcycle(source, sweeps, level, coarse_solve, bottom):
    if level == bottom:
        return coarse_solve(source, sweeps)
    repeats = sweeps[level]
    guess = OMEGA * source / 6.0
    guess = lax.fori_loop(1, repeats, lambda number, state: relax(state, source), guess)
    residue = source - laplace_shared(guess)
    guess = guess + prolong(vcycle(restrict(residue), sweeps, level + 1, coarse_solve, bottom))
    return lax.fori_loop(0, repeats, lambda number, state: relax(state, source), guess)


def divergence(padded):
    total = padded[:, 0, 2:, 1:-1, 1:-1] - padded[:, 0, :-2, 1:-1, 1:-1]
    total = total + padded[:, 1, 1:-1, 2:, 1:-1] - padded[:, 1, 1:-1, :-2, 1:-1]
    total = total + padded[:, 2, 1:-1, 1:-1, 2:] - padded[:, 2, 1:-1, 1:-1, :-2]
    return 0.5 * total


def gradient(padded):
    return 0.5 * jnp.stack(
        [
            padded[:, 2:, 1:-1, 1:-1] - padded[:, :-2, 1:-1, 1:-1],
            padded[:, 1:-1, 2:, 1:-1] - padded[:, 1:-1, :-2, 1:-1],
            padded[:, 1:-1, 1:-1, 2:] - padded[:, 1:-1, 1:-1, :-2],
        ],
        axis=1,
    )


def project(fields, sweeps, coarse_solve, bottom):
    batch, comps, size_x, size_y, size_z = fields.shape
    padded = near_faces(fields.reshape(batch * comps, size_x, size_y, size_z))
    padded = padded.reshape(batch, comps, size_x + 2, size_y + 2, size_z + 2)
    source = divergence(padded)
    pressure = vcycle(source, sweeps, 0, coarse_solve, bottom)
    pressure = pressure + vcycle(source - laplace_shared(pressure), sweeps, 0, coarse_solve, bottom)
    return fields + gradient(near_faces(pressure))


def corrections(near, first_weight, first_bias, second_weight, second_bias, planes):
    span_y = near.shape[2] - 2
    span_z = near.shape[3] - 2

    def corrections_one_plane(index):
        region = lax.dynamic_slice_in_dim(near, index, 3, 1)
        feats = stencil_features(region)
        hidden = jax.nn.silu(
            jnp.dot(first_weight, feats, precision=lax.Precision.HIGHEST) + first_bias[:, None]
        )
        return (
            jnp.dot(second_weight, hidden, precision=lax.Precision.HIGHEST) + second_bias[:, None]
        )

    result = lax.map(corrections_one_plane, jnp.arange(planes, dtype=jnp.int32))
    return result.reshape(planes, 3, span_y, span_z).transpose(1, 0, 2, 3)


def back_planes(wide, cot_pad, first_weight, first_bias, second_weight, planes):
    span_y = cot_pad.shape[2] - 2
    span_z = cot_pad.shape[3] - 2

    def back_one_plane(index):
        region = lax.dynamic_slice_in_dim(wide, index, 3, 1)
        feats = stencil_features(region)
        pre = jnp.dot(first_weight, feats, precision=lax.Precision.HIGHEST) + first_bias[:, None]
        sig = jax.nn.sigmoid(pre)
        slope = sig * (1.0 + pre * (1.0 - sig))
        incoming = lax.dynamic_index_in_dim(cot_pad, index, 1, keepdims=False).reshape(3, -1)
        back = jnp.dot(second_weight.T, incoming, precision=lax.Precision.HIGHEST) * slope
        spread = jnp.dot(first_weight.T, back, precision=lax.Precision.HIGHEST)
        spread = spread.reshape(3, 3, 3, 3, span_y + 2, span_z + 2)
        parts = []
        for first in range(3):
            total = jnp.zeros((3, span_y, span_z), jnp.float32)
            for second in range(3):
                for third in range(3):
                    total = (
                        total
                        + spread[
                            first,
                            second,
                            third,
                            :,
                            2 - second : 2 - second + span_y,
                            2 - third : 2 - third + span_z,
                        ]
                    )
            parts.append(total)
        return jnp.stack(parts)

    pieces = lax.map(back_one_plane, jnp.arange(planes + 2, dtype=jnp.int32))
    return pieces[:-2, 2] + pieces[1:-1, 1] + pieces[2:, 0]


def shards(velocity, cotangent, first_weight, first_bias, second_weight, second_bias, sweeps):
    planes = velocity.shape[1]
    near = with_halo(velocity, (("gx", 1), ("gy", 2), ("gz", 3)), 1)
    coarse_solve, bottom = (coarse_spread, LEVELS)
    closed = velocity + corrections(
        near, first_weight, first_bias, second_weight, second_bias, planes
    )
    updated = project(closed[None], sweeps, coarse_solve, bottom)[0]
    adjoint_closed = project(cotangent[None], sweeps, coarse_solve, bottom)[0]
    wide = with_halo(velocity, (("gx", 1), ("gy", 2), ("gz", 3)), 2)
    cot_pad = with_halo(adjoint_closed, (("gx", 1), ("gy", 2), ("gz", 3)), 1)
    summed = back_planes(wide, cot_pad, first_weight, first_bias, second_weight, planes)
    grad_velocity = adjoint_closed + summed.transpose(1, 0, 2, 3)
    return (updated, grad_velocity)


AXES = ("gx", "gy", "gz")
STEP = OMEGA / 6.0
KEEP = 1.0 - OMEGA
WIDTH = 32
SPAN = 10
ROWS = 112
PLANE = 2 * ROWS
REACH = 768
DEEP = 1024
HIDDEN = SPAN * WIDTH
SENT = 72
SENT_OWN = 88
F32 = jnp.float32
BF16 = jnp.bfloat16


def roll(value, shift, axis):
    return pltpu.roll(value, shift, axis)


def lanes(shape=(8, 128)):
    return lax.broadcasted_iota(jnp.int32, shape, len(shape) - 1)


def rows_of(shape=(8, 128)):
    return lax.broadcasted_iota(jnp.int32, shape, len(shape) - 2)


def split(value):
    high = value.astype(BF16)
    return high, (value - high.astype(F32)).astype(BF16)


def exact(left, right):
    high = left.astype(BF16)
    rest = left - high.astype(F32)
    middle, low = split(rest)
    right = right.astype(BF16)
    return (once(high, right) + once(middle, right)) + once(low, right)


def once(left, right):
    return jnp.dot(left, right, preferred_element_type=F32)


def one_hot(condition):
    return jnp.where(condition, 1.0, 0.0).astype(BF16)


def column_of(line, size):
    square = (size, size)
    return jnp.sum(jnp.where(rows_of(square) == lanes(square), line, 0.0), axis=1, keepdims=True)


def weights_kernel(first_hbm, bias_hbm, second_hbm, wide_ref, tall_ref, out_ref, back_ref,
                   pad_ref, first_ref, bias_ref, second_ref, sems):
    pairs = ((first_hbm, first_ref), (bias_hbm, bias_ref), (second_hbm, second_ref))
    copies = [pltpu.make_async_copy(source, target, sems.at[i]) for i, (source, target) in enumerate(pairs)]
    for copy in copies:
        copy.start()
    for copy in copies:
        copy.wait()
    count = first_ref.shape[1]
    pad_ref[...] = jnp.zeros((256, 128), F32)
    pad_ref[0:WIDTH, 0:count] = first_ref[...]
    pad_ref[128:131, 0:WIDTH] = second_ref[...]
    first = pad_ref[0:128, :]
    second = pad_ref[128:256, :]
    high, low = split(first[0:WIDTH])
    column = lanes((1, REACH))
    rest = column % ROWS
    real = (rest < 108) & (column < 3 * PLANE)
    height = jnp.where(real, rest % 12, -1)
    feature = jnp.where(real, 27 * (column // PLANE) + rest // 12, -1000)
    upper = (column % PLANE) < ROWS
    bias_high, bias_low = split(column_of(bias_ref[...], WIDTH))
    totals = [jnp.where(column == 108, part.astype(F32), 0.0) for part in (bias_high, bias_low)]
    row = rows_of((128, REACH))
    parts = []
    for b in range(3):
        chosen = one_hot(row - 9 * b == feature)
        parts.append((once(high, chosen), jnp.where(upper, once(low, chosen), 0.0)))
    for y in range(SPAN):
        for half in range(2):
            total = totals[half]
            for b in range(3):
                total = total + jnp.where(height == y + b, parts[b][half], 0.0)
            wide_ref[half * HIDDEN + y * WIDTH:half * HIDDEN + (y + 1) * WIDTH, :] = total.astype(BF16)
    high, low = split(first.T)
    column = lanes((1, DEEP))
    row = rows_of((128, DEEP))
    place = (column % HIDDEN) // WIDTH
    term = column // HIDDEN
    tiled = one_hot((row == column % WIDTH) & (column < 3 * HIDDEN))
    copies = jnp.where(term == 2, once(low, tiled), once(high, tiled)).astype(BF16)
    line = lax.broadcasted_iota(jnp.int32, (216, 128), 0)
    lane = lanes((216, 128))
    tops = line[:, 0:1] % 8 + 2
    total = jnp.zeros((216, DEEP), F32)
    for b in range(3):
        lift = one_hot(lane - 9 * b == 27 * (line // 72) + (line % 72) // 8)
        total = total + jnp.where(tops - b == place, once(lift, copies), 0.0)
    tall_ref[...] = total.astype(BF16)
    for k in range(3):
        line = second[k:k + 1, 0:WIDTH]
        out_ref[WIDTH * k:WIDTH * (k + 1), :] = jnp.broadcast_to(column_of(line, WIDTH), (WIDTH, 128))
    high, low = split(second.T[0:WIDTH])
    column = lanes((1, 256))
    row = rows_of((128, 256))
    inner = one_hot((row == (column % 48) // 16) & (column < 144))
    copies = jnp.where(column // 48 == 2, once(low, inner), once(high, inner))
    for y in range(SPAN):
        back_ref[y * WIDTH:(y + 1) * WIDTH, :] = jnp.where(column % 16 == y, copies, 0.0).astype(BF16)


def depth_order():
    first = lax.broadcasted_iota(jnp.int32, (128, 128), 0)
    return jnp.where((first % 2) * 64 + first // 2 == lanes((128, 128)), 1.0, 0.0)


def send_rows(get, flat_ref, sent_ref):
    lane = lanes()
    row = rows_of()
    faces = jnp.zeros((8, 128), F32)
    for x in range(8):
        up = get(2, x + 1, 1)
        value = get(0, x + 2, 1) - get(0, x, 1) + get(1, x + 1, 2) - get(1, x + 1, 0)
        value = value + jnp.where(lane == 127, 0.0, roll(up, 127, 1)) - jnp.where(lane == 0, 0.0, roll(up, 1, 1))
        flat_ref[8 * x:8 * x + 8, :] = 0.5 * value
        faces = faces + jnp.where(lane == 8 * x + row, 0.5 * up[:, 0:1], 0.0)
        faces = faces - jnp.where(lane == 64 + 8 * x + row, 0.5 * up[:, 127:128], 0.0)
    sent_ref[0:64, :] = exact(flat_ref[...], depth_order())
    sent_ref[64:72, :] = jnp.where(row == 0, jnp.sum(faces, axis=0, keepdims=True), 0.0)


def own_rows_kernel(field_ref, sent_ref, flat_ref):
    lane = lanes()
    row = rows_of()
    faces = jnp.zeros((8, 128), F32)
    for x in range(8):
        along = field_ref[1, x + 1]
        up = field_ref[2, x + 1]
        value = jnp.where(row == 7, 0.0, roll(along, 7, 0)) - jnp.where(row == 0, 0.0, roll(along, 1, 0))
        value = value + jnp.where(lane == 127, 0.0, roll(up, 127, 1)) - jnp.where(lane == 0, 0.0, roll(up, 1, 1))
        flat_ref[8 * x:8 * x + 8, :] = 0.5 * (value + field_ref[0, x + 2] - field_ref[0, x])
        flat_ref[64 + x:65 + x, :] = 0.5 * along[0:1, :]
        flat_ref[72 + x:73 + x, :] = -0.5 * along[7:8, :]
        faces = faces + jnp.where(lane == 8 * x + row, 0.5 * up[:, 0:1], 0.0)
        faces = faces - jnp.where(lane == 64 + 8 * x + row, 0.5 * up[:, 127:128], 0.0)
    turned = exact(flat_ref[...], depth_order())
    sent_ref[0:64, :] = turned[0:64]
    sent_ref[64:72, :] = jnp.where(row == 0, jnp.sum(faces, axis=0, keepdims=True), 0.0)
    sent_ref[72:88, :] = turned[64:80]


def fold(values):
    row = rows_of()
    low = row < 4
    values = [jnp.where(low, a, b) + roll(jnp.where(low, b, a), 4, 0) for a, b in zip(values[:4], values[4:])]
    for step in (2, 1):
        low = (row // step) % 2 == 0
        values = [jnp.where(low, a + roll(a, 8 - step, 0), b + roll(b, step, 0))
                  for a, b in zip(values[:step], values[step:])]
    return values[0]


def forward_kernel(ids_ref, bias_ref, ext_ref, col_ref, wide_ref, out_ref, closed_ref, slope_ref, sent_ref,
                   plane_ref, feat_ref, hid_ref, ce_ref, flat_ref, kept_ref, sems, rows_ref, row_sems):
    gx, gy, gz = ids_ref[0], ids_ref[1], ids_ref[2]
    low_side = jnp.where(gz == 0, 1.0, 0.0)
    high_side = 1.0 - low_side
    lane = lanes((12, 128))
    pad_row = rows_of((8, 128))
    plane_ref[104:112, :] = jnp.where(pad_row == 4, 1.0, 0.0)
    feat_ref[7 * PLANE:, :] = jnp.zeros((REACH - 3 * PLANE, 256), BF16)
    corner = rows_of((12, 12)) == lanes((12, 12))
    beyond = [[jnp.sum(jnp.where(corner, col_ref[k, at:at + 1, :], 0.0), axis=1, keepdims=True) for at in range(12)]
              for k in range(3)]
    for step in range(7):
        for half in range(2):
            at = step + 5 * half
            for k in range(3):
                here = ext_ref[k, at]
                below = jnp.where(lane == 0, beyond[k][at] * high_side, roll(here, 1, 1))
                above = jnp.where(lane == 127, beyond[k][at] * low_side, roll(here, 127, 1))
                for c, piece in ((0, below), (1, here), (2, above)):
                    plane_ref[pl.ds((c * 3 + k) * 12, 12), :] = piece
            high, low = split(plane_ref[...])
            col = slice(128 * half, 128 * half + 128)
            feat_ref[step * PLANE:step * PLANE + ROWS, col] = high
            feat_ref[step * PLANE + ROWS:step * PLANE + 2 * ROWS, col] = low
    row = rows_of((10, 128))
    inside = jnp.where((row == 0) & (gy == 0), 0.0, 1.0)
    inside = jnp.where((row == 9) & (gy == ids_ref[4] - 1), 0.0, inside)
    for x in range(5):
        both = once(wide_ref[...], feat_ref[x * PLANE:x * PLANE + REACH, :])
        pre = both[0:HIDDEN] + both[HIDDEN:]
        sig = 0.5 * jnp.tanh(0.5 * pre) + 0.5
        kept_ref[x] = sig * (1.0 + pre * (1.0 - sig))
        pltpu.make_async_copy(kept_ref.at[x], slope_ref.at[x], sems.at[x]).start()
        hid_ref[...] = pre * sig
        for half in range(2):
            e = x + 5 * half
            mask = inside
            if e == 0:
                mask = inside * jnp.where(gx == 0, 0.0, 1.0)
            if e == 9:
                mask = inside * jnp.where(gx == ids_ref[3] - 1, 0.0, 1.0)
            sums = []
            for y in range(SPAN):
                here = [hid_ref[y * WIDTH + 8 * i:y * WIDTH + 8 * i + 8, 128 * half:128 * half + 128] for i in range(4)]
                for k in range(3):
                    terms = [out_ref[WIDTH * k + 8 * i:WIDTH * k + 8 * i + 8, :] * here[i] for i in range(4)]
                    sums.append((terms[0] + terms[1]) + (terms[2] + terms[3]))
            rest = fold([sums[3 * y + k] for k in range(3) for y in (8, 9)] + [sums[0]] * 2)
            for k in range(3):
                ce_ref[k, e, 0:8, :] = fold([sums[3 * y + k] for y in range(8)])
                ce_ref[k, e, 8:10, :] = rest[2 * k:2 * k + 2, :]
                ce_ref[k, e, 0:10, :] = (ce_ref[k, e, 0:10, :] + bias_ref[k] + ext_ref[k, e + 1, 1:11, :]) * mask
    for k in range(3):
        for x in range(8):
            closed_ref[k, x] = ce_ref[k, x + 1, 1:9, :]
    send_rows(lambda k, x, y: ce_ref[k, x, pl.ds(y, 8), :], flat_ref, rows_ref)
    copies = [pltpu.make_async_copy(rows_ref, sent_ref.at[i], row_sems.at[i]) for i in range(sent_ref.shape[0])]
    for copy in copies:
        copy.start()
    for copy in copies:
        copy.wait()
    for x in range(5):
        pltpu.make_async_copy(kept_ref.at[x], slope_ref.at[x], sems.at[x]).wait()


def around(grid, wide, masks):
    (x_low, x_high, y_low, y_high) = masks
    lane = lanes()
    size = len(grid[0])
    result = []
    for c in range(2):
        plane = []
        for x in range(size):
            line = []
            for y in range(size):
                here = grid[c][x][y]
                total = jnp.where(lane >= wide, roll(here, wide, 1), 0.0)
                total = total + jnp.where(lane < 128 - wide, roll(here, 128 - wide, 1), 0.0)
                total = total + (grid[c][x - 1][y] if x > 0 else roll(grid[c][size - 1][y], 1, 0) * x_low)
                total = total + (grid[c][x + 1][y] if x < size - 1 else roll(grid[c][0][y], 7, 0) * x_high)
                if y > 0:
                    total = total + grid[c][x][y - 1]
                else:
                    edge = grid[1 - c][x][size - 1]
                    total = total + (edge if c == 1 else roll(edge, 4, 0) * y_low)
                if y < size - 1:
                    total = total + grid[c][x][y + 1]
                else:
                    edge = grid[1 - c][x][0]
                    total = total + (edge if c == 0 else roll(edge, 4, 0) * y_high)
                line.append(total)
            plane.append(line)
        result.append(plane)
    return result


def over(function, *grids):
    size = len(grids[0][0])
    return [[[function(*(g[c][x][y] for g in grids)) for y in range(size)] for x in range(size)] for c in range(2)]


def flat(grid):
    return tuple(v for plane in grid for line in plane for v in line)


def unflat(values, size):
    values = list(values)
    return [[[values[(c * size + x) * size + y] for y in range(size)] for x in range(size)] for c in range(2)]


def relax_level(guess, source, wide, masks):
    return over(lambda g, s, n: KEEP * g + STEP * (s + n), guess, source, around(guess, wide, masks))


def residue_level(guess, source, wide, masks):
    return over(lambda g, s, n: s - 6.0 * g + n, guess, source, around(guess, wide, masks))


def coarser(grid, wide):
    lane = lanes()
    size = len(grid[0]) // 2
    even = (lane // wide) % 2 == 0
    result = []
    for c in range(2):
        plane = []
        for x in range(size):
            line = []
            for y in range(size):
                t = grid[c][2 * x][2 * y] + grid[c][2 * x][2 * y + 1]
                t = t + grid[c][2 * x + 1][2 * y] + grid[c][2 * x + 1][2 * y + 1]
                line.append(0.5 * (t + jnp.where(even, roll(t, 128 - wide, 1), roll(t, wide, 1))))
            plane.append(line)
        result.append(plane)
    return result


def add_coarse(grid, coarse):
    size = len(grid[0])
    return [[[grid[c][x][y] + coarse[c][x // 2][y // 2] for y in range(size)] for x in range(size)] for c in range(2)]


def coarsest(source, wide, masks):
    (x_low, x_high, y_low, y_high) = masks
    lane = lanes()
    reach = COARSE_SWEEPS - 1
    moved, inside = {}, {}
    for j in range(-reach, reach + 1):
        at = lane + wide * j
        inside[j] = jnp.where((at >= 0) & (at < 128), 1.0, 0.0)
        for c in range(2):
            here = source[c][0][0]
            moved[j, c] = here if j == 0 else roll(here, (-wide * j) % 128, 1) * inside[j]
    guess = {at: STEP * value for at, value in moved.items()}
    for k in range(1, reach + 1):
        after = {}
        for j in range(k - reach, reach - k + 1):
            for c in range(2):
                here, other = guess[j, c], guess[j, 1 - c]
                across = roll(other, 4, 0) * (y_low if c == 0 else y_high)
                total = (guess[j - 1, c] + guess[j + 1, c]) + (other + moved[j, c])
                total = total + ((roll(here, 1, 0) * x_low + roll(here, 7, 0) * x_high) + across)
                value = KEEP * here + STEP * total
                after[j, c] = value if j == 0 else value * inside[j]
        guess = after
    return [[[guess[0, c]]] for c in range(2)]


def level_solve(source, level, sweeps_ref, masks):
    wide = 1 << (level - 1)
    if level == LEVELS:
        return coarsest(source, wide, masks)
    size = len(source[0])
    guess = over(lambda s: STEP * s, source)
    repeats = sweeps_ref[level]

    def body(number, state):
        return flat(relax_level(unflat(state, size), source, wide, masks))

    guess = unflat(lax.fori_loop(1, repeats, body, flat(guess)), size)
    coarse = coarser(residue_level(guess, source, wide, masks), wide)
    guess = add_coarse(guess, level_solve(coarse, level + 1, sweeps_ref, masks))
    return unflat(lax.fori_loop(0, repeats, body, flat(guess)), size)


def project_kernel(ext, ids_ref, sweeps_ref, field_ref, *refs):
    source_refs, refs = refs[:4 if ext else 2], refs[4 if ext else 2:]
    if ext:
        result_ref, s_ref, x_ref, p_ref, wrap_ref, edge_ref, c_ref, win_ref, nat_ref = refs
    else:
        part_ref, over_ref, result_ref, grad_ref, s_ref, x_ref, p_ref, wrap_ref, edge_ref, c_ref, win_ref, nat_ref = refs
        join(ids_ref, part_ref, over_ref, grad_ref)
    sent = SENT_OWN if ext else SENT
    gx, gy, gz = ids_ref[0], ids_ref[1], ids_ref[2]
    core = lax.rem(gy, 2)
    lane = lanes()
    sub = rows_of()
    x_low = jnp.where(sub % 4 != 0, 1.0, 0.0)
    x_high = jnp.where(sub % 4 != 3, 1.0, 0.0)
    y_low = jnp.where(sub >= 4, 1.0, 0.0)
    y_high = jnp.where(sub < 4, 1.0, 0.0)
    masks = (x_low, x_high, y_low, y_high)
    z_low = jnp.where(lane != 0, 1.0, 0.0)
    z_high = jnp.where(lane != 127, 1.0, 0.0)
    lower = lane < 64

    if ext:
        near_ref, far_ref, near_twin_ref, far_twin_ref = source_refs
        sources = ((near_ref, far_ref, core), (near_twin_ref, far_twin_ref, 1 - core))
    else:
        mine_ref, other_ref = source_refs
        sources = ((mine_ref, mine_ref.at[pl.ds(8 * sent, 8 * sent)], core),
                   (other_ref, other_ref.at[pl.ds(8 * sent, 8 * sent)], 1 - core))

    def both(near_ref, far_ref, i):
        near = near_ref[pl.ds(i, 8, stride=sent), :]
        far = far_ref[pl.ds(i, 8, stride=sent), :]
        if ext:
            return jnp.where(gz == 0, near, far), jnp.where(gz == 0, far, near)
        return near, far

    def halves(near_ref, far_ref, i):
        first, second = both(near_ref, far_ref, i)
        return jnp.where(lower, first, roll(second, 64, 1)), jnp.where(lower, roll(first, 64, 1), second)

    for near_ref, far_ref, slot in sources:
        face0, face1 = both(near_ref, far_ref, 64)
        for x in range(8):
            for y in range(8):
                i = 8 * x + y
                even, odd = halves(near_ref, far_ref, i)
                even = even + jnp.where(lane == 64, roll(face0, (128 - i) % 128, 1), 0.0)
                odd = odd + jnp.where(lane == 63, roll(face1, (63 - i) % 128, 1), 0.0)
                for zi, value in ((0, even), (1, odd)):
                    s_ref[slot, zi, x, y] = value
                    x_ref[slot, zi, x, y] = STEP * value

    def also(slot, zi, x, y, value):
        s_ref[slot, zi, x, y] = s_ref[slot, zi, x, y] + value
        x_ref[slot, zi, x, y] = x_ref[slot, zi, x, y] + STEP * value

    if ext:
        for near_ref, far_ref, slot in sources:
            for at in range(8):
                for zi, value in enumerate(halves(near_ref, far_ref, 72 + at)):
                    also(1 - slot, zi, at, 7, jnp.where(slot == 1, value, roll(value, 4, 0) * y_high))
                for zi, value in enumerate(halves(near_ref, far_ref, 80 + at)):
                    also(1 - slot, zi, at, 0, jnp.where(slot == 0, value, roll(value, 4, 0) * y_low))

    every = [(zi, y) for zi in range(2) for y in range(8)]

    def visit(use, coarse=None):
        def load(c, zi, x, y):
            value = x_ref[c, zi, x, y]
            return value if coarse is None else value + coarse[c, x // 2, y // 2]

        for c in range(2):
            first = {at: load(c, at[0], 0, at[1]) for at in every}
            before = {at: roll(load(c, at[0], 7, at[1]), 1, 0) * x_low for at in every}
            for at in every:
                wrap_ref[at[0], at[1]] = roll(first[at], 7, 0) * x_high
            own = first
            for x in range(8):
                after = {at: load(c, at[0], x + 1, at[1]) if x < 7 else wrap_ref[at[0], at[1]] for at in every}
                for zi in range(2):
                    if c == 0:
                        down = roll(load(1, zi, x, 7), 4, 0) * y_low
                        up = load(1, zi, x, 0)
                        edge_ref[zi, x, 0] = own[zi, 7]
                        edge_ref[zi, x, 1] = roll(own[zi, 0], 4, 0) * y_high
                    else:
                        down = edge_ref[zi, x, 0]
                        up = edge_ref[zi, x, 1]
                    for y in range(8):
                        beside = own[1 - zi, y]
                        total = before[zi, y] + after[zi, y] + beside
                        total = total + (own[zi, y - 1] if y > 0 else down) + (own[zi, y + 1] if y < 7 else up)
                        if zi == 0:
                            total = total + roll(beside, 1, 1) * z_low
                        else:
                            total = total + roll(beside, 127, 1) * z_high
                        value = use(c, zi, x, y, own[zi, y], total)
                        if value is not None:
                            x_ref[c, zi, x, y] = value
                before, own = own, after

    def relaxed(c, zi, x, y, own, total):
        return KEEP * own + STEP * (s_ref[c, zi, x, y] + total)

    def sweep(number, carry):
        visit(relaxed)
        return carry

    repeats = sweeps_ref[0]

    def cycle(number, carry):
        lax.fori_loop(1, repeats, sweep, 0)
        sums = {}

        def gather(c, zi, x, y, own, total):
            e = s_ref[c, zi, x, y] - 6.0 * own + total
            at = (c, x // 2, y // 2)
            sums[at] = sums[at] + e if at in sums else e

        visit(gather)
        coarse = [[[0.5 * sums[c, x, y] for y in range(4)] for x in range(4)] for c in range(2)]
        coarse = level_solve(coarse, 1, sweeps_ref, masks)
        for c in range(2):
            for x in range(4):
                for y in range(4):
                    c_ref[c, x, y] = coarse[c][x][y]
        visit(relaxed, c_ref)
        lax.fori_loop(1, repeats, sweep, 0)

        @pl.when(number == 0)
        def _():
            def restart(c, zi, x, y, own, total):
                p_ref[c, zi, x, y] = own
                rest = s_ref[c, zi, x, y] - 6.0 * own + total
                s_ref[c, zi, x, y] = rest
                return STEP * rest

            visit(restart)

        return carry

    lax.fori_loop(0, CYCLES, cycle, 0)

    x_rows = x_ref.reshape(2 * 2 * 8 * 8 * 8, 128)
    p_rows = p_ref.reshape(2 * 2 * 8 * 8 * 8, 128)
    last_x, last_y = ids_ref[3] - 1, ids_ref[4] - 1
    for wx in range(12):
        dx = -1 if wx < 2 else (1 if wx > 9 else 0)
        xi = (wx - 2) % 8
        bx = gx + dx
        for dy in (-1, 0, 1):
            by = gy + dy
            ok = (bx >= 0) & (bx <= last_x) & (by >= 0) & (by <= last_y)
            ax = jnp.clip(bx, 0, last_x)
            ay = jnp.clip(by, 0, last_y)
            at = (ay // 2) * 4 + ax
            c = lax.rem(ay, 2)
            for zi in range(2):
                start = ((c * 2 + zi) * 8 + xi) * 64 + at
                first = x_rows[pl.ds(start, 8, stride=8), :]
                second = p_rows[pl.ds(start, 8, stride=8), :]
                win_ref[wx * 24 + 8 * (dy + 1):wx * 24 + 8 * (dy + 1) + 8, 128 * zi:128 * zi + 128] = jnp.where(
                    ok, first + second, 0.0)
    source = lax.broadcasted_iota(jnp.int32, (256, 256), 0)
    target = lanes((256, 256))
    depth = 2 * (source % 128) + source // 128
    wanted = jnp.where(target == 255, -1, target) + gz * 128
    pick = jnp.where((depth == wanted) & ((target <= 128) | (target == 255)), 1.0, 0.0)
    nat_ref[...] = exact(win_ref[...], pick)

    size = 16 if ext else 8
    count = 10 if ext else 8
    lane = lanes((count, 128))
    row = rows_of((count, 128))
    for i in range(count):
        x = i - 1 if ext else i
        top = 7 if ext else 8
        base = (x + 2) * 24 + top
        mid = nat_ref[pl.ds(base, count), 0:128]
        tail = nat_ref[pl.ds(base, count), 128:256]
        sx = nat_ref[pl.ds(base + 24, count), 0:128] - nat_ref[pl.ds(base - 24, count), 0:128]
        sy = nat_ref[pl.ds(base + 1, count), 0:128] - nat_ref[pl.ds(base - 1, count), 0:128]
        sz = roll(jnp.where(lane == 0, tail, mid), 127, 1) - roll(jnp.where(lane == 127, tail, mid), 1, 1)
        for k, s in enumerate((sx, sy, sz)):
            if ext:
                value = field_ref[k, i] + 0.5 * s
                good = jnp.where((row == 0) & (gy == 0), 0.0, 1.0)
                good = jnp.where((row == 9) & (gy == last_y), 0.0, good)
                if i == 0:
                    good = good * jnp.where(gx == 0, 0.0, 1.0)
                if i == 9:
                    good = good * jnp.where(gx == last_x, 0.0, 1.0)
                result_ref[k, i] = jnp.zeros((16, 128), F32)
                result_ref[k, i, 0:10, :] = value * good
            else:
                result_ref[k, i] = field_ref[k, i] + 0.5 * s


def backward_kernel(ids_ref, adj_ref, slope_ref, tall_ref, back_ref, grad_ref, over_ref, in_ref, bb_ref, acc_ref):
    gz = ids_ref[2]
    in_ref[144:256, :] = jnp.zeros((112, 256), BF16)
    bb_ref[3 * HIDDEN:DEEP, :] = jnp.zeros((DEEP - 3 * HIDDEN, 256), BF16)
    acc_ref[...] = jnp.zeros(acc_ref.shape, F32)
    for x in range(5):
        for half in range(2):
            col = slice(128 * half, 128 * half + 128)
            for k in range(3):
                high, low = split(adj_ref[k, x + 5 * half])
                in_ref[16 * k:16 * k + 16, col] = high
                in_ref[48 + 16 * k:64 + 16 * k, col] = low
                in_ref[96 + 16 * k:112 + 16 * k, col] = high
        high, low = split(once(back_ref[...], in_ref[...]) * slope_ref[x])
        bb_ref[0:HIDDEN, :] = high
        bb_ref[HIDDEN:2 * HIDDEN, :] = low
        bb_ref[2 * HIDDEN:3 * HIDDEN, :] = high
        total = once(tall_ref[...], bb_ref[...])
        for half in range(2):
            for a in range(3):
                at = x + 5 * half + a
                acc_ref[at] = acc_ref[at] + total[72 * a:72 * a + 72, 128 * half:128 * half + 128]
    lane = lanes()
    row = rows_of()
    for k in range(3):
        packed = jnp.zeros((8, 128), F32)
        for x in range(8):
            low = acc_ref[x + 2, 8 * k:8 * k + 8, :]
            mid = acc_ref[x + 2, 24 + 8 * k:32 + 8 * k, :]
            high = acc_ref[x + 2, 48 + 8 * k:56 + 8 * k, :]
            value = adj_ref[k, x + 1, 1:9, :] + mid
            value = value + jnp.where(lane == 127, 0.0, roll(low, 127, 1))
            grad_ref[k, x] = value + jnp.where(lane == 0, 0.0, roll(high, 1, 1))
            out = jnp.where(gz == 0, high[:, 127:128], low[:, 0:1])
            packed = packed + jnp.where(lane == 8 * x + row, out, 0.0)
        over_ref[k:k + 1, :] = jnp.sum(packed, axis=0, keepdims=True)
    over_ref[3:8, :] = jnp.zeros((5, 128), F32)


def join(ids_ref, part_ref, over_ref, grad_ref):
    gz = ids_ref[2]
    lane = lanes()
    row = rows_of()
    edge = jnp.where(gz == 0, 127, 0)
    for k in range(3):
        for x in range(8):
            column = jnp.sum(jnp.where(lane == 8 * x + row, over_ref[k:k + 1, :], 0.0), axis=1, keepdims=True)
            grad_ref[k, x] = part_ref[k, x] + jnp.where(lane == edge, column, 0.0)


VMEM = pl.BlockSpec(memory_space=pltpu.VMEM)
SMEM = pl.BlockSpec(memory_space=pltpu.SMEM)


def call(kernel, specs, shapes, scratch, *operands, flops=0, size=1 << 20, outs=None):
    return pl.pallas_call(
        kernel,
        in_specs=specs,
        out_specs=outs or [VMEM] * len(shapes),
        out_shape=[s if hasattr(s, "memory_space") else jax.ShapeDtypeStruct(*s) for s in shapes],
        scratch_shapes=scratch,
        compiler_params=pltpu.CompilerParams(vmem_limit_bytes=12 * 2**20),
        cost_estimate=pl.CostEstimate(flops=flops, bytes_accessed=size, transcendentals=0),
    )(*operands)


def trade(velocity, cotangent, axis, dim):
    count = lax.axis_size(axis)
    odd = lax.rem(lax.axis_index(axis), 2) == 1
    size = velocity.shape[dim]

    def cut(array, start, stop):
        return lax.slice_in_dim(array, start, stop, axis=dim)

    other = 3 - dim
    grow = [(0, 0)] * 4
    grow[other] = (0, velocity.shape[other] - cotangent.shape[other])
    low = jnp.concatenate([cut(velocity, 0, 2), jnp.pad(cut(cotangent, 0, 1), grow)], axis=dim)
    high = jnp.concatenate([cut(velocity, size - 2, size), jnp.pad(cut(cotangent, size - 1, size), grow)], axis=dim)
    pairs = [(i, i ^ 1) for i in range(count)]
    gaps = [(i, i + 1) for i in range(1, count - 1, 2)]
    gaps = gaps + [(j, i) for i, j in gaps]
    second = lax.ppermute(jnp.where(odd, high, low), axis, gaps)
    first = lax.ppermute(jnp.where(odd, low, high), axis, pairs)
    below, above = jnp.where(odd, first, second), jnp.where(odd, second, first)
    wide = jnp.concatenate([cut(below, 0, 2), velocity, cut(above, 0, 2)], axis=dim)
    kept = cotangent.shape[other]
    narrow = jnp.concatenate([lax.slice_in_dim(cut(below, 2, 3), 0, kept, axis=other), cotangent,
                              lax.slice_in_dim(cut(above, 2, 3), 0, kept, axis=other)], axis=dim)
    return wide, narrow


def gather_own(rows):
    nx, ny, nz = (lax.axis_size(a) for a in AXES)
    groups = [[(x * ny + 2 * y + c) * nz + z for z in range(nz) for y in range(ny // 2) for x in range(nx)]
              for c in range(2)]
    mine = lax.all_to_all(rows, AXES, 0, 0, axis_index_groups=groups)
    return mine.reshape(rows.shape[0] * rows.shape[1], rows.shape[2])


def twin(mine):
    return lax.ppermute(mine, "gy", [(i, i ^ 1) for i in range(lax.axis_size("gy"))])


def collect(rows):
    x = lax.axis_index("gx")
    odd, upper = lax.rem(x, 2) == 1, x >= 2
    one, two, three = (lax.ppermute(rows, "gx", [(i, i ^ d) for i in range(4)]) for d in (1, 2, 3))
    a, b = jnp.where(odd, one, rows), jnp.where(odd, rows, one)
    c, d = jnp.where(odd, three, two), jnp.where(odd, two, three)
    line = jnp.concatenate([jnp.where(upper, c, a), jnp.where(upper, d, b),
                            jnp.where(upper, a, c), jnp.where(upper, b, d)], axis=0)
    across = lax.ppermute(line, "gy", [(i, i ^ 2) for i in range(4)])
    upper = lax.axis_index("gy") >= 2
    near = jnp.concatenate([jnp.where(upper, across, line), jnp.where(upper, line, across)], axis=0)
    return near, lax.ppermute(near, "gz", [(0, 1), (1, 0)])


def project_rows(ext, ids, sweeps, field, *more):
    block = ((3, 8, 8, 128), F32)
    scratch = [
        pltpu.VMEM((2, 2, 8, 8, 8, 128), F32),
        pltpu.VMEM((2, 2, 8, 8, 8, 128), F32),
        pltpu.VMEM((2, 2, 8, 8, 8, 128), F32),
        pltpu.VMEM((2, 8, 8, 128), F32),
        pltpu.VMEM((2, 8, 2, 8, 128), F32),
        pltpu.VMEM((2, 4, 4, 8, 128), F32),
        pltpu.VMEM((288, 256), F32),
        pltpu.VMEM((288, 256), F32),
    ]
    return call(functools.partial(project_kernel, ext), [SMEM, SMEM] + [VMEM] * (1 + len(more)),
                [((3, 10, 16, 128), F32)] if ext else [block, block], scratch,
                ids, sweeps, field, *more, flops=6 * 10**9)


def weights(first_weight, first_bias, second_weight):
    return call(
        weights_kernel, [pl.BlockSpec(memory_space=pltpu.HBM)] * 3,
        [((2 * HIDDEN, REACH), BF16), ((216, DEEP), BF16), ((3 * WIDTH, 128), F32), ((HIDDEN, 256), BF16)],
        [pltpu.VMEM((256, 128), F32), pltpu.VMEM(first_weight.shape, F32), pltpu.VMEM((1, WIDTH), F32),
         pltpu.VMEM(second_weight.shape, F32), pltpu.SemaphoreType.DMA((3,))],
        *(pltpu.with_memory_space_constraint(a, pltpu.HBM) for a in (first_weight, first_bias[None], second_weight)),
        flops=10**9)


def forward(ids, second_bias, near, face, wide, out, count):
    return call(
        forward_kernel, [SMEM, SMEM] + [VMEM] * 4,
        [((3, 8, 8, 128), F32), pltpu.HBM((5, HIDDEN, 256), F32), pltpu.HBM((count, SENT, 128), F32)],
        [pltpu.VMEM((ROWS, 128), F32), pltpu.VMEM((4 * PLANE + REACH, 256), BF16), pltpu.VMEM((HIDDEN, 256), F32),
         pltpu.VMEM((3, 10, 16, 128), F32), pltpu.VMEM((64, 128), F32), pltpu.VMEM((5, HIDDEN, 256), F32),
         pltpu.SemaphoreType.DMA((5,)), pltpu.VMEM((SENT, 128), F32), pltpu.SemaphoreType.DMA((count,))],
        ids, second_bias, near, face, wide, out, flops=4 * 10**9,
        outs=[VMEM] + [pl.BlockSpec(memory_space=pltpu.HBM)] * 2)


def gathered(velocity, cotangent, first_weight, first_bias, second_weight, second_bias, sweeps):
    swap = [(0, 1), (1, 0)]
    ids = jnp.stack([lax.axis_index("gx"), lax.axis_index("gy"), lax.axis_index("gz"),
                     jnp.int32(lax.axis_size("gx")), jnp.int32(lax.axis_size("gy"))]).astype(jnp.int32)
    near, cot_near = trade(velocity, cotangent, "gx", 1)
    cot_rows = call(own_rows_kernel, [VMEM], [((SENT_OWN, 128), F32)], [pltpu.VMEM((80, 128), F32)], cot_near)[0]
    cot_own, cot_far = collect(cot_rows)
    near, cot_near = trade(near, cot_near, "gy", 2)
    face = jnp.where(ids[2] == 0, near[:, :, :, 127], near[:, :, :, 0])
    face = lax.ppermute(face, "gz", swap)
    wide, tall, out, back = weights(first_weight, first_bias, second_weight)
    closed, slope, rows = forward(ids, second_bias, near, face, wide, out, lax.axis_size(AXES) // 2)
    mine = gather_own(rows)
    cot_far, rows = lax.optimization_barrier((cot_far, rows))
    adjoint = project_rows(True, ids, sweeps, cot_near, cot_own, cot_far, twin(cot_own), twin(cot_far))[0]
    part, over_rows = call(
        backward_kernel, [SMEM] + [VMEM] * 4, [((3, 8, 8, 128), F32), ((8, 128), F32)],
        [pltpu.VMEM((256, 256), BF16), pltpu.VMEM((DEEP, 256), BF16), pltpu.VMEM((12, 72, 128), F32)],
        ids, adjoint, slope, tall, back, flops=10**6)
    over_rows = lax.ppermute(over_rows, "gz", swap)
    mine, part, over_rows = lax.optimization_barrier((mine, part, over_rows))
    updated, grad = project_rows(False, ids, sweeps, closed, mine, twin(mine), part, over_rows)
    return updated, grad


def one_gather(velocity, first_weight):
    nx, ny, nz = (lax.axis_size(a) for a in AXES)
    return (velocity.shape == (3, 8, 8, 128) and nx == 4 and ny == 4 and nz == 2
            and first_weight.shape == (WIDTH, 81))


def dispatch(velocity, cotangent, first_weight, first_bias, second_weight, second_bias, sweeps):
    path = gathered if one_gather(velocity, first_weight) else shards
    return path(velocity, cotangent, first_weight, first_bias, second_weight, second_bias, sweeps)


def solution(mesh):
    return jax.shard_map(
        dispatch,
        mesh=mesh,
        in_specs=(P(None, "gx", "gy", "gz"), P(None, "gx", "gy", "gz"), P(), P(), P(), P(), P()),
        out_specs=(P(None, "gx", "gy", "gz"), P(None, "gx", "gy", "gz")),
        check_vma=False,
    )
```

```python
import functools

import jax
import jax.numpy as jnp
from jax import lax
from jax.experimental import pallas as pl
from jax.experimental.pallas import tpu as pltpu
from jax.sharding import PartitionSpec as P

LEVELS = 3
COARSE_SWEEPS = 6
CYCLES = 2


OMEGA = 0.8


def with_halo(block, sides, width):
    for axis, dim in sides:
        count = lax.axis_size(axis)
        forward = [(i, i + 1) for i in range(count - 1)]
        backward = [(target, source) for source, target in forward]
        low = lax.ppermute(
            lax.slice_in_dim(block, block.shape[dim] - width, None, axis=dim), axis, forward
        )
        high = lax.ppermute(lax.slice_in_dim(block, 0, width, axis=dim), axis, backward)
        block = jnp.concatenate([low, block, high], axis=dim)
    return block


def stencil_features(region):
    span_y = region.shape[2] - 2
    span_z = region.shape[3] - 2
    shifted = [
        region[:, first, second : second + span_y, third : third + span_z]
        for first in range(3)
        for second in range(3)
        for third in range(3)
    ]
    return jnp.stack(shifted).reshape(27 * region.shape[0], span_y * span_z)


def six_point(field, padded):
    beside = padded[:, 2:, 1:-1, 1:-1] + padded[:, :-2, 1:-1, 1:-1]
    beside = beside + padded[:, 1:-1, 2:, 1:-1] + padded[:, 1:-1, :-2, 1:-1]
    beside = beside + padded[:, 1:-1, 1:-1, 2:] + padded[:, 1:-1, 1:-1, :-2]
    return 6.0 * field - beside


def near_faces(field):
    return with_halo(field, (("gx", 1), ("gy", 2), ("gz", 3)), 1)


def laplace_shared(field):
    return six_point(field, near_faces(field))


def relax(guess, source):
    return guess + OMEGA * (source - laplace_shared(guess)) / 6.0


def restrict(residue):
    batch, size_x, size_y, size_z = residue.shape
    folded = residue.reshape(batch, size_x // 2, 2, size_y // 2, 2, size_z // 2, 2)
    return 0.5 * folded.sum(axis=(2, 4, 6))


def prolong(coarse):
    return jnp.repeat(jnp.repeat(jnp.repeat(coarse, 2, axis=1), 2, axis=2), 2, axis=3)


def coarse_spread(source, sweeps):
    guess = OMEGA * source / 6.0
    return lax.fori_loop(1, COARSE_SWEEPS, lambda number, state: relax(state, source), guess)


def vcycle(source, sweeps, level, coarse_solve, bottom):
    if level == bottom:
        return coarse_solve(source, sweeps)
    repeats = sweeps[level]
    guess = OMEGA * source / 6.0
    guess = lax.fori_loop(1, repeats, lambda number, state: relax(state, source), guess)
    residue = source - laplace_shared(guess)
    guess = guess + prolong(vcycle(restrict(residue), sweeps, level + 1, coarse_solve, bottom))
    return lax.fori_loop(0, repeats, lambda number, state: relax(state, source), guess)


def divergence(padded):
    total = padded[:, 0, 2:, 1:-1, 1:-1] - padded[:, 0, :-2, 1:-1, 1:-1]
    total = total + padded[:, 1, 1:-1, 2:, 1:-1] - padded[:, 1, 1:-1, :-2, 1:-1]
    total = total + padded[:, 2, 1:-1, 1:-1, 2:] - padded[:, 2, 1:-1, 1:-1, :-2]
    return 0.5 * total


def gradient(padded):
    return 0.5 * jnp.stack(
        [
            padded[:, 2:, 1:-1, 1:-1] - padded[:, :-2, 1:-1, 1:-1],
            padded[:, 1:-1, 2:, 1:-1] - padded[:, 1:-1, :-2, 1:-1],
            padded[:, 1:-1, 1:-1, 2:] - padded[:, 1:-1, 1:-1, :-2],
        ],
        axis=1,
    )


def project(fields, sweeps, coarse_solve, bottom):
    batch, comps, size_x, size_y, size_z = fields.shape
    padded = near_faces(fields.reshape(batch * comps, size_x, size_y, size_z))
    padded = padded.reshape(batch, comps, size_x + 2, size_y + 2, size_z + 2)
    source = divergence(padded)
    pressure = vcycle(source, sweeps, 0, coarse_solve, bottom)
    pressure = pressure + vcycle(source - laplace_shared(pressure), sweeps, 0, coarse_solve, bottom)
    return fields + gradient(near_faces(pressure))


def corrections(near, first_weight, first_bias, second_weight, second_bias, planes):
    span_y = near.shape[2] - 2
    span_z = near.shape[3] - 2

    def corrections_one_plane(index):
        region = lax.dynamic_slice_in_dim(near, index, 3, 1)
        feats = stencil_features(region)
        hidden = jax.nn.silu(
            jnp.dot(first_weight, feats, precision=lax.Precision.HIGHEST) + first_bias[:, None]
        )
        return (
            jnp.dot(second_weight, hidden, precision=lax.Precision.HIGHEST) + second_bias[:, None]
        )

    result = lax.map(corrections_one_plane, jnp.arange(planes, dtype=jnp.int32))
    return result.reshape(planes, 3, span_y, span_z).transpose(1, 0, 2, 3)


def back_planes(wide, cot_pad, first_weight, first_bias, second_weight, planes):
    span_y = cot_pad.shape[2] - 2
    span_z = cot_pad.shape[3] - 2

    def back_one_plane(index):
        region = lax.dynamic_slice_in_dim(wide, index, 3, 1)
        feats = stencil_features(region)
        pre = jnp.dot(first_weight, feats, precision=lax.Precision.HIGHEST) + first_bias[:, None]
        sig = jax.nn.sigmoid(pre)
        slope = sig * (1.0 + pre * (1.0 - sig))
        incoming = lax.dynamic_index_in_dim(cot_pad, index, 1, keepdims=False).reshape(3, -1)
        back = jnp.dot(second_weight.T, incoming, precision=lax.Precision.HIGHEST) * slope
        spread = jnp.dot(first_weight.T, back, precision=lax.Precision.HIGHEST)
        spread = spread.reshape(3, 3, 3, 3, span_y + 2, span_z + 2)
        parts = []
        for first in range(3):
            total = jnp.zeros((3, span_y, span_z), jnp.float32)
            for second in range(3):
                for third in range(3):
                    total = (
                        total
                        + spread[
                            first,
                            second,
                            third,
                            :,
                            2 - second : 2 - second + span_y,
                            2 - third : 2 - third + span_z,
                        ]
                    )
            parts.append(total)
        return jnp.stack(parts)

    pieces = lax.map(back_one_plane, jnp.arange(planes + 2, dtype=jnp.int32))
    return pieces[:-2, 2] + pieces[1:-1, 1] + pieces[2:, 0]


def shards(velocity, cotangent, first_weight, first_bias, second_weight, second_bias, sweeps):
    planes = velocity.shape[1]
    near = with_halo(velocity, (("gx", 1), ("gy", 2), ("gz", 3)), 1)
    coarse_solve, bottom = (coarse_spread, LEVELS)
    closed = velocity + corrections(
        near, first_weight, first_bias, second_weight, second_bias, planes
    )
    updated = project(closed[None], sweeps, coarse_solve, bottom)[0]
    adjoint_closed = project(cotangent[None], sweeps, coarse_solve, bottom)[0]
    wide = with_halo(velocity, (("gx", 1), ("gy", 2), ("gz", 3)), 2)
    cot_pad = with_halo(adjoint_closed, (("gx", 1), ("gy", 2), ("gz", 3)), 1)
    summed = back_planes(wide, cot_pad, first_weight, first_bias, second_weight, planes)
    grad_velocity = adjoint_closed + summed.transpose(1, 0, 2, 3)
    return (updated, grad_velocity)


AXES = ("gx", "gy", "gz")
STEP = OMEGA / 6.0
KEEP = 1.0 - OMEGA
WIDTH = 32
SPAN = 10
ROWS = 112
PLANE = 2 * ROWS
REACH = 768
DEEP = 1024
HIDDEN = SPAN * WIDTH
SENT = 72
SENT_OWN = 88
F32 = jnp.float32
BF16 = jnp.bfloat16


def roll(value, shift, axis):
    return pltpu.roll(value, shift, axis)


def lanes(shape=(8, 128)):
    return lax.broadcasted_iota(jnp.int32, shape, len(shape) - 1)


def rows_of(shape=(8, 128)):
    return lax.broadcasted_iota(jnp.int32, shape, len(shape) - 2)


def split(value):
    high = value.astype(BF16)
    return high, (value - high.astype(F32)).astype(BF16)


def exact(left, right):
    high = left.astype(BF16)
    rest = left - high.astype(F32)
    middle, low = split(rest)
    right = right.astype(BF16)
    return (once(high, right) + once(middle, right)) + once(low, right)


def once(left, right):
    return jnp.dot(left, right, preferred_element_type=F32)


def one_hot(condition):
    return jnp.where(condition, 1.0, 0.0).astype(BF16)


def column_of(line, size):
    square = (size, size)
    return jnp.sum(jnp.where(rows_of(square) == lanes(square), line, 0.0), axis=1, keepdims=True)


def weights_kernel(first_hbm, bias_hbm, second_hbm, wide_ref, tall_ref, out_ref, back_ref,
                   pad_ref, first_ref, bias_ref, second_ref, sems):
    pairs = ((first_hbm, first_ref), (bias_hbm, bias_ref), (second_hbm, second_ref))
    copies = [pltpu.make_async_copy(source, target, sems.at[i]) for i, (source, target) in enumerate(pairs)]
    for copy in copies:
        copy.start()
    for copy in copies:
        copy.wait()
    count = first_ref.shape[1]
    pad_ref[...] = jnp.zeros((256, 128), F32)
    pad_ref[0:WIDTH, 0:count] = first_ref[...]
    pad_ref[128:131, 0:WIDTH] = second_ref[...]
    first = pad_ref[0:128, :]
    second = pad_ref[128:256, :]
    high, low = split(first[0:WIDTH])
    column = lanes((1, REACH))
    rest = column % ROWS
    real = (rest < 108) & (column < 3 * PLANE)
    height = jnp.where(real, rest % 12, -1)
    feature = jnp.where(real, 27 * (column // PLANE) + rest // 12, -1000)
    upper = (column % PLANE) < ROWS
    bias_high, bias_low = split(column_of(bias_ref[...], WIDTH))
    totals = [jnp.where(column == 108, part.astype(F32), 0.0) for part in (bias_high, bias_low)]
    row = rows_of((128, REACH))
    parts = []
    for b in range(3):
        chosen = one_hot(row - 9 * b == feature)
        parts.append((once(high, chosen), jnp.where(upper, once(low, chosen), 0.0)))
    for y in range(SPAN):
        for half in range(2):
            total = totals[half]
            for b in range(3):
                total = total + jnp.where(height == y + b, parts[b][half], 0.0)
            wide_ref[half * HIDDEN + y * WIDTH:half * HIDDEN + (y + 1) * WIDTH, :] = total.astype(BF16)
    high, low = split(first.T)
    column = lanes((1, DEEP))
    row = rows_of((128, DEEP))
    place = (column % HIDDEN) // WIDTH
    term = column // HIDDEN
    tiled = one_hot((row == column % WIDTH) & (column < 3 * HIDDEN))
    copies = jnp.where(term == 2, once(low, tiled), once(high, tiled)).astype(BF16)
    line = lax.broadcasted_iota(jnp.int32, (216, 128), 0)
    lane = lanes((216, 128))
    tops = line[:, 0:1] % 8 + 2
    total = jnp.zeros((216, DEEP), F32)
    for b in range(3):
        lift = one_hot(lane - 9 * b == 27 * (line // 72) + (line % 72) // 8)
        total = total + jnp.where(tops - b == place, once(lift, copies), 0.0)
    tall_ref[...] = total.astype(BF16)
    for k in range(3):
        line = second[k:k + 1, 0:WIDTH]
        out_ref[WIDTH * k:WIDTH * (k + 1), :] = jnp.broadcast_to(column_of(line, WIDTH), (WIDTH, 128))
    high, low = split(second.T[0:WIDTH])
    column = lanes((1, 256))
    row = rows_of((128, 256))
    inner = one_hot((row == (column % 48) // 16) & (column < 144))
    copies = jnp.where(column // 48 == 2, once(low, inner), once(high, inner))
    for y in range(SPAN):
        back_ref[y * WIDTH:(y + 1) * WIDTH, :] = jnp.where(column % 16 == y, copies, 0.0).astype(BF16)


def depth_order():
    first = lax.broadcasted_iota(jnp.int32, (128, 128), 0)
    return jnp.where((first % 2) * 64 + first // 2 == lanes((128, 128)), 1.0, 0.0)


def send_rows(get, flat_ref, sent_ref):
    lane = lanes()
    row = rows_of()
    faces = jnp.zeros((8, 128), F32)
    for x in range(8):
        up = get(2, x + 1, 1)
        value = get(0, x + 2, 1) - get(0, x, 1) + get(1, x + 1, 2) - get(1, x + 1, 0)
        value = value + jnp.where(lane == 127, 0.0, roll(up, 127, 1)) - jnp.where(lane == 0, 0.0, roll(up, 1, 1))
        flat_ref[8 * x:8 * x + 8, :] = 0.5 * value
        faces = faces + jnp.where(lane == 8 * x + row, 0.5 * up[:, 0:1], 0.0)
        faces = faces - jnp.where(lane == 64 + 8 * x + row, 0.5 * up[:, 127:128], 0.0)
    sent_ref[0:64, :] = exact(flat_ref[...], depth_order())
    sent_ref[64:72, :] = jnp.where(row == 0, jnp.sum(faces, axis=0, keepdims=True), 0.0)


def own_rows_kernel(field_ref, sent_ref, flat_ref):
    lane = lanes()
    row = rows_of()
    faces = jnp.zeros((8, 128), F32)
    for x in range(8):
        along = field_ref[1, x + 1]
        up = field_ref[2, x + 1]
        value = jnp.where(row == 7, 0.0, roll(along, 7, 0)) - jnp.where(row == 0, 0.0, roll(along, 1, 0))
        value = value + jnp.where(lane == 127, 0.0, roll(up, 127, 1)) - jnp.where(lane == 0, 0.0, roll(up, 1, 1))
        flat_ref[8 * x:8 * x + 8, :] = 0.5 * (value + field_ref[0, x + 2] - field_ref[0, x])
        flat_ref[64 + x:65 + x, :] = 0.5 * along[0:1, :]
        flat_ref[72 + x:73 + x, :] = -0.5 * along[7:8, :]
        faces = faces + jnp.where(lane == 8 * x + row, 0.5 * up[:, 0:1], 0.0)
        faces = faces - jnp.where(lane == 64 + 8 * x + row, 0.5 * up[:, 127:128], 0.0)
    turned = exact(flat_ref[...], depth_order())
    sent_ref[0:64, :] = turned[0:64]
    sent_ref[64:72, :] = jnp.where(row == 0, jnp.sum(faces, axis=0, keepdims=True), 0.0)
    sent_ref[72:88, :] = turned[64:80]


def fold(values):
    row = rows_of()
    low = row < 4
    values = [jnp.where(low, a, b) + roll(jnp.where(low, b, a), 4, 0) for a, b in zip(values[:4], values[4:])]
    for step in (2, 1):
        low = (row // step) % 2 == 0
        values = [jnp.where(low, a + roll(a, 8 - step, 0), b + roll(b, step, 0))
                  for a, b in zip(values[:step], values[step:])]
    return values[0]


def forward_kernel(ids_ref, bias_ref, ext_ref, col_ref, wide_ref, out_ref, closed_ref, slope_ref, sent_ref,
                   plane_ref, feat_ref, hid_ref, ce_ref, flat_ref, kept_ref, sems, rows_ref, row_sems):
    gx, gy, gz = ids_ref[0], ids_ref[1], ids_ref[2]
    low_side = jnp.where(gz == 0, 1.0, 0.0)
    high_side = 1.0 - low_side
    lane = lanes((12, 128))
    pad_row = rows_of((8, 128))
    plane_ref[104:112, :] = jnp.where(pad_row == 4, 1.0, 0.0)
    feat_ref[7 * PLANE:, :] = jnp.zeros((REACH - 3 * PLANE, 256), BF16)
    corner = rows_of((12, 12)) == lanes((12, 12))
    beyond = [[jnp.sum(jnp.where(corner, col_ref[k, at:at + 1, :], 0.0), axis=1, keepdims=True) for at in range(12)]
              for k in range(3)]
    for step in range(7):
        for half in range(2):
            at = step + 5 * half
            for k in range(3):
                here = ext_ref[k, at]
                below = jnp.where(lane == 0, beyond[k][at] * high_side, roll(here, 1, 1))
                above = jnp.where(lane == 127, beyond[k][at] * low_side, roll(here, 127, 1))
                for c, piece in ((0, below), (1, here), (2, above)):
                    plane_ref[pl.ds((c * 3 + k) * 12, 12), :] = piece
            high, low = split(plane_ref[...])
            col = slice(128 * half, 128 * half + 128)
            feat_ref[step * PLANE:step * PLANE + ROWS, col] = high
            feat_ref[step * PLANE + ROWS:step * PLANE + 2 * ROWS, col] = low
    row = rows_of((10, 128))
    inside = jnp.where((row == 0) & (gy == 0), 0.0, 1.0)
    inside = jnp.where((row == 9) & (gy == ids_ref[4] - 1), 0.0, inside)
    for x in range(5):
        both = once(wide_ref[...], feat_ref[x * PLANE:x * PLANE + REACH, :])
        pre = both[0:HIDDEN] + both[HIDDEN:]
        sig = 0.5 * jnp.tanh(0.5 * pre) + 0.5
        kept_ref[x] = sig * (1.0 + pre * (1.0 - sig))
        pltpu.make_async_copy(kept_ref.at[x], slope_ref.at[x], sems.at[x]).start()
        hid_ref[...] = pre * sig
        for half in range(2):
            e = x + 5 * half
            mask = inside
            if e == 0:
                mask = inside * jnp.where(gx == 0, 0.0, 1.0)
            if e == 9:
                mask = inside * jnp.where(gx == ids_ref[3] - 1, 0.0, 1.0)
            sums = []
            for y in range(SPAN):
                here = [hid_ref[y * WIDTH + 8 * i:y * WIDTH + 8 * i + 8, 128 * half:128 * half + 128] for i in range(4)]
                for k in range(3):
                    terms = [out_ref[WIDTH * k + 8 * i:WIDTH * k + 8 * i + 8, :] * here[i] for i in range(4)]
                    sums.append((terms[0] + terms[1]) + (terms[2] + terms[3]))
            rest = fold([sums[3 * y + k] for k in range(3) for y in (8, 9)] + [sums[0]] * 2)
            for k in range(3):
                ce_ref[k, e, 0:8, :] = fold([sums[3 * y + k] for y in range(8)])
                ce_ref[k, e, 8:10, :] = rest[2 * k:2 * k + 2, :]
                ce_ref[k, e, 0:10, :] = (ce_ref[k, e, 0:10, :] + bias_ref[k] + ext_ref[k, e + 1, 1:11, :]) * mask
    for k in range(3):
        for x in range(8):
            closed_ref[k, x] = ce_ref[k, x + 1, 1:9, :]
    send_rows(lambda k, x, y: ce_ref[k, x, pl.ds(y, 8), :], flat_ref, rows_ref)
    copies = [pltpu.make_async_copy(rows_ref, sent_ref.at[i], row_sems.at[i]) for i in range(sent_ref.shape[0])]
    for copy in copies:
        copy.start()
    for copy in copies:
        copy.wait()
    for x in range(5):
        pltpu.make_async_copy(kept_ref.at[x], slope_ref.at[x], sems.at[x]).wait()


def around(grid, wide, masks):
    (x_low, x_high, y_low, y_high) = masks
    lane = lanes()
    size = len(grid[0])
    result = []
    for c in range(2):
        plane = []
        for x in range(size):
            line = []
            for y in range(size):
                here = grid[c][x][y]
                total = jnp.where(lane >= wide, roll(here, wide, 1), 0.0)
                total = total + jnp.where(lane < 128 - wide, roll(here, 128 - wide, 1), 0.0)
                total = total + (grid[c][x - 1][y] if x > 0 else roll(grid[c][size - 1][y], 1, 0) * x_low)
                total = total + (grid[c][x + 1][y] if x < size - 1 else roll(grid[c][0][y], 7, 0) * x_high)
                if y > 0:
                    total = total + grid[c][x][y - 1]
                else:
                    edge = grid[1 - c][x][size - 1]
                    total = total + (edge if c == 1 else roll(edge, 4, 0) * y_low)
                if y < size - 1:
                    total = total + grid[c][x][y + 1]
                else:
                    edge = grid[1 - c][x][0]
                    total = total + (edge if c == 0 else roll(edge, 4, 0) * y_high)
                line.append(total)
            plane.append(line)
        result.append(plane)
    return result


def over(function, *grids):
    size = len(grids[0][0])
    return [[[function(*(g[c][x][y] for g in grids)) for y in range(size)] for x in range(size)] for c in range(2)]


def flat(grid):
    return tuple(v for plane in grid for line in plane for v in line)


def unflat(values, size):
    values = list(values)
    return [[[values[(c * size + x) * size + y] for y in range(size)] for x in range(size)] for c in range(2)]


def relax_level(guess, source, wide, masks):
    return over(lambda g, s, n: KEEP * g + STEP * (s + n), guess, source, around(guess, wide, masks))


def residue_level(guess, source, wide, masks):
    return over(lambda g, s, n: s - 6.0 * g + n, guess, source, around(guess, wide, masks))


def coarser(grid, wide):
    lane = lanes()
    size = len(grid[0]) // 2
    even = (lane // wide) % 2 == 0
    result = []
    for c in range(2):
        plane = []
        for x in range(size):
            line = []
            for y in range(size):
                t = grid[c][2 * x][2 * y] + grid[c][2 * x][2 * y + 1]
                t = t + grid[c][2 * x + 1][2 * y] + grid[c][2 * x + 1][2 * y + 1]
                line.append(0.5 * (t + jnp.where(even, roll(t, 128 - wide, 1), roll(t, wide, 1))))
            plane.append(line)
        result.append(plane)
    return result


def add_coarse(grid, coarse):
    size = len(grid[0])
    return [[[grid[c][x][y] + coarse[c][x // 2][y // 2] for y in range(size)] for x in range(size)] for c in range(2)]


def coarsest(source, wide, masks):
    (x_low, x_high, y_low, y_high) = masks
    lane = lanes()
    reach = COARSE_SWEEPS - 1
    moved, inside = {}, {}
    for j in range(-reach, reach + 1):
        at = lane + wide * j
        inside[j] = jnp.where((at >= 0) & (at < 128), 1.0, 0.0)
        for c in range(2):
            here = source[c][0][0]
            moved[j, c] = here if j == 0 else roll(here, (-wide * j) % 128, 1) * inside[j]
    guess = {at: STEP * value for at, value in moved.items()}
    for k in range(1, reach + 1):
        after = {}
        for j in range(k - reach, reach - k + 1):
            for c in range(2):
                here, other = guess[j, c], guess[j, 1 - c]
                across = roll(other, 4, 0) * (y_low if c == 0 else y_high)
                total = (guess[j - 1, c] + guess[j + 1, c]) + (other + moved[j, c])
                total = total + ((roll(here, 1, 0) * x_low + roll(here, 7, 0) * x_high) + across)
                value = KEEP * here + STEP * total
                after[j, c] = value if j == 0 else value * inside[j]
        guess = after
    return [[[guess[0, c]]] for c in range(2)]


def level_solve(source, level, sweeps_ref, masks):
    wide = 1 << (level - 1)
    if level == LEVELS:
        return coarsest(source, wide, masks)
    size = len(source[0])
    guess = over(lambda s: STEP * s, source)
    repeats = sweeps_ref[level]

    def body(number, state):
        return flat(relax_level(unflat(state, size), source, wide, masks))

    guess = unflat(lax.fori_loop(1, repeats, body, flat(guess)), size)
    coarse = coarser(residue_level(guess, source, wide, masks), wide)
    guess = add_coarse(guess, level_solve(coarse, level + 1, sweeps_ref, masks))
    return unflat(lax.fori_loop(0, repeats, body, flat(guess)), size)


def project_kernel(ext, ids_ref, sweeps_ref, field_ref, *refs):
    source_refs, refs = refs[:4 if ext else 2], refs[4 if ext else 2:]
    if ext:
        result_ref, s_ref, x_ref, p_ref, wrap_ref, edge_ref, c_ref, win_ref, nat_ref = refs
    else:
        part_ref, over_ref, result_ref, grad_ref, s_ref, x_ref, p_ref, wrap_ref, edge_ref, c_ref, win_ref, nat_ref = refs
        join(ids_ref, part_ref, over_ref, grad_ref)
    sent = SENT_OWN if ext else SENT
    gx, gy, gz = ids_ref[0], ids_ref[1], ids_ref[2]
    core = lax.rem(gy, 2)
    lane = lanes()
    sub = rows_of()
    x_low = jnp.where(sub % 4 != 0, 1.0, 0.0)
    x_high = jnp.where(sub % 4 != 3, 1.0, 0.0)
    y_low = jnp.where(sub >= 4, 1.0, 0.0)
    y_high = jnp.where(sub < 4, 1.0, 0.0)
    masks = (x_low, x_high, y_low, y_high)
    z_low = jnp.where(lane != 0, 1.0, 0.0)
    z_high = jnp.where(lane != 127, 1.0, 0.0)
    lower = lane < 64

    if ext:
        near_ref, far_ref, near_twin_ref, far_twin_ref = source_refs
        sources = ((near_ref, far_ref, core), (near_twin_ref, far_twin_ref, 1 - core))
    else:
        mine_ref, other_ref = source_refs
        sources = ((mine_ref, mine_ref.at[pl.ds(8 * sent, 8 * sent)], core),
                   (other_ref, other_ref.at[pl.ds(8 * sent, 8 * sent)], 1 - core))

    def both(near_ref, far_ref, i):
        near = near_ref[pl.ds(i, 8, stride=sent), :]
        far = far_ref[pl.ds(i, 8, stride=sent), :]
        if ext:
            return jnp.where(gz == 0, near, far), jnp.where(gz == 0, far, near)
        return near, far

    def halves(near_ref, far_ref, i):
        first, second = both(near_ref, far_ref, i)
        return jnp.where(lower, first, roll(second, 64, 1)), jnp.where(lower, roll(first, 64, 1), second)

    for near_ref, far_ref, slot in sources:
        face0, face1 = both(near_ref, far_ref, 64)
        for x in range(8):
            for y in range(8):
                i = 8 * x + y
                even, odd = halves(near_ref, far_ref, i)
                even = even + jnp.where(lane == 64, roll(face0, (128 - i) % 128, 1), 0.0)
                odd = odd + jnp.where(lane == 63, roll(face1, (63 - i) % 128, 1), 0.0)
                for zi, value in ((0, even), (1, odd)):
                    s_ref[slot, zi, x, y] = value
                    x_ref[slot, zi, x, y] = STEP * value

    def also(slot, zi, x, y, value):
        s_ref[slot, zi, x, y] = s_ref[slot, zi, x, y] + value
        x_ref[slot, zi, x, y] = x_ref[slot, zi, x, y] + STEP * value

    if ext:
        for near_ref, far_ref, slot in sources:
            for at in range(8):
                for zi, value in enumerate(halves(near_ref, far_ref, 72 + at)):
                    also(1 - slot, zi, at, 7, jnp.where(slot == 1, value, roll(value, 4, 0) * y_high))
                for zi, value in enumerate(halves(near_ref, far_ref, 80 + at)):
                    also(1 - slot, zi, at, 0, jnp.where(slot == 0, value, roll(value, 4, 0) * y_low))

    every = [(zi, y) for zi in range(2) for y in range(8)]

    def visit(use, coarse=None):
        def load(c, zi, x, y):
            value = x_ref[c, zi, x, y]
            return value if coarse is None else value + coarse[c, x // 2, y // 2]

        for c in range(2):
            first = {at: load(c, at[0], 0, at[1]) for at in every}
            before = {at: roll(load(c, at[0], 7, at[1]), 1, 0) * x_low for at in every}
            for at in every:
                wrap_ref[at[0], at[1]] = roll(first[at], 7, 0) * x_high
            own = first
            for x in range(8):
                after = {at: load(c, at[0], x + 1, at[1]) if x < 7 else wrap_ref[at[0], at[1]] for at in every}
                for zi in range(2):
                    if c == 0:
                        down = roll(load(1, zi, x, 7), 4, 0) * y_low
                        up = load(1, zi, x, 0)
                        edge_ref[zi, x, 0] = own[zi, 7]
                        edge_ref[zi, x, 1] = roll(own[zi, 0], 4, 0) * y_high
                    else:
                        down = edge_ref[zi, x, 0]
                        up = edge_ref[zi, x, 1]
                    for y in range(8):
                        beside = own[1 - zi, y]
                        total = before[zi, y] + after[zi, y] + beside
                        total = total + (own[zi, y - 1] if y > 0 else down) + (own[zi, y + 1] if y < 7 else up)
                        if zi == 0:
                            total = total + roll(beside, 1, 1) * z_low
                        else:
                            total = total + roll(beside, 127, 1) * z_high
                        value = use(c, zi, x, y, own[zi, y], total)
                        if value is not None:
                            x_ref[c, zi, x, y] = value
                before, own = own, after

    def relaxed(c, zi, x, y, own, total):
        return KEEP * own + STEP * (s_ref[c, zi, x, y] + total)

    def sweep(number, carry):
        visit(relaxed)
        return carry

    repeats = sweeps_ref[0]

    def cycle(number, carry):
        lax.fori_loop(1, repeats, sweep, 0)
        sums = {}

        def gather(c, zi, x, y, own, total):
            e = s_ref[c, zi, x, y] - 6.0 * own + total
            at = (c, x // 2, y // 2)
            sums[at] = sums[at] + e if at in sums else e

        visit(gather)
        coarse = [[[0.5 * sums[c, x, y] for y in range(4)] for x in range(4)] for c in range(2)]
        coarse = level_solve(coarse, 1, sweeps_ref, masks)
        for c in range(2):
            for x in range(4):
                for y in range(4):
                    c_ref[c, x, y] = coarse[c][x][y]
        visit(relaxed, c_ref)
        lax.fori_loop(1, repeats, sweep, 0)

        @pl.when(number == 0)
        def _():
            def restart(c, zi, x, y, own, total):
                p_ref[c, zi, x, y] = own
                rest = s_ref[c, zi, x, y] - 6.0 * own + total
                s_ref[c, zi, x, y] = rest
                return STEP * rest

            visit(restart)

        return carry

    lax.fori_loop(0, CYCLES, cycle, 0)

    x_rows = x_ref.reshape(2 * 2 * 8 * 8 * 8, 128)
    p_rows = p_ref.reshape(2 * 2 * 8 * 8 * 8, 128)
    last_x, last_y = ids_ref[3] - 1, ids_ref[4] - 1
    for wx in range(12):
        dx = -1 if wx < 2 else (1 if wx > 9 else 0)
        xi = (wx - 2) % 8
        bx = gx + dx
        for dy in (-1, 0, 1):
            by = gy + dy
            ok = (bx >= 0) & (bx <= last_x) & (by >= 0) & (by <= last_y)
            ax = jnp.clip(bx, 0, last_x)
            ay = jnp.clip(by, 0, last_y)
            at = (ay // 2) * 4 + ax
            c = lax.rem(ay, 2)
            for zi in range(2):
                start = ((c * 2 + zi) * 8 + xi) * 64 + at
                first = x_rows[pl.ds(start, 8, stride=8), :]
                second = p_rows[pl.ds(start, 8, stride=8), :]
                win_ref[wx * 24 + 8 * (dy + 1):wx * 24 + 8 * (dy + 1) + 8, 128 * zi:128 * zi + 128] = jnp.where(
                    ok, first + second, 0.0)
    source = lax.broadcasted_iota(jnp.int32, (256, 256), 0)
    target = lanes((256, 256))
    depth = 2 * (source % 128) + source // 128
    wanted = jnp.where(target == 255, -1, target) + gz * 128
    pick = jnp.where((depth == wanted) & ((target <= 128) | (target == 255)), 1.0, 0.0)
    nat_ref[...] = exact(win_ref[...], pick)

    size = 16 if ext else 8
    count = 10 if ext else 8
    lane = lanes((count, 128))
    row = rows_of((count, 128))
    for i in range(count):
        x = i - 1 if ext else i
        top = 7 if ext else 8
        base = (x + 2) * 24 + top
        mid = nat_ref[pl.ds(base, count), 0:128]
        tail = nat_ref[pl.ds(base, count), 128:256]
        sx = nat_ref[pl.ds(base + 24, count), 0:128] - nat_ref[pl.ds(base - 24, count), 0:128]
        sy = nat_ref[pl.ds(base + 1, count), 0:128] - nat_ref[pl.ds(base - 1, count), 0:128]
        sz = roll(jnp.where(lane == 0, tail, mid), 127, 1) - roll(jnp.where(lane == 127, tail, mid), 1, 1)
        for k, s in enumerate((sx, sy, sz)):
            if ext:
                value = field_ref[k, i] + 0.5 * s
                good = jnp.where((row == 0) & (gy == 0), 0.0, 1.0)
                good = jnp.where((row == 9) & (gy == last_y), 0.0, good)
                if i == 0:
                    good = good * jnp.where(gx == 0, 0.0, 1.0)
                if i == 9:
                    good = good * jnp.where(gx == last_x, 0.0, 1.0)
                result_ref[k, i] = jnp.zeros((16, 128), F32)
                result_ref[k, i, 0:10, :] = value * good
            else:
                result_ref[k, i] = field_ref[k, i] + 0.5 * s


def backward_kernel(ids_ref, adj_ref, slope_ref, tall_ref, back_ref, grad_ref, over_ref, in_ref, bb_ref, acc_ref):
    gz = ids_ref[2]
    in_ref[144:256, :] = jnp.zeros((112, 256), BF16)
    bb_ref[3 * HIDDEN:DEEP, :] = jnp.zeros((DEEP - 3 * HIDDEN, 256), BF16)
    acc_ref[...] = jnp.zeros(acc_ref.shape, F32)
    for x in range(5):
        for half in range(2):
            col = slice(128 * half, 128 * half + 128)
            for k in range(3):
                high, low = split(adj_ref[k, x + 5 * half])
                in_ref[16 * k:16 * k + 16, col] = high
                in_ref[48 + 16 * k:64 + 16 * k, col] = low
                in_ref[96 + 16 * k:112 + 16 * k, col] = high
        high, low = split(once(back_ref[...], in_ref[...]) * slope_ref[x])
        bb_ref[0:HIDDEN, :] = high
        bb_ref[HIDDEN:2 * HIDDEN, :] = low
        bb_ref[2 * HIDDEN:3 * HIDDEN, :] = high
        total = once(tall_ref[...], bb_ref[...])
        for half in range(2):
            for a in range(3):
                at = x + 5 * half + a
                acc_ref[at] = acc_ref[at] + total[72 * a:72 * a + 72, 128 * half:128 * half + 128]
    lane = lanes()
    row = rows_of()
    for k in range(3):
        packed = jnp.zeros((8, 128), F32)
        for x in range(8):
            low = acc_ref[x + 2, 8 * k:8 * k + 8, :]
            mid = acc_ref[x + 2, 24 + 8 * k:32 + 8 * k, :]
            high = acc_ref[x + 2, 48 + 8 * k:56 + 8 * k, :]
            value = adj_ref[k, x + 1, 1:9, :] + mid
            value = value + jnp.where(lane == 127, 0.0, roll(low, 127, 1))
            grad_ref[k, x] = value + jnp.where(lane == 0, 0.0, roll(high, 1, 1))
            out = jnp.where(gz == 0, high[:, 127:128], low[:, 0:1])
            packed = packed + jnp.where(lane == 8 * x + row, out, 0.0)
        over_ref[k:k + 1, :] = jnp.sum(packed, axis=0, keepdims=True)
    over_ref[3:8, :] = jnp.zeros((5, 128), F32)


def join(ids_ref, part_ref, over_ref, grad_ref):
    gz = ids_ref[2]
    lane = lanes()
    row = rows_of()
    edge = jnp.where(gz == 0, 127, 0)
    for k in range(3):
        for x in range(8):
            column = jnp.sum(jnp.where(lane == 8 * x + row, over_ref[k:k + 1, :], 0.0), axis=1, keepdims=True)
            grad_ref[k, x] = part_ref[k, x] + jnp.where(lane == edge, column, 0.0)


VMEM = pl.BlockSpec(memory_space=pltpu.VMEM)
SMEM = pl.BlockSpec(memory_space=pltpu.SMEM)


def call(kernel, specs, shapes, scratch, *operands, flops=0, size=1 << 20, outs=None):
    return pl.pallas_call(
        kernel,
        in_specs=specs,
        out_specs=outs or [VMEM] * len(shapes),
        out_shape=[s if hasattr(s, "memory_space") else jax.ShapeDtypeStruct(*s) for s in shapes],
        scratch_shapes=scratch,
        compiler_params=pltpu.CompilerParams(vmem_limit_bytes=12 * 2**20),
        cost_estimate=pl.CostEstimate(flops=flops, bytes_accessed=size, transcendentals=0),
    )(*operands)


def trade(velocity, cotangent, axis, dim):
    count = lax.axis_size(axis)
    odd = lax.rem(lax.axis_index(axis), 2) == 1
    size = velocity.shape[dim]

    def cut(array, start, stop):
        return lax.slice_in_dim(array, start, stop, axis=dim)

    other = 3 - dim
    grow = [(0, 0)] * 4
    grow[other] = (0, velocity.shape[other] - cotangent.shape[other])
    low = jnp.concatenate([cut(velocity, 0, 2), jnp.pad(cut(cotangent, 0, 1), grow)], axis=dim)
    high = jnp.concatenate([cut(velocity, size - 2, size), jnp.pad(cut(cotangent, size - 1, size), grow)], axis=dim)
    pairs = [(i, i ^ 1) for i in range(count)]
    gaps = [(i, i + 1) for i in range(1, count - 1, 2)]
    gaps = gaps + [(j, i) for i, j in gaps]
    second = lax.ppermute(jnp.where(odd, high, low), axis, gaps)
    first = lax.ppermute(jnp.where(odd, low, high), axis, pairs)
    below, above = jnp.where(odd, first, second), jnp.where(odd, second, first)
    wide = jnp.concatenate([cut(below, 0, 2), velocity, cut(above, 0, 2)], axis=dim)
    kept = cotangent.shape[other]
    narrow = jnp.concatenate([lax.slice_in_dim(cut(below, 2, 3), 0, kept, axis=other), cotangent,
                              lax.slice_in_dim(cut(above, 2, 3), 0, kept, axis=other)], axis=dim)
    return wide, narrow


def gather_own(rows):
    nx, ny, nz = (lax.axis_size(a) for a in AXES)
    groups = [[(x * ny + 2 * y + c) * nz + z for z in range(nz) for y in range(ny // 2) for x in range(nx)]
              for c in range(2)]
    mine = lax.all_to_all(rows, AXES, 0, 0, axis_index_groups=groups)
    return mine.reshape(rows.shape[0] * rows.shape[1], rows.shape[2])


def twin(mine):
    return lax.ppermute(mine, "gy", [(i, i ^ 1) for i in range(lax.axis_size("gy"))])


def collect(rows):
    x = lax.axis_index("gx")
    odd, upper = lax.rem(x, 2) == 1, x >= 2
    one, two, three = (lax.ppermute(rows, "gx", [(i, i ^ d) for i in range(4)]) for d in (1, 2, 3))
    a, b = jnp.where(odd, one, rows), jnp.where(odd, rows, one)
    c, d = jnp.where(odd, three, two), jnp.where(odd, two, three)
    line = jnp.concatenate([jnp.where(upper, c, a), jnp.where(upper, d, b),
                            jnp.where(upper, a, c), jnp.where(upper, b, d)], axis=0)
    across = lax.ppermute(line, "gy", [(i, i ^ 2) for i in range(4)])
    upper = lax.axis_index("gy") >= 2
    near = jnp.concatenate([jnp.where(upper, across, line), jnp.where(upper, line, across)], axis=0)
    return near, lax.ppermute(near, "gz", [(0, 1), (1, 0)])


def project_rows(ext, ids, sweeps, field, *more):
    block = ((3, 8, 8, 128), F32)
    scratch = [
        pltpu.VMEM((2, 2, 8, 8, 8, 128), F32),
        pltpu.VMEM((2, 2, 8, 8, 8, 128), F32),
        pltpu.VMEM((2, 2, 8, 8, 8, 128), F32),
        pltpu.VMEM((2, 8, 8, 128), F32),
        pltpu.VMEM((2, 8, 2, 8, 128), F32),
        pltpu.VMEM((2, 4, 4, 8, 128), F32),
        pltpu.VMEM((288, 256), F32),
        pltpu.VMEM((288, 256), F32),
    ]
    return call(functools.partial(project_kernel, ext), [SMEM, SMEM] + [VMEM] * (1 + len(more)),
                [((3, 10, 16, 128), F32)] if ext else [block, block], scratch,
                ids, sweeps, field, *more, flops=7 * 10**9)


def weights(first_weight, first_bias, second_weight):
    return call(
        weights_kernel, [pl.BlockSpec(memory_space=pltpu.HBM)] * 3,
        [((2 * HIDDEN, REACH), BF16), ((216, DEEP), BF16), ((3 * WIDTH, 128), F32), ((HIDDEN, 256), BF16)],
        [pltpu.VMEM((256, 128), F32), pltpu.VMEM(first_weight.shape, F32), pltpu.VMEM((1, WIDTH), F32),
         pltpu.VMEM(second_weight.shape, F32), pltpu.SemaphoreType.DMA((3,))],
        *(pltpu.with_memory_space_constraint(a, pltpu.HBM) for a in (first_weight, first_bias[None], second_weight)),
        flops=10**9)


def forward(ids, second_bias, near, face, wide, out, count):
    return call(
        forward_kernel, [SMEM, SMEM] + [VMEM] * 4,
        [((3, 8, 8, 128), F32), pltpu.HBM((5, HIDDEN, 256), F32), pltpu.HBM((count, SENT, 128), F32)],
        [pltpu.VMEM((ROWS, 128), F32), pltpu.VMEM((4 * PLANE + REACH, 256), BF16), pltpu.VMEM((HIDDEN, 256), F32),
         pltpu.VMEM((3, 10, 16, 128), F32), pltpu.VMEM((64, 128), F32), pltpu.VMEM((5, HIDDEN, 256), F32),
         pltpu.SemaphoreType.DMA((5,)), pltpu.VMEM((SENT, 128), F32), pltpu.SemaphoreType.DMA((count,))],
        ids, second_bias, near, face, wide, out, flops=4 * 10**9,
        outs=[VMEM] + [pl.BlockSpec(memory_space=pltpu.HBM)] * 2)


def gathered(velocity, cotangent, first_weight, first_bias, second_weight, second_bias, sweeps):
    swap = [(0, 1), (1, 0)]
    ids = jnp.stack([lax.axis_index("gx"), lax.axis_index("gy"), lax.axis_index("gz"),
                     jnp.int32(lax.axis_size("gx")), jnp.int32(lax.axis_size("gy"))]).astype(jnp.int32)
    near, cot_near = trade(velocity, cotangent, "gx", 1)
    cot_rows = call(own_rows_kernel, [VMEM], [((SENT_OWN, 128), F32)], [pltpu.VMEM((80, 128), F32)], cot_near)[0]
    cot_own, cot_far = collect(cot_rows)
    near, cot_near = trade(near, cot_near, "gy", 2)
    face = jnp.where(ids[2] == 0, near[:, :, :, 127], near[:, :, :, 0])
    face = lax.ppermute(face, "gz", swap)
    wide, tall, out, back = weights(first_weight, first_bias, second_weight)
    closed, slope, rows = forward(ids, second_bias, near, face, wide, out, lax.axis_size(AXES) // 2)
    mine = gather_own(rows)
    cot_far, rows = lax.optimization_barrier((cot_far, rows))
    adjoint = project_rows(True, ids, sweeps, cot_near, cot_own, cot_far, twin(cot_own), twin(cot_far))[0]
    part, over_rows = call(
        backward_kernel, [SMEM] + [VMEM] * 4, [((3, 8, 8, 128), F32), ((8, 128), F32)],
        [pltpu.VMEM((256, 256), BF16), pltpu.VMEM((DEEP, 256), BF16), pltpu.VMEM((12, 72, 128), F32)],
        ids, adjoint, slope, tall, back, flops=10**6)
    over_rows = lax.ppermute(over_rows, "gz", swap)
    mine, part, over_rows = lax.optimization_barrier((mine, part, over_rows))
    updated, grad = project_rows(False, ids, sweeps, closed, mine, twin(mine), part, over_rows)
    return updated, grad


def one_gather(velocity, first_weight):
    nx, ny, nz = (lax.axis_size(a) for a in AXES)
    return (velocity.shape == (3, 8, 8, 128) and nx == 4 and ny == 4 and nz == 2
            and first_weight.shape == (WIDTH, 81))


def dispatch(velocity, cotangent, first_weight, first_bias, second_weight, second_bias, sweeps):
    path = gathered if one_gather(velocity, first_weight) else shards
    return path(velocity, cotangent, first_weight, first_bias, second_weight, second_bias, sweeps)


def solution(mesh):
    return jax.shard_map(
        dispatch,
        mesh=mesh,
        in_specs=(P(None, "gx", "gy", "gz"), P(None, "gx", "gy", "gz"), P(), P(), P(), P(), P()),
        out_specs=(P(None, "gx", "gy", "gz"), P(None, "gx", "gy", "gz")),
        check_vma=False,
    )
```
